256 devices in a mesh: chan: 32 (over z, y), row: 8 (over x, core).
Axes of the slice: x: 4, y: 4, z: 8, core: 2. Of those that a mesh axis runs over, the one named last changes fastest.
Arguments:
- env_blocks: bfloat16 [192, 8192, 256], P('chan', 'row'), may hold values from -6 to 6
- site_rows: bfloat16 [512, 4, 8192], P('chan', None, 'row'), may hold values from -0.0625 to 0.0625
- route_dest: int32 [192, 5], replicated, may hold values from 0 to 191, as said below
- pair_index: int32 [192, 5, 2], P('chan'), may hold values from 0 to 15
- pair_value: float32 [192, 5, 2], P('chan'), may hold values from -1.5 to 1.5
Outputs:
- new_env: float32 [192, 32768], P('chan', 'row')
The draws below stay inside these ranges and needn't reach their ends.
Inputs may be any that keep to these rules, and one draw needn't show every extreme that they name: `route_dest`: for every g and h, the terms of input channels 6 * g to 6 * g + 5 name at most 2 output channels (with repetition) among 6 * h to 6 * h + 5; for every g exactly 2 for some h.
All inputs are finite; a program needn't handle non-finite values.
Results may differ from the reference program's by a relative error of at most 0.0003.
Values may be sent and summed in bfloat16 or wider, within the bound.
A program may use at most 128 MiB of HBM per device.

```python
import jax
import jax.numpy as jnp
from jax import lax

CH = 192
CHI = 8192
PD = 4
P_SIZE = 64
AR = 512
K = 5
PAIRS = 2
N_CHAN = 32


def draw_route_dest(key, part):
    key = jax.random.fold_in(key, 11)
    per_dev = CH // N_CHAN
    slot_count = per_dev * K
    bound = max(2, (3 * slot_count + 2 * N_CHAN - 1) // (2 * N_CHAN))

    def one_group(group_key):
        first_key, order_key, shuffle_key, local_key = jax.random.split(group_key, 4)
        first = jax.random.randint(first_key, (), 0, N_CHAN)
        order = jax.random.permutation(order_key, N_CHAN * bound)
        inside = (order // bound == first).astype(jnp.int32)
        rest = order[jnp.argsort(inside, stable=True)]
        chosen = jnp.concatenate([first * bound + jnp.arange(bound, dtype=jnp.int32), rest[:slot_count - bound].astype(jnp.int32)])
        chosen = jax.random.permutation(shuffle_key, chosen)
        groups = chosen // bound
        local = jax.random.randint(local_key, (slot_count,), 0, per_dev)
        return (groups * per_dev + local).astype(jnp.int32)
    group_keys = jax.random.split(key, N_CHAN)
    return jax.vmap(one_group)(group_keys).reshape(CH, K)


def touch_ends(array, stream_key, least, largest):
    longest = array.shape.index(max(array.shape))
    spots = []
    for shift in (0, 1):
        where = [jax.random.randint(jax.random.fold_in(stream_key, axis), (), 0, length) for axis, length in enumerate(array.shape)]
        where[longest] = (where[longest] + shift) % array.shape[longest]
        spots.append(tuple(where))
    return array.at[spots[0]].set(least).at[spots[1]].set(largest)


def block_scale(stream_key, shape, pieces, smallest, largest):
    def one(dim, blocks):
        draws = jax.random.uniform(jax.random.fold_in(jax.random.fold_in(stream_key, 6), dim), (blocks,), jnp.float32, smallest / len(pieces), largest / len(pieces))
        return jnp.repeat(jnp.exp(draws), shape[dim] // blocks).reshape((-1,) + (1,) * (len(shape) - dim - 1))

    level = one(*pieces[0])
    for cut in pieces[1:]:
        level = level * one(*cut)
    return level


def scatter_about(own_key, shape, deviation, most, cuts=(), held_as=jnp.bfloat16):
    level = block_scale(own_key, shape, cuts, -0.22, 0.18) if cuts else 1.0
    values = jax.random.normal(own_key, shape, jnp.float32) * deviation * level
    return jnp.minimum(jnp.maximum(values, -most), most).astype(held_as)


def setup_inputs(seed: int = 0) -> dict:
    splits = jax.random.split(jax.random.key(seed), 6)
    env_blocks = scatter_about(splits[0], (CH, CHI, PD * P_SIZE), 1.0, 6.0, ((0, 32), (1, 8)))
    site_rows = scatter_about(splits[1], (AR, PD, CHI), CHI ** -0.5, 0.0625, ((0, 32), (2, 8)))
    route_dest = draw_route_dest(jax.random.fold_in(splits[5], 71), 0)
    pair_index = touch_ends(jax.random.randint(splits[3], (CH, K, PAIRS), 0, PD * PD), jax.random.fold_in(splits[3], 1), 0, (PD * PD) - 1).astype(jnp.int32)
    pair_value = jnp.clip(jax.random.uniform(splits[4], (CH, K, PAIRS), jnp.float32, -1.5, 1.5) * block_scale(splits[4], (CH, K, PAIRS), ((0, 32),), -0.4, 0.0), -1.5, 1.5)
    return dict(env_blocks=env_blocks, site_rows=site_rows, route_dest=route_dest, pair_index=pair_index, pair_value=pair_value)


def pair_weights(pair_index, pair_value):
    codes = jnp.arange(PD * PD, dtype=jnp.int32)
    onehot = (pair_index[..., None] == codes).astype(jnp.float32)
    weights = jnp.einsum('bkj,bkjq->bkq', pair_value.astype(jnp.float32), onehot, precision=lax.Precision.HIGHEST)
    return weights.reshape(pair_index.shape[0], pair_index.shape[1], PD, PD)


def reference(env_blocks, site_rows, route_dest, pair_index, pair_value):
    flat_site = site_rows.reshape(AR * PD, CHI)
    weights = pair_weights(pair_index, pair_value)
    channels = jnp.arange(CH, dtype=jnp.int32)

    def step(carry, inputs):
        block, dest, weight = inputs
        prod = jnp.dot(flat_site, block, preferred_element_type=jnp.float32).reshape(AR, PD, PD, P_SIZE)
        terms = jnp.einsum('kst,astp->kap', weight, prod, precision=lax.Precision.HIGHEST)
        target = (dest[:, None] == channels[None, :]).astype(jnp.float32)
        carry = carry + jnp.einsum('kc,kx->cx', target, terms.reshape(K, AR * P_SIZE), precision=lax.Precision.HIGHEST)
        return carry, None

    start = jnp.zeros((CH, AR * P_SIZE), jnp.float32)
    result, _ = lax.scan(step, start, (env_blocks, route_dest, weights))
    return result
```

```python
import functools

import jax
import jax.numpy as jnp
from jax import lax
from jax.experimental import pallas as pl
from jax.experimental.pallas import tpu as pltpu
from jax.sharding import PartitionSpec as P

PD = 4
P_SIZE = 64
K = 5
NZ, NY, NX = 8, 4, 4
PER = 6
SLOTS = PER * K
OFFS = (0, 1, -1, 2)
MESH = pl.DeviceIdType.MESH
F32 = jnp.float32


def route_tables(route_dest, z):
    dest = lax.dynamic_slice_in_dim(route_dest.reshape(NZ, NY, SLOTS), z, 1, 0)[0]
    group = dest // PER
    term = jnp.arange(SLOTS, dtype=jnp.int32)
    same = group[:, :, None] == group[:, None, :]
    earlier = term[:, None] > term[None, :]
    rank = jnp.sum((same & earlier[None]).astype(jnp.int32), axis=2)
    slot = group * 2 + rank
    hit = slot[:, None, :] == jnp.arange(NZ * NY * 2, dtype=jnp.int32)[None, :, None]
    index = SLOTS + jnp.sum(jnp.where(hit, term - SLOTS, 0), axis=2)
    local = jnp.sum(jnp.where(hit, (dest - group * PER)[:, None, :], 0), axis=2)
    return jnp.concatenate([index, local], axis=0)


def kernel(
    table, pair_index, pair_value, site, env_hbm, out,
    env, g, prod, terms, mate_in, part, x_in, final, slots, y_in, acc, z_in,
    local_sem, g_send, g_recv, c_send, c_recv, x_send, x_recv, y_send, y_recv, z_send, z_recv,
):
    chan, row = lax.axis_index("chan"), lax.axis_index("row")
    z, y = chan // NY, lax.rem(chan, NY)
    x, core = row // 2, lax.rem(row, 2)
    flip = 1 - 2 * core

    def at_z(d):
        return (lax.rem(z + d + NZ, NZ) * NY + y, row)

    def at_y(d):
        return (z * NY + lax.rem(y + d + NY, NY), row)

    def at_x(d):
        return (chan, lax.rem(x + d + NX, NX) * 2 + core)

    mate = (chan, x * 2 + 1 - core)

    def zi(d):
        return lax.rem(z + d + NZ, NZ)

    def yi(d):
        return lax.rem(y + d + NY, NY)

    def xi(d):
        return lax.rem(x + d + NX, NX)

    env_copy = pltpu.make_async_copy(env_hbm, env, local_sem.at[0])
    own_copies = [
        pltpu.make_async_copy(site.at[h], g.at[y, h, z], local_sem.at[1 + h]) for h in range(2)
    ]
    for c in own_copies:
        c.start()
    env_copy.start()

    barrier = pltpu.get_barrier_semaphore()
    partners = [mate, at_x(1), at_x(-1), at_y(1), at_y(-1), at_y(2), at_z(1), at_z(-1)]
    for p in partners:
        pl.semaphore_signal(barrier, inc=1, device_id=p, device_id_type=MESH)
    acc[...] = jnp.zeros_like(acc)
    for d in range(4):
        final[d, SLOTS] = jnp.zeros((8, 128), F32)
    pl.semaphore_wait(barrier, len(partners))

    pending = []

    def send(src, dst, s_sem, r_sem, dev):
        c = pltpu.make_async_remote_copy(
            src_ref=src, dst_ref=dst, send_sem=s_sem, recv_sem=r_sem, device_id=dev, device_id_type=MESH
        )
        c.start()
        pending.append(c)

    def arrived(dst, r_sem, s_sem, dev):
        pltpu.make_async_remote_copy(
            src_ref=dst, dst_ref=dst, send_sem=s_sem, recv_sem=r_sem, device_id=dev, device_id_type=MESH
        ).wait_recv()

    g_count = [0]
    seen = set()

    def g_fwd(dy, h, dz, dev):
        a, b = yi(dy), zi(dz)
        n = g_count[0]
        g_count[0] += 1
        send(g.at[a, h, b], g.at[a, h, b], g_send.at[n], g_recv.at[a, h, b], dev)

    def g_wait(dy, h, dz):
        key = (dy % NY, h, dz if isinstance(dz, str) else dz % NZ)
        if key in seen:
            return
        seen.add(key)
        a, b = yi(dy), zi(dz)
        arrived(g.at[a, h, b], g_recv.at[a, h, b], g_send.at[0], at_z(1))

    lane_half = lax.broadcasted_iota(jnp.int32, (1, 1, 128), 2) // P_SIZE

    def product(d, h):
        a = yi(OFFS[d])

        def body(b, _):
            lhs = g[a, h].reshape(NZ * 32, -1)
            v = jnp.dot(lhs, env[b], preferred_element_type=F32).reshape(NZ, 2, 16, 256)
            for s in range(2):
                for t in range(2):
                    prod[d, b, t * 4 + 2 * h + s] = v[:, s, :, 128 * t:128 * (t + 1)]
            return 0

        lax.fori_loop(0, PER, body, 0)

    def make_terms(d):
        def body(i, _):
            b = i // K
            k = i - b * K
            total = None
            for j in range(2):
                code = pair_index[b, k, j]
                s, t = code >> 2, code & 3
                w = jnp.where(lane_half == (t & 1), pair_value[b, k, j], 0.0)
                one = w * prod[d, b, (t >> 1) * 4 + s]
                total = one if total is None else total + one
            even, odd = total[:, :8], total[:, 8:]
            low = lane_half == 0
            both = jnp.where(low, even, odd) + pltpu.roll(jnp.where(low, odd, even), P_SIZE, 2)
            for r in range(NZ):
                terms[d, r % 2, r // 2, i] = both[r]
            return 0

        lax.fori_loop(0, SLOTS, body, 0)
        send(terms.at[d, 1 - core], mate_in.at[d], c_send.at[d], c_recv.at[d], mate)

    def x_first(d):
        arrived(mate_in.at[d], c_recv.at[d], c_send.at[d], mate)

        def body(i, _):
            part[d, :, i // 15, lax.rem(i, 15)] = terms[d, core, :, i] + mate_in[d, :, i]
            return 0

        lax.fori_loop(0, SLOTS, body, 0)

        def go(dx, half, to, way, kind):
            send(part.at[d, xi(dx), half], x_in.at[d, way, kind], x_send.at[d, way, kind],
                 x_recv.at[d, way, kind], at_x(to))

        go(2, 0, 1, 0, 0)
        go(2, 1, -1, 1, 0)
        go(1, 1, 1, 0, 1)
        go(-1, 0, -1, 1, 1)

    def x_wait(d, way, kind):
        arrived(x_in.at[d, way, kind], x_recv.at[d, way, kind], x_send.at[d, way, kind], at_x(1))

    def x_second(d):
        for way, dx in ((0, 1), (1, -1)):
            x_wait(d, way, 0)
            part[d, xi(dx), way] += x_in[d, way, 0]
            send(part.at[d, xi(dx), way], x_in.at[d, way, 2], x_send.at[d, way, 2],
                 x_recv.at[d, way, 2], at_x(dx))

    def y_send_slots(d):
        for way in (0, 1):
            for kind in (1, 2):
                x_wait(d, way, kind)
        final[d, 0:15] = part[d, x, 0] + x_in[d, 0, 2] + x_in[d, 1, 1]
        final[d, 15:30] = part[d, x, 1] + x_in[d, 0, 1] + x_in[d, 1, 2]

        def body(i, _):
            for m in range(2):
                for q in range(NY):
                    pick = table[y, (i * NY + q) * 2 + m]
                    slots[d, q, i * 2 + m] = final[d, pick]
            return 0

        lax.fori_loop(0, NZ, body, 0)
        for n, dy in enumerate((1, -1, 2)):
            send(slots.at[d, yi(dy)], y_in.at[d, n], y_send.at[d, n], y_recv.at[d, n], at_y(dy))

    def gather_slots(d, own):
        sources = ((None, 0),) if own else ((0, -1), (1, 1), (2, 2))
        for n, dy in sources:
            if n is not None:
                arrived(y_in.at[d, n], y_recv.at[d, n], y_send.at[d, n], at_y(1))
            src = yi(dy)
            where_a = yi(dy + OFFS[d])

            def body(i, _):
                tiles, locs = [], []
                for m in range(2):
                    tiles.append(slots[d, y, i * 2 + m] if n is None else y_in[d, n, i * 2 + m])
                    locs.append(table[NY + src, (i * NY + y) * 2 + m])
                for c in range(PER):
                    add = sum(jnp.where(l == c, 1.0, 0.0).astype(F32) * t for t, l in zip(tiles, locs))
                    acc[i, c // 3, c % 3, where_a] += add
                return 0

            lax.fori_loop(0, NZ, body, 0)

    def z_step(way, half, dist):
        sgn = 1 - 2 * way
        a = zi(sgn * dist)
        if dist < (4 if half == way else 3):
            arrived(z_in.at[way, half, dist], z_recv.at[way, half, dist], z_send.at[way, half, dist], at_z(1))
            acc[a, half] += z_in[way, half, dist]
        send(acc.at[a, half], z_in.at[way, half, dist - 1], z_send.at[way, half, dist - 1],
             z_recv.at[way, half, dist - 1], at_z(sgn))

    for c in own_copies:
        c.wait()
    for h in (0, 1):
        g_fwd(0, h, 0, at_z(1))
        g_fwd(0, h, 0, at_z(-1))
    g_fwd(0, 1, 0, at_y(1))
    g_fwd(0, 1, 0, at_y(-1))
    g_fwd(0, 0, 0, at_y(1))
    g_fwd(0, 0, 0, at_y(-1))
    g_fwd(0, 1, 0, at_y(2))
    for s in (1, 2, 3):
        for sgn in (1, -1):
            for h in (0, 1):
                g_wait(0, h, -sgn * s)
                if s < 3 or h == (0 if sgn == 1 else 1):
                    g_fwd(0, h, -sgn * s, at_z(sgn))
        for off in (-s, s):
            g_fwd(0, 0, off, at_y(1))
            g_fwd(0, 0, off, at_y(-1))
    for dy in (1, -1):
        g_wait(dy, 1, 0)
        for sgn in (1, -1):
            g_fwd(dy, 1, 0, at_z(sgn))
    g_wait(0, 0, 4)
    g_fwd(0, 0, 4, at_y(1))
    g_fwd(0, 0, 4, at_y(-1))
    env_copy.wait()

    def ring(dy, s):
        for sgn in (1, -1):
            if dy == 2:
                last = None
            else:
                last = dy
            if s < 4:
                g_wait(dy, 1, -sgn * s)
            if s < 3:
                g_fwd(dy, 1, -sgn * s, at_z(sgn))
            elif s == 3 and last == sgn:
                g_fwd(dy, 1, -sgn * s, at_z(sgn))
        if s == 3 and dy == 2:
            a, b = yi(2), lax.rem(z - 3 * flip + NZ, NZ)
            n = g_count[0]
            g_count[0] += 1
            send(g.at[a, 1, b], g.at[a, 1, b], g_send.at[n], g_recv.at[a, 1, b],
                 (lax.rem(z + flip + NZ, NZ) * NY + y, row))
        if s == 4:
            g_wait(dy, 1, 4)

    def second_hop(up, down):
        for off in up:
            g_wait(-1, 0, off)
            g_fwd(-1, 0, off, at_y(1))
        for off in down:
            g_wait(1, 0, off)
            g_fwd(1, 0, off, at_y(-1))

    second_hop((0,), (-1,))
    product(0, 0)
    g_wait(0, 1, 4)
    for dy in (1, -1):
        ring(dy, 1)
    second_hop((1,), (-2,))
    product(0, 1)
    make_terms(0)
    g_wait(2, 1, 0)
    for sgn in (1, -1):
        g_fwd(2, 1, 0, at_z(sgn))
    for dy in (1, -1):
        ring(dy, 2)
    second_hop((2, 3), (-3, 4))
    x_first(0)
    for off in range(NZ):
        g_wait(1, 0, off)
    product(1, 0)
    for dy in (1, -1):
        ring(dy, 3)
    ring(2, 1)
    x_second(0)
    for off in range(NZ):
        g_wait(-1, 0, off)
    product(2, 0)
    ring(2, 2)
    ring(1, 4)
    product(1, 1)
    make_terms(1)
    ring(-1, 4)
    ring(2, 3)
    y_send_slots(0)
    product(2, 1)
    make_terms(2)
    x_first(1)
    for off in range(NZ):
        g_wait(2, 0, off)
    product(3, 0)
    x_first(2)
    x_second(1)
    gather_slots(0, True)
    x_second(2)
    ring(2, 4)
    product(3, 1)
    make_terms(3)
    y_send_slots(1)
    y_send_slots(2)
    x_first(3)
    gather_slots(0, False)
    x_second(3)
    gather_slots(1, True)
    gather_slots(2, True)
    gather_slots(1, False)
    y_send_slots(3)
    gather_slots(2, False)
    gather_slots(3, True)
    gather_slots(3, False)
    for way, half, dist in (
        (0, 0, 4), (1, 1, 4), (0, 1, 3), (1, 0, 3), (0, 0, 3), (1, 1, 3), (0, 1, 2), (1, 0, 2),
        (0, 0, 2), (1, 1, 2), (0, 1, 1), (1, 0, 1), (0, 0, 1), (1, 1, 1),
    ):
        z_step(way, half, dist)
    for half in (1, 0):
        for way in (0, 1):
            arrived(z_in.at[way, half, 0], z_recv.at[way, half, 0], z_send.at[way, half, 0], at_z(1))
        total = acc[z, half] + z_in[0, half, 0] + z_in[1, half, 0]
        out[3 * half:3 * half + 3] = total.reshape(3, 32, 128)
    for c in pending:
        c.wait_send()


def shards(env_blocks, site_rows, route_dest, pair_index, pair_value):
    chan = lax.axis_index("chan")
    table = route_tables(route_dest, chan // NY)
    depth = env_blocks.shape[1]
    site = site_rows.reshape(8, 2, PD, depth).transpose(2, 1, 0, 3).reshape(2, 32, depth)
    tile = (8, 128)
    bf16 = jnp.bfloat16
    dma = pltpu.SemaphoreType.DMA
    out = pl.pallas_call(
        kernel,
        out_shape=jax.ShapeDtypeStruct((PER, 32, 128), F32),
        in_specs=[pl.BlockSpec(memory_space=pltpu.SMEM)] * 3 + [pl.BlockSpec(memory_space=pl.ANY)] * 2,
        out_specs=pl.BlockSpec(memory_space=pltpu.VMEM),
        scratch_shapes=[
            pltpu.VMEM((PER, depth, PD * P_SIZE), bf16),
            pltpu.VMEM((NY, 2, NZ, 32, depth), bf16),
            pltpu.VMEM((4, PER, 8, NZ, 16, 128), F32),
            pltpu.VMEM((4, 2, NX, SLOTS) + tile, F32),
            pltpu.VMEM((4, NX, SLOTS) + tile, F32),
            pltpu.VMEM((4, NX, 2, SLOTS // 2) + tile, F32),
            pltpu.VMEM((4, 2, 3, SLOTS // 2) + tile, F32),
            pltpu.VMEM((4, SLOTS + 1) + tile, F32),
            pltpu.VMEM((4, NY, 2 * NZ) + tile, F32),
            pltpu.VMEM((4, 3, 2 * NZ) + tile, F32),
            pltpu.VMEM((NZ, 2, 3, 4) + tile, F32),
            pltpu.VMEM((2, 2, 4, 3, 4) + tile, F32),
            dma((3,)),
            dma((64,)),
            dma((NY, 2, NZ)),
            dma((4,)),
            dma((4,)),
            dma((4, 2, 3)),
            dma((4, 2, 3)),
            dma((4, 3)),
            dma((4, 3)),
            dma((2, 2, 4)),
            dma((2, 2, 4)),
        ],
        compiler_params=pltpu.CompilerParams(
            collective_id=0, has_side_effects=True, vmem_limit_bytes=56 * 1024 * 1024
        ),
        cost_estimate=pl.CostEstimate(
            flops=2 * 2048 * depth * PER * 256, bytes_accessed=4 * 1024 * 1024, transcendentals=0
        ),
    )(table, pair_index, pair_value, site, env_blocks)
    return out.reshape(PER, -1)


def solution(mesh):
    in_specs = (
        P("chan", "row", None),
        P("chan", None, "row"),
        P(),
        P("chan", None, None),
        P("chan", None, None),
    )
    out_specs = P("chan", "row")
    return jax.shard_map(shards, mesh=mesh, in_specs=in_specs, out_specs=out_specs, check_vma=False)
```

```python
import jax
import jax.numpy as jnp
from jax import lax
from jax.experimental import pallas as pl
from jax.experimental.pallas import tpu as pltpu
from jax.sharding import PartitionSpec as P

PD = 4
P_SIZE = 64
K = 5
NZ, NY, NX = 8, 4, 4
PER = 6
SLOTS = PER * K
OFFS = (0, 1, -1, 2)
ROWS = (48, 16)
LINKS = ((1, 0), (-1, 0), (0, 1), (0, -1), (0, 2))
MESH = pl.DeviceIdType.MESH
F32 = jnp.float32
I16 = jnp.int16

ORDER = (
    ("F", 0, 1, 0, (0, 1, 2, 3, 4)),
    ("F", 0, 0, 0, (0, 1, 2, 3)),
    ("F", 0, 1, -1, (0,)),
    ("F", 0, 1, 1, (1,)),
    ("F", -1, 1, 0, ()),
    ("F", 1, 1, 0, ()),
    ("F", 2, 1, 0, ()),
    ("F", 0, 0, -1, (0, 2, 3)),
    ("F", 0, 0, 1, (1, 2, 3)),
    ("F", 1, 0, 0, ()),
    ("S", -1, 1, 0, (0,)),
    ("S", -1, 1, 0, (1,)),
    ("S", 1, 1, 0, (0,)),
    ("S", 1, 1, 0, (1,)),
    ("S", 2, 1, 0, (0,)),
    ("S", 2, 1, 0, (1,)),
    ("F", 0, 1, -2, (0,)),
    ("F", 0, 1, 2, (1,)),
    ("F", -1, 0, 0, ()),
    ("F", 0, 0, -2, (0, 2, 3)),
    ("F", -1, 0, -1, ()),
    ("F", 1, 0, -1, ()),
    ("F", 0, 0, 2, (1, 2, 3)),
    ("F", -1, 1, -1, ()),
    ("S", -1, 1, -1, (0,)),
    ("F", -1, 1, 1, ()),
    ("S", -1, 1, 1, (1,)),
    ("F", 1, 1, -1, ()),
    ("S", 1, 1, -1, (0,)),
    ("F", 1, 1, 1, ()),
    ("S", 1, 1, 1, (1,)),
    ("F", 2, 1, -1, ()),
    ("S", 2, 1, -1, (0,)),
    ("F", -1, 0, 1, ()),
    ("F", 1, 0, 1, ()),
    ("F", 2, 1, 1, ()),
    ("S", 2, 1, 1, (1,)),
    ("F", 0, 1, -3, ()),
    ("F", 0, 1, 3, (1,)),
    ("F", -1, 0, -2, ()),
    ("F", 1, 0, -2, ()),
    ("F", 0, 0, -3, (0, 2, 3)),
    ("F", 0, 0, 3, (2, 3)),
    ("F", -1, 1, -2, ()),
    ("S", -1, 1, -2, (0,)),
    ("F", -1, 1, 2, ()),
    ("S", -1, 1, 2, (1,)),
    ("F", 1, 1, -2, ()),
    ("S", 1, 1, -2, (0,)),
    ("F", -1, 0, 2, ()),
    ("F", 1, 0, 2, ()),
    ("F", 1, 1, 2, ()),
    ("S", 1, 1, 2, (1,)),
    ("F", 2, 1, -2, ()),
    ("S", 2, 1, -2, (0,)),
    ("F", 2, 1, 2, ()),
    ("S", 2, 1, 2, (1,)),
    ("F", 0, 1, 4, ()),
    ("F", -1, 1, 3, ()),
    ("S", -1, 1, 3, (1,)),
    ("F", -1, 0, -3, ()),
    ("F", 1, 0, -3, ()),
    ("F", 0, 0, 4, (2, 3)),
    ("S", -1, 0, 0, (2,)),
    ("S", -1, 0, -1, (2,)),
    ("S", 1, 0, 1, (3,)),
    ("S", 1, 0, -2, (3,)),
    ("S", -1, 0, 2, (2,)),
    ("S", -1, 0, -3, (2,)),
    ("F", 1, 1, 3, ()),
    ("S", 1, 1, 3, (1,)),
    ("P", 0, 2, 0, ()),
    ("F", -1, 1, -3, ()),
    ("F", 2, 1, 3, ()),
    ("F", 1, 1, -3, ()),
    ("F", -1, 0, 3, ()),
    ("F", 1, 0, 3, ()),
    ("F", 2, 1, -3, ()),
    ("F", -1, 1, 4, ()),
    ("S", 2, 1, 3, (1,)),
    ("S", 1, 0, 3, (3,)),
    ("T", 0, 0, 0, ()),
    ("F", 1, 1, 4, ()),
    ("F", -1, 0, 4, ()),
    ("P", 2, 2, 0, ()),
    ("F", 1, 0, 4, ()),
    ("F", 2, 1, 4, ()),
    ("S", 1, 0, 4, (3,)),
    ("X", 0, 0, 0, ()),
    ("F", 2, 0, 0, ()),
    ("F", 2, 0, 1, ()),
    ("T", 2, 0, 0, ()),
    ("P", 1, 2, 0, ()),
    ("F", 2, 0, -1, ()),
    ("F", 2, 0, -2, ()),
    ("T", 1, 0, 0, ()),
    ("F", 2, 0, 2, ()),
    ("F", 2, 0, 3, ()),
    ("X", 2, 0, 0, ()),
    ("P", 3, 1, 0, ()),
    ("Z", 0, 0, 0, ()),
    ("F", 2, 0, -3, ()),
    ("F", 2, 0, 4, ()),
    ("X", 1, 0, 0, ()),
    ("P", 3, 0, 0, ()),
    ("T", 3, 0, 0, ()),
    ("Z", 2, 0, 0, ()),
    ("X", 3, 0, 0, ()),
    ("Y", 0, 0, 0, ()),
    ("Z", 1, 0, 0, ()),
    ("O", 0, 0, 0, ()),
    ("Y", 2, 0, 0, ()),
    ("Z", 3, 0, 0, ()),
    ("Y", 1, 0, 0, ()),
    ("O", 2, 0, 0, ()),
    ("O", 1, 0, 0, ()),
    ("Y", 3, 0, 0, ()),
    ("O", 3, 0, 0, ()),
)


def route_tables(route_dest, y):
    dest = lax.dynamic_slice_in_dim(route_dest.reshape(NZ, NY, SLOTS), y, 1, 1)[:, 0]
    group = dest // PER
    term = jnp.arange(SLOTS, dtype=jnp.int32)
    same = group[:, :, None] == group[:, None, :]
    earlier = term[:, None] > term[None, :]
    rank = jnp.sum((same & earlier[None]).astype(jnp.int32), axis=2)
    slot = group * 2 + rank
    hit = slot[:, None, :] == jnp.arange(NZ * NY * 2, dtype=jnp.int32)[None, :, None]
    index = SLOTS + jnp.sum(jnp.where(hit, term - SLOTS, 0), axis=2)
    local = jnp.sum(jnp.where(hit, (dest - group * PER)[:, None, :], 0), axis=2)
    return jnp.concatenate([index, local], axis=0)


def encode(v):
    most = jnp.maximum(jnp.max(jnp.abs(v), axis=0), 1e-30)
    code = jnp.ceil(jnp.log2(most) * 8.0)
    inverse = 32000.0 / jnp.exp2(code * 0.125)
    q = jnp.round(v * inverse[None]).astype(jnp.int32).astype(I16)
    return q, code.astype(jnp.int32).astype(I16)


def decode(q):
    n = q.shape[0] - 1
    scale = jnp.exp2(q[n].astype(F32) * 0.125) * (1.0 / 32000.0)
    return q[0:n].astype(F32) * scale[None]


def kernel(
    table, pair_index, pair_value, site, env_hbm, out,
    env, g0, g1, prod, terms, mate_in, x_own, x_out, x_in, final, z_own, z_out, z_in, y_sum, y_out, y_in,
    local_sem, g_send, g_recv, c_send, c_recv, x_send, x_recv, z_send, z_recv, y_send, y_recv,
):
    chan, row = lax.axis_index("chan"), lax.axis_index("row")
    z, y = chan // NY, lax.rem(chan, NY)
    x, core = row // 2, lax.rem(row, 2)
    g = (g0, g1)

    def zi(d):
        return lax.rem(z + d + NZ, NZ)

    def yi(d):
        return lax.rem(y + d + NY, NY)

    def xi(d):
        return lax.rem(x + d + NX, NX)

    def at_zy(dz, dy):
        return (zi(dz) * NY + yi(dy), row)

    def at_x(d):
        return (chan, xi(d) * 2 + core)

    mate = (chan, x * 2 + 1 - core)

    own_copies = [
        pltpu.make_async_copy(site.at[0:48], g0.at[y, z], local_sem.at[1]),
        pltpu.make_async_copy(site.at[48:64], g1.at[y, z], local_sem.at[2]),
    ]
    for c in own_copies:
        c.start()
    env_copy = pltpu.make_async_copy(env_hbm, env, local_sem.at[0])
    env_copy.start()

    barrier = pltpu.get_barrier_semaphore()
    partners = [mate] + [at_x(d) for d in (1, 2, 3)] + [at_zy(0, d) for d in (1, 2, 3)]
    partners += [at_zy(d, 0) for d in range(1, NZ)]
    for p in partners:
        pl.semaphore_signal(barrier, inc=1, device_id=p, device_id_type=MESH)
    out[...] = jnp.zeros_like(out)
    for d in range(4):
        final[d, SLOTS] = jnp.zeros((8, 128), F32)
    pl.semaphore_wait(barrier, len(partners))

    pending = []

    def send(src, dst, s_sem, r_sem, dev):
        c = pltpu.make_async_remote_copy(
            src_ref=src, dst_ref=dst, send_sem=s_sem, recv_sem=r_sem, device_id=dev, device_id_type=MESH
        )
        c.start()
        pending.append(c)

    def arrived(dst, r_sem, s_sem):
        pltpu.make_async_remote_copy(
            src_ref=dst, dst_ref=dst, send_sem=s_sem, recv_sem=r_sem, device_id=mate, device_id_type=MESH
        ).wait_recv()

    g_count = [0]

    def g_fwd(dy, h, dz, links):
        a, b = yi(dy), zi(dz)
        for link in links:
            send(g[h].at[a, b], g[h].at[a, b], g_send.at[g_count[0]], g_recv.at[a, h, b], at_zy(*LINKS[link]))
            g_count[0] += 1

    def g_wait(dy, h, dz):
        a, b = yi(dy), zi(dz)
        if (dy, dz) == (0, 0):
            own_copies[h].wait()
        else:
            arrived(g[h].at[a, b], g_recv.at[a, h, b], g_send.at[0])

    lane_half = lax.broadcasted_iota(jnp.int32, (1, 1, 128), 2) // P_SIZE

    def product(d, part):
        a = yi(OFFS[d])
        parts = (0, 1) if part == 2 else (part,)

        def one(b):
            lhs = [g[h][a].reshape(NZ * ROWS[h], -1) for h in parts]
            lhs = jnp.concatenate(lhs, axis=0) if len(lhs) > 1 else lhs[0]
            v = jnp.dot(lhs, env[b], preferred_element_type=F32)
            at = 0
            for h in parts:
                n = ROWS[h] // 16
                w = v[at:at + NZ * ROWS[h]].reshape(NZ, n, 16, 256)
                at += NZ * ROWS[h]
                for s in range(n):
                    for t in range(2):
                        prod[d, b, t * 4 + 3 * h + s] = w[:, s, :, 128 * t:128 * (t + 1)]

        def body(i, _):
            one(2 * i)
            one(2 * i + 1)
            return 0

        lax.fori_loop(0, PER // 2, body, 0)

    def make_terms(d, lo, hi):
        def body(b, _):
            for k in range(K):
                total = None
                for j in range(2):
                    code = pair_index[b, k, j]
                    s, t = code >> 2, code & 3
                    w = jnp.where(lane_half == (t & 1), pair_value[b, k, j], 0.0)
                    add = w * prod[d, b, (t >> 1) * 4 + s]
                    total = add if total is None else total + add
                even, odd = total[:, :8], total[:, 8:]
                low = lane_half == 0
                both = jnp.where(low, even, odd) + pltpu.roll(jnp.where(low, odd, even), P_SIZE, 2)
                for r in range(NZ):
                    terms[d, r % 2, r // 2, b * K + k] = both[r]
            return 0

        lax.fori_loop(lo, hi, body, 0)

    def mate_send(d):
        send(terms.at[d, 1 - core], mate_in.at[d], c_send.at[d], c_recv.at[d], mate)

    def x_step(d):
        arrived(mate_in.at[d], c_recv.at[d], c_send.at[d])
        for n, dx in enumerate((2, 1, -1, 0)):
            to = xi(dx)
            v = (terms[d, core, to] + mate_in[d, to]).reshape(SLOTS // 2, 16, 128)
            if dx == 0:
                x_own[d] = v
                continue
            q, code = encode(v)
            x_out[d, n, 0:SLOTS // 2] = q
            x_out[d, n, SLOTS // 2] = code
            send(x_out.at[d, n], x_in.at[d, n], x_send.at[d, n], x_recv.at[d, n], at_x(dx))

    def z_step(d):
        v = x_own[d]
        for n in (1, 2, 0):
            arrived(x_in.at[d, n], x_recv.at[d, n], x_send.at[d, n])
            v = v + decode(x_in[d, n])
        final[d, 0:SLOTS] = v.reshape(SLOTS, 8, 128)
        for dz in (4, 3, -3, 2, -2, 1, -1, 0):
            to = zi(dz)
            tiles = []
            for q in range(NY):
                for m in range(2):
                    tiles.append(final[d, table[z, (to * NY + q) * 2 + m]])
            v = jnp.stack(tiles).reshape(NY, 16, 128)
            if dz == 0:
                z_own[d] = v
                continue
            n = dz % NZ - 1
            q, code = encode(v)
            z_out[d, n, 0:NY] = q
            z_out[d, n, NY] = code
            send(z_out.at[d, n], z_in.at[d, n], z_send.at[d, n], z_recv.at[d, n], at_zy(dz, 0))

    def y_step(d):
        for dz in (1, -1, 2, -2, 3, -3, 4):
            n = dz % NZ - 1
            arrived(z_in.at[d, n], z_recv.at[d, n], z_send.at[d, n])
        sums = [[None] * PER for _ in range(NY)]
        for n in range(NZ):
            src = z if n == 0 else zi(-n)
            v = z_own[d] if n == 0 else decode(z_in[d, n - 1])
            for q in range(NY):
                for m in range(2):
                    local = table[NZ + src, (z * NY + q) * 2 + m]
                    tile = v[q, 8 * m:8 * m + 8]
                    for c in range(PER):
                        add = jnp.where(local == c, 1.0, 0.0).astype(F32) * tile
                        sums[q][c] = add if sums[q][c] is None else sums[q][c] + add
        for q in range(NY):
            y_sum[d, q] = jnp.stack(sums[q])
        for n, dy in enumerate((2, 1, -1)):
            q, code = encode(y_sum[d, yi(dy)].reshape(PER // 2, 16, 128))
            y_out[d, n, 0:PER // 2] = q
            y_out[d, n, PER // 2] = code
            send(y_out.at[d, n], y_in.at[d, n], y_send.at[d, n], y_recv.at[d, n], at_zy(0, dy))
        out[:, yi(OFFS[d])] += y_sum[d, y]

    def out_step(d):
        for n, dy in ((1, -1), (2, 1), (0, 2)):
            arrived(y_in.at[d, n], y_recv.at[d, n], y_send.at[d, n])
            out[:, yi(dy + OFFS[d])] += decode(y_in[d, n]).reshape(PER, 8, 128)

    waited = False
    for kind, d, h, dz, links in ORDER:
        if kind == "F":
            g_wait(d, h, dz)
            g_fwd(d, h, dz, links)
        elif kind == "S":
            g_fwd(d, h, dz, links)
        elif kind == "P":
            if not waited:
                env_copy.wait()
                waited = True
            product(d, h)
        elif kind == "T":
            make_terms(d, 0, PER)
            mate_send(d)
        elif kind == "X":
            x_step(d)
        elif kind == "Z":
            z_step(d)
        elif kind == "Y":
            y_step(d)
        else:
            out_step(d)
    for c in pending:
        c.wait_send()


def shards(env_blocks, site_rows, route_dest, pair_index, pair_value):
    chan = lax.axis_index("chan")
    table = route_tables(route_dest, lax.rem(chan, NY))
    depth = env_blocks.shape[1]
    site = site_rows.reshape(8, 2, PD, depth).transpose(2, 1, 0, 3).reshape(64, depth)
    tile = (8, 128)
    tile16 = (16, 128)
    bf16 = jnp.bfloat16
    dma = pltpu.SemaphoreType.DMA
    out = pl.pallas_call(
        kernel,
        out_shape=jax.ShapeDtypeStruct((PER, NY, 8, 128), F32),
        in_specs=[pl.BlockSpec(memory_space=pltpu.SMEM)] * 3 + [pl.BlockSpec(memory_space=pl.ANY)] * 2,
        out_specs=pl.BlockSpec(memory_space=pltpu.VMEM),
        scratch_shapes=[
            pltpu.VMEM((PER, depth, PD * P_SIZE), bf16),
            pltpu.VMEM((NY, NZ, ROWS[0], depth), bf16),
            pltpu.VMEM((NY, NZ, ROWS[1], depth), bf16),
            pltpu.VMEM((4, PER, 8, NZ, 16, 128), F32),
            pltpu.VMEM((4, 2, NX, SLOTS) + tile, F32),
            pltpu.VMEM((4, NX, SLOTS) + tile, F32),
            pltpu.VMEM((4, SLOTS // 2) + tile16, F32),
            pltpu.VMEM((4, 3, SLOTS // 2 + 1) + tile16, I16),
            pltpu.VMEM((4, 3, SLOTS // 2 + 1) + tile16, I16),
            pltpu.VMEM((4, SLOTS + 1) + tile, F32),
            pltpu.VMEM((4, NY) + tile16, F32),
            pltpu.VMEM((4, NZ - 1, NY + 1) + tile16, I16),
            pltpu.VMEM((4, NZ - 1, NY + 1) + tile16, I16),
            pltpu.VMEM((4, NY, PER) + tile, F32),
            pltpu.VMEM((4, 3, PER // 2 + 1) + tile16, I16),
            pltpu.VMEM((4, 3, PER // 2 + 1) + tile16, I16),
            dma((3,)),
            dma((62,)),
            dma((NY, 2, NZ)),
            dma((4,)),
            dma((4,)),
            dma((4, 3)),
            dma((4, 3)),
            dma((4, NZ - 1)),
            dma((4, NZ - 1)),
            dma((4, 3)),
            dma((4, 3)),
        ],
        compiler_params=pltpu.CompilerParams(
            collective_id=0, has_side_effects=True, vmem_limit_bytes=56 * 1024 * 1024
        ),
        cost_estimate=pl.CostEstimate(
            flops=2 * 2048 * depth * PER * 256, bytes_accessed=4 * 1024 * 1024, transcendentals=0
        ),
    )(table, pair_index, pair_value, site, env_blocks)
    return out.reshape(PER, -1)


def solution(mesh):
    in_specs = (
        P("chan", "row", None),
        P("chan", None, "row"),
        P(),
        P("chan", None, None),
        P("chan", None, None),
    )
    out_specs = P("chan", "row")
    return jax.shard_map(shards, mesh=mesh, in_specs=in_specs, out_specs=out_specs, check_vma=False)
```

```python
import jax
import jax.numpy as jnp
from jax import lax
from jax.experimental import pallas as pl
from jax.experimental.pallas import tpu as pltpu
from jax.sharding import PartitionSpec as P

PD = 4
P_SIZE = 64
K = 5
NZ, NY, NX = 8, 4, 4
PER = 6
SLOTS = PER * K
OFFS = (0, 1, -1, 2)
CUTS = ((0, 48), (48, 64))
CUTS_FAR = ((0, 32), (32, 64))
LINKS = ((1, 0), (-1, 0), (0, 1), (0, -1), (0, 2))
MESH = pl.DeviceIdType.MESH
F32 = jnp.float32
I16 = jnp.int16

ORDER = (
    ("F", 0, 1, 0, (0, 1, 2, 3, 4)),
    ("F", 0, 0, 0, (0, 1, 2, 3)),
    ("G", 0, 0, 0, ()),
    ("I", 0, 0, 0, ()),
    ("L", 0, 0, 0, ()),
    ("F", 0, 1, -1, (0,)),
    ("F", 0, 1, 1, (1,)),
    ("F", -1, 1, 0, ()),
    ("F", 1, 1, 0, ()),
    ("F", 2, 1, 0, ()),
    ("F", 0, 0, -1, (0, 2, 3)),
    ("F", 0, 0, 1, (1, 2, 3)),
    ("F", 1, 0, 0, ()),
    ("S", -1, 1, 0, (0,)),
    ("S", -1, 1, 0, (1,)),
    ("S", 1, 1, 0, (0,)),
    ("S", 1, 1, 0, (1,)),
    ("S", 2, 1, 0, (0,)),
    ("S", 2, 1, 0, (1,)),
    ("F", 0, 1, -2, (0,)),
    ("F", 0, 1, 2, (1,)),
    ("F", -1, 0, 0, ()),
    ("F", 0, 0, -2, (0, 2, 3)),
    ("F", -1, 0, -1, ()),
    ("F", 1, 0, -1, ()),
    ("F", 0, 0, 2, (1, 2, 3)),
    ("F", -1, 1, -1, ()),
    ("S", -1, 1, -1, (0,)),
    ("F", -1, 1, 1, ()),
    ("S", -1, 1, 1, (1,)),
    ("F", 1, 1, -1, ()),
    ("S", 1, 1, -1, (0,)),
    ("F", 1, 1, 1, ()),
    ("S", 1, 1, 1, (1,)),
    ("F", -1, 0, 1, ()),
    ("F", 1, 0, 1, ()),
    ("F", 2, 1, -1, ()),
    ("S", 2, 1, -1, (0,)),
    ("F", 2, 1, 1, ()),
    ("S", 2, 1, 1, (1,)),
    ("F", 0, 1, -3, ()),
    ("F", 0, 1, 3, (1,)),
    ("F", -1, 0, -2, ()),
    ("F", 1, 0, -2, ()),
    ("F", 0, 0, -3, (0, 2, 3)),
    ("F", 0, 0, 3, (2, 3)),
    ("F", -1, 1, -2, ()),
    ("S", -1, 1, -2, (0,)),
    ("F", -1, 0, 2, ()),
    ("F", 1, 0, 2, ()),
    ("F", -1, 1, 2, ()),
    ("S", -1, 1, 2, (1,)),
    ("F", 1, 1, -2, ()),
    ("S", 1, 1, -2, (0,)),
    ("F", 1, 1, 2, ()),
    ("S", 1, 1, 2, (1,)),
    ("F", 2, 1, -2, ()),
    ("S", 2, 1, -2, (0,)),
    ("F", 2, 1, 2, ()),
    ("S", 2, 1, 2, (1,)),
    ("F", 0, 1, 4, ()),
    ("F", -1, 0, -3, ()),
    ("F", 1, 0, -3, ()),
    ("F", -1, 1, 3, ()),
    ("S", -1, 1, 3, (1,)),
    ("F", 0, 0, 4, (2, 3)),
    ("S", -1, 0, 0, (2,)),
    ("S", -1, 0, -1, (2,)),
    ("S", 1, 0, 1, (3,)),
    ("S", 1, 0, -2, (3,)),
    ("S", -1, 0, 2, (2,)),
    ("S", -1, 0, -3, (2,)),
    ("F", 1, 1, 3, ()),
    ("S", 1, 1, 3, (1,)),
    ("P", 0, 2, 0, ()),
    ("F", -1, 1, -3, ()),
    ("F", -1, 0, 3, ()),
    ("F", 1, 0, 3, ()),
    ("F", 1, 1, -3, ()),
    ("F", 2, 1, 3, ()),
    ("F", -1, 1, 4, ()),
    ("S", 1, 0, 3, (3,)),
    ("S", 2, 1, 3, (1,)),
    ("T", 0, 0, 0, ()),
    ("F", 2, 1, -3, ()),
    ("F", 1, 1, 4, ()),
    ("F", -1, 0, 4, ()),
    ("P", 2, 2, 0, ()),
    ("F", 1, 0, 4, ()),
    ("F", 2, 0, 0, ()),
    ("F", 2, 0, 1, ()),
    ("F", 2, 1, 4, ()),
    ("S", 1, 0, 4, (3,)),
    ("X", 0, 0, 0, ()),
    ("F", 2, 0, -1, ()),
    ("F", 2, 0, -2, ()),
    ("T", 2, 0, 0, ()),
    ("P", 1, 2, 0, ()),
    ("F", 2, 0, 2, ()),
    ("F", 2, 0, 3, ()),
    ("F", 2, 0, -3, ()),
    ("F", 2, 0, 4, ()),
    ("X", 2, 0, 0, ()),
    ("T", 1, 0, 0, ()),
    ("P", 3, 1, 0, ()),
    ("Z", 0, 0, 0, ()),
    ("P", 3, 0, 0, ()),
    ("X", 1, 0, 0, ()),
    ("T", 3, 0, 0, ()),
    ("Z", 2, 0, 0, ()),
    ("X", 3, 0, 0, ()),
    ("Y", 0, 0, 0, ()),
    ("Z", 1, 0, 0, ()),
    ("Y", 2, 0, 0, ()),
    ("O", 0, 0, 0, ()),
    ("Z", 3, 0, 0, ()),
    ("O", 2, 0, 0, ()),
    ("Y", 1, 0, 0, ()),
    ("Y", 3, 0, 0, ()),
    ("O", 1, 0, 0, ()),
    ("O", 3, 0, 0, ()),
)


def encode(v):
    most = jnp.maximum(jnp.max(jnp.abs(v), axis=0), 1e-30)
    code = jnp.ceil(jnp.log2(most) * 8.0)
    inverse = 32000.0 / jnp.exp2(code * 0.125)
    q = jnp.round(v * inverse[None]).astype(jnp.int32).astype(I16)
    return q, code.astype(jnp.int32).astype(I16)


def decode(q):
    n = q.shape[0] - 1
    scale = jnp.exp2(q[n].astype(F32) * 0.125) * (1.0 / 32000.0)
    return q[0:n].astype(F32) * scale[None]


def kernel(
    route, pair_index, pair_value, site_hbm, env_hbm, out,
    env, site, g, prod, terms, mate_in, x_own, x_out, x_in, final, z_own, z_out, z_in, y_sum, y_out, y_in,
    group, local, pick, place,
    local_sem, g_send, g_recv, c_send, c_recv, x_send, x_recv, z_send, z_recv, y_send, y_recv,
):
    chan, row = lax.axis_index("chan"), lax.axis_index("row")
    z, y = chan // NY, lax.rem(chan, NY)
    x, core = row // 2, lax.rem(row, 2)

    def zi(d):
        return lax.rem(z + d + NZ, NZ)

    def yi(d):
        return lax.rem(y + d + NY, NY)

    def xi(d):
        return lax.rem(x + d + NX, NX)

    def at_zy(dz, dy):
        return (zi(dz) * NY + yi(dy), row)

    def at_x(d):
        return (chan, xi(d) * 2 + core)

    mate = (chan, x * 2 + 1 - core)

    site_copy = pltpu.make_async_copy(site_hbm, site, local_sem.at[1])
    site_copy.start()
    env_copy = pltpu.make_async_copy(env_hbm, env, local_sem.at[0])
    env_copy.start()

    barrier = pltpu.get_barrier_semaphore()
    partners = [mate] + [at_x(d) for d in (1, 2, 3)] + [at_zy(0, d) for d in (1, 2, 3)]
    partners += [at_zy(d, 0) for d in range(1, NZ)]
    for p in partners:
        pl.semaphore_signal(barrier, inc=1, device_id=p, device_id_type=MESH)
    out[...] = jnp.zeros_like(out)
    for d in range(4):
        final[d, SLOTS] = jnp.zeros((8, 128), F32)
    new = lax.broadcasted_iota(jnp.int32, (64, 64), 0)
    old = lax.broadcasted_iota(jnp.int32, (64, 64), 1)
    moved = (new & 7) * 8 + ((new >> 3) & 1) * 4 + (new >> 4)
    turn = jnp.where(moved == old, 1.0, 0.0).astype(jnp.bfloat16)
    site_copy.wait()
    rows = site[...].astype(F32).reshape(64, site.shape[2]).astype(jnp.bfloat16)
    g[y, z] = jnp.dot(turn, rows, preferred_element_type=F32).astype(jnp.bfloat16)
    pl.semaphore_wait(barrier, len(partners))

    pending = []

    def send(src, dst, s_sem, r_sem, dev):
        c = pltpu.make_async_remote_copy(
            src_ref=src, dst_ref=dst, send_sem=s_sem, recv_sem=r_sem, device_id=dev, device_id_type=MESH
        )
        c.start()
        pending.append(c)

    def arrived(dst, r_sem, s_sem):
        pltpu.make_async_remote_copy(
            src_ref=dst, dst_ref=dst, send_sem=s_sem, recv_sem=r_sem, device_id=mate, device_id_type=MESH
        ).wait_recv()

    g_count = [0]

    def part(dy, h, dz):
        lo, hi = (CUTS_FAR if dy == 2 else CUTS)[h]
        return g.at[yi(dy), zi(dz), lo:hi]

    def g_fwd(dy, h, dz, links):
        for link in links:
            there = (dy - LINKS[link][1] + 1) % NY - 1
            lo, hi = (CUTS_FAR if there == 2 else CUTS)[h]
            ref = g.at[yi(dy), zi(dz), lo:hi]
            send(ref, ref, g_send.at[g_count[0]], g_recv.at[yi(dy), h, zi(dz)], at_zy(*LINKS[link]))
            g_count[0] += 1

    def g_wait(dy, h, dz):
        if (dy, dz) != (0, 0):
            arrived(part(dy, h, dz), g_recv.at[yi(dy), h, zi(dz)], g_send.at[0])

    def read_groups():
        def body(src, _):
            for i in range(SLOTS):
                dest = route[i % K, (src * NY + y) * PER + i // K]
                here = (dest * 10923) >> 16
                group[src, i] = here
                local[src, i] = dest - here * PER
            return 0

        lax.fori_loop(0, NZ, body, 0)

    def read_picks():
        def body(h, _):
            first, last = jnp.int32(SLOTS), jnp.int32(SLOTS)
            for i in range(SLOTS):
                j = SLOTS - 1 - i
                first = jnp.where(group[z, j] == h, j, first)
                last = jnp.where(group[z, i] == h, i, last)
            pick[h, 0] = first
            pick[h, 1] = jnp.where(last == first, SLOTS, last)
            return 0

        lax.fori_loop(0, NZ * NY, body, 0)

    def read_places():
        def body(n, _):
            src, h = n // NY, z * NY + lax.rem(n, NY)
            first, last = jnp.int32(0), jnp.int32(0)
            for i in range(SLOTS):
                j = SLOTS - 1 - i
                first = jnp.where(group[src, j] == h, local[src, j], first)
                last = jnp.where(group[src, i] == h, local[src, i], last)
            place[n, 0] = first
            place[n, 1] = last
            return 0

        lax.fori_loop(0, NZ * NY, body, 0)

    lane_half = lax.broadcasted_iota(jnp.int32, (1, 1, 128), 2) // P_SIZE

    def product(d, half):
        a = yi(OFFS[d])
        lo, hi = (0, 64) if half == 2 else CUTS_FAR[half]
        n = (hi - lo) // 16

        def one(b):
            lhs = g[a, :, lo:hi].reshape(NZ * (hi - lo), -1)
            v = jnp.dot(lhs, env[b], preferred_element_type=F32).reshape(NZ, n, 16, 256)
            for s in range(n):
                for t in range(2):
                    prod[d, b, t * 4 + lo // 16 + s] = v[:, s, :, 128 * t:128 * (t + 1)]

        def body(i, _):
            one(2 * i)
            one(2 * i + 1)
            return 0

        lax.fori_loop(0, PER // 2, body, 0)

    def make_terms(d, lo, hi):
        def body(b, _):
            for k in range(K):
                total = None
                for j in range(2):
                    code = pair_index[k, j, b]
                    s, t = code >> 2, code & 3
                    w = jnp.where(lane_half == (t & 1), pair_value[k, j, b], 0.0)
                    add = w * prod[d, b, (t >> 1) * 4 + s]
                    total = add if total is None else total + add
                even, odd = total[:, :8], total[:, 8:]
                low = lane_half == 0
                both = jnp.where(low, even, odd) + pltpu.roll(jnp.where(low, odd, even), P_SIZE, 2)
                for r in range(NZ):
                    terms[d, r % 2, r // 2, b * K + k] = both[r]
            return 0

        lax.fori_loop(lo, hi, body, 0)

    def mate_send(d):
        send(terms.at[d, 1 - core], mate_in.at[d], c_send.at[d], c_recv.at[d], mate)

    def x_step(d):
        arrived(mate_in.at[d], c_recv.at[d], c_send.at[d])
        for n, dx in enumerate((2, 1, -1, 0)):
            to = xi(dx)
            v = (terms[d, core, to] + mate_in[d, to]).reshape(SLOTS // 2, 16, 128)
            if dx == 0:
                x_own[d] = v
                continue
            q, code = encode(v)
            x_out[d, n, 0:SLOTS // 2] = q
            x_out[d, n, SLOTS // 2] = code
            send(x_out.at[d, n], x_in.at[d, n], x_send.at[d, n], x_recv.at[d, n], at_x(dx))

    def z_step(d):
        v = x_own[d]
        for n in (1, 2, 0):
            arrived(x_in.at[d, n], x_recv.at[d, n], x_send.at[d, n])
            v = v + decode(x_in[d, n])
        final[d, 0:SLOTS] = v.reshape(SLOTS, 8, 128)
        for dz in (4, 3, -3, 2, -2, 1, -1, 0):
            to = zi(dz)
            tiles = []
            for q in range(NY):
                for m in range(2):
                    tiles.append(final[d, pick[to * NY + q, m]])
            v = jnp.stack(tiles).reshape(NY, 16, 128)
            if dz == 0:
                z_own[d] = v
                continue
            n = dz % NZ - 1
            q, code = encode(v)
            z_out[d, n, 0:NY] = q
            z_out[d, n, NY] = code
            send(z_out.at[d, n], z_in.at[d, n], z_send.at[d, n], z_recv.at[d, n], at_zy(dz, 0))

    def y_step(d):
        for dz in (1, -1, 2, -2, 3, -3, 4):
            n = dz % NZ - 1
            arrived(z_in.at[d, n], z_recv.at[d, n], z_send.at[d, n])
        sums = [[None] * PER for _ in range(NY)]
        for n in range(NZ):
            src = z if n == 0 else zi(-n)
            v = z_own[d] if n == 0 else decode(z_in[d, n - 1])
            for q in range(NY):
                for m in range(2):
                    at = place[src * NY + q, m]
                    tile = v[q, 8 * m:8 * m + 8]
                    for c in range(PER):
                        add = jnp.where(at == c, 1.0, 0.0).astype(F32) * tile
                        sums[q][c] = add if sums[q][c] is None else sums[q][c] + add
        for q in range(NY):
            y_sum[d, q] = jnp.stack(sums[q])
        for n, dy in enumerate((2, 1, -1)):
            q, code = encode(y_sum[d, yi(dy)].reshape(PER // 2, 16, 128))
            y_out[d, n, 0:PER // 2] = q
            y_out[d, n, PER // 2] = code
            send(y_out.at[d, n], y_in.at[d, n], y_send.at[d, n], y_recv.at[d, n], at_zy(0, dy))
        out[:, yi(OFFS[d])] += y_sum[d, y]

    def out_step(d):
        for n, dy in ((1, -1), (2, 1), (0, 2)):
            arrived(y_in.at[d, n], y_recv.at[d, n], y_send.at[d, n])
            out[:, yi(dy + OFFS[d])] += decode(y_in[d, n]).reshape(PER, 8, 128)

    waited = False
    for kind, d, h, dz, links in ORDER:
        if kind == "F":
            g_wait(d, h, dz)
            g_fwd(d, h, dz, links)
        elif kind == "G":
            read_groups()
        elif kind == "I":
            read_picks()
        elif kind == "L":
            read_places()
        elif kind == "S":
            g_fwd(d, h, dz, links)
        elif kind == "P":
            if not waited:
                env_copy.wait()
                waited = True
            product(d, h)
        elif kind == "T":
            make_terms(d, 0, PER)
            mate_send(d)
        elif kind == "X":
            x_step(d)
        elif kind == "Z":
            z_step(d)
        elif kind == "Y":
            y_step(d)
        else:
            out_step(d)
    for c in pending:
        c.wait_send()


def shards(env_blocks, site_rows, route_dest, pair_index, pair_value):
    depth = env_blocks.shape[1]
    tile = (8, 128)
    tile16 = (16, 128)
    bf16 = jnp.bfloat16
    dma = pltpu.SemaphoreType.DMA
    out = pl.pallas_call(
        kernel,
        out_shape=jax.ShapeDtypeStruct((PER, NY, 8, 128), F32),
        in_specs=[pl.BlockSpec(memory_space=pltpu.SMEM)] * 3 + [pl.BlockSpec(memory_space=pl.ANY)] * 2,
        out_specs=pl.BlockSpec(memory_space=pltpu.VMEM),
        scratch_shapes=[
            pltpu.VMEM((PER, depth, PD * P_SIZE), bf16),
            pltpu.VMEM(site_rows.shape, bf16),
            pltpu.VMEM((NY, NZ, 64, depth), bf16),
            pltpu.VMEM((4, PER, 8, NZ, 16, 128), F32),
            pltpu.VMEM((4, 2, NX, SLOTS) + tile, F32),
            pltpu.VMEM((4, NX, SLOTS) + tile, F32),
            pltpu.VMEM((4, SLOTS // 2) + tile16, F32),
            pltpu.VMEM((4, 3, SLOTS // 2 + 1) + tile16, I16),
            pltpu.VMEM((4, 3, SLOTS // 2 + 1) + tile16, I16),
            pltpu.VMEM((4, SLOTS + 1) + tile, F32),
            pltpu.VMEM((4, NY) + tile16, F32),
            pltpu.VMEM((4, NZ - 1, NY + 1) + tile16, I16),
            pltpu.VMEM((4, NZ - 1, NY + 1) + tile16, I16),
            pltpu.VMEM((4, NY, PER) + tile, F32),
            pltpu.VMEM((4, 3, PER // 2 + 1) + tile16, I16),
            pltpu.VMEM((4, 3, PER // 2 + 1) + tile16, I16),
            pltpu.SMEM((NZ, SLOTS), jnp.int32),
            pltpu.SMEM((NZ, SLOTS), jnp.int32),
            pltpu.SMEM((NZ * NY, 2), jnp.int32),
            pltpu.SMEM((NZ * NY, 2), jnp.int32),
            dma((2,)),
            dma((62,)),
            dma((NY, 2, NZ)),
            dma((4,)),
            dma((4,)),
            dma((4, 3)),
            dma((4, 3)),
            dma((4, NZ - 1)),
            dma((4, NZ - 1)),
            dma((4, 3)),
            dma((4, 3)),
        ],
        compiler_params=pltpu.CompilerParams(
            collective_id=0, has_side_effects=True, vmem_limit_bytes=56 * 1024 * 1024
        ),
        cost_estimate=pl.CostEstimate(
            flops=2 * 2048 * depth * PER * 256, bytes_accessed=4 * 1024 * 1024, transcendentals=0
        ),
    )(route_dest.T, pair_index.transpose(1, 2, 0), pair_value.transpose(1, 2, 0), site_rows, env_blocks)
    return out.reshape(PER, -1)


def solution(mesh):
    in_specs = (
        P("chan", "row", None),
        P("chan", None, "row"),
        P(),
        P("chan", None, None),
        P("chan", None, None),
    )
    out_specs = P("chan", "row")
    return jax.shard_map(shards, mesh=mesh, in_specs=in_specs, out_specs=out_specs, check_vma=False)
```

```python
import jax
import jax.numpy as jnp
from jax import lax
from jax.experimental import pallas as pl
from jax.experimental.pallas import tpu as pltpu
from jax.sharding import PartitionSpec as P

PD = 4
P_SIZE = 64
K = 5
NZ, NY, NX = 8, 4, 4
PER = 6
SLOTS = PER * K
OFFS = (0, 1, -1, 2)
CUTS = ((0, 48), (48, 64))
CUTS_FAR = ((0, 32), (32, 64))
GROUPS = ((0, -1, 1, -2), (2, -3, 3, 4))
PAIRS = ((0, -1), (1, -2), (2, -3), (3, 4))
LINKS = ((1, 0), (-1, 0), (0, 1), (0, -1), (0, 2))
MESH = pl.DeviceIdType.MESH
F32 = jnp.float32
I16 = jnp.int16

ORDER = (
    ("F", 0, 1, 0, (0, 1, 2, 3, 4)),
    ("F", 0, 0, 0, (0, 1, 2, 3)),
    ("G", 0, 0, 0, ()),
    ("I", 0, 0, 0, ()),
    ("L", 0, 0, 0, ()),
    ("F", 0, 1, -1, (0,)),
    ("F", 0, 1, 1, (1,)),
    ("F", -1, 1, 0, ()),
    ("F", 1, 1, 0, ()),
    ("F", 2, 1, 0, ()),
    ("F", 0, 0, -1, (0, 2, 3)),
    ("F", 0, 0, 1, (1, 2, 3)),
    ("F", 1, 0, 0, ()),
    ("S", -1, 1, 0, (0,)),
    ("S", -1, 1, 0, (1,)),
    ("S", 1, 1, 0, (0,)),
    ("S", 1, 1, 0, (1,)),
    ("S", 2, 1, 0, (0,)),
    ("S", 2, 1, 0, (1,)),
    ("F", 0, 1, -2, (0,)),
    ("F", 0, 1, 2, (1,)),
    ("F", -1, 0, 0, ()),
    ("F", 0, 0, -2, (0, 2, 3)),
    ("F", -1, 0, -1, ()),
    ("F", 1, 0, -1, ()),
    ("F", 0, 0, 2, (1, 2, 3)),
    ("P", 0, 0, 0, ()),
    ("F", -1, 1, -1, (0,)),
    ("F", -1, 1, 1, (1,)),
    ("F", 1, 1, -1, (0,)),
    ("T", 0, 0, 0, ()),
    ("F", 1, 1, 1, (1,)),
    ("F", -1, 0, 1, ()),
    ("F", 1, 0, 1, ()),
    ("F", 2, 1, -1, (0,)),
    ("F", 2, 1, 1, (1,)),
    ("F", 0, 1, -3, ()),
    ("F", 0, 1, 3, (1,)),
    ("F", -1, 0, -2, ()),
    ("F", 1, 0, -2, ()),
    ("F", 0, 0, -3, (0, 2, 3)),
    ("F", 0, 0, 3, (2, 3)),
    ("F", -1, 1, -2, (0,)),
    ("F", -1, 0, 2, ()),
    ("F", 1, 0, 2, ()),
    ("P", 2, 0, 0, ()),
    ("F", -1, 1, 2, (1,)),
    ("F", 1, 1, -2, (0,)),
    ("F", 1, 1, 2, (1,)),
    ("T", 2, 0, 0, ()),
    ("P", 1, 0, 0, ()),
    ("F", 2, 1, -2, (0,)),
    ("F", 2, 1, 2, (1,)),
    ("T", 1, 0, 0, ()),
    ("F", 0, 1, 4, ()),
    ("F", -1, 0, -3, ()),
    ("F", 1, 0, -3, ()),
    ("F", -1, 1, 3, (1,)),
    ("F", 0, 0, 4, (2, 3)),
    ("S", -1, 0, 0, (2,)),
    ("S", -1, 0, -1, (2,)),
    ("S", 1, 0, 1, (3,)),
    ("S", 1, 0, -2, (3,)),
    ("S", -1, 0, 2, (2,)),
    ("S", -1, 0, -3, (2,)),
    ("F", 1, 1, 3, (1,)),
    ("P", 0, 1, 0, ()),
    ("F", -1, 1, -3, ()),
    ("F", -1, 0, 3, ()),
    ("F", 1, 0, 3, (3,)),
    ("F", 1, 1, -3, ()),
    ("T", 0, 1, 0, ()),
    ("F", 2, 1, 3, (1,)),
    ("F", -1, 1, 4, ()),
    ("F", 2, 1, -3, ()),
    ("F", 1, 1, 4, ()),
    ("X", 0, 0, 0, ()),
    ("F", -1, 0, 4, ()),
    ("F", 1, 0, 4, (3,)),
    ("P", 1, 1, 0, ()),
    ("T", 1, 1, 0, ()),
    ("F", 2, 1, 4, ()),
    ("F", 2, 0, 0, ()),
    ("F", 2, 0, 1, ()),
    ("P", 2, 1, 0, ()),
    ("T", 2, 1, 0, ()),
    ("F", 2, 0, -1, ()),
    ("F", 2, 0, -2, ()),
    ("P", 3, 0, 0, ()),
    ("X", 1, 0, 0, ()),
    ("F", 2, 0, 2, ()),
    ("F", 2, 0, 3, ()),
    ("T", 3, 0, 0, ()),
    ("X", 2, 0, 0, ()),
    ("Z", 0, 0, 0, ()),
    ("F", 2, 0, -3, ()),
    ("F", 2, 0, 4, ()),
    ("P", 3, 1, 0, ()),
    ("T", 3, 1, 0, ()),
    ("X", 3, 0, 0, ()),
    ("Z", 1, 0, 0, ()),
    ("Y", 0, 0, 0, ()),
    ("Z", 2, 0, 0, ()),
    ("Z", 3, 0, 0, ()),
    ("O", 0, 0, 0, ()),
    ("Y", 1, 0, 0, ()),
    ("O", 1, 0, 0, ()),
    ("Y", 2, 0, 0, ()),
    ("Y", 3, 0, 0, ()),
    ("O", 2, 0, 0, ()),
    ("O", 3, 0, 0, ()),
)


def encode(v):
    most = jnp.maximum(jnp.max(jnp.abs(v), axis=0), 1e-30)
    code = jnp.ceil(jnp.log2(most) * 8.0)
    inverse = 32000.0 / jnp.exp2(code * 0.125)
    q = jnp.round(v * inverse[None]).astype(jnp.int32).astype(I16)
    return q, code.astype(jnp.int32).astype(I16)


def decode(q):
    n = q.shape[0] - 1
    scale = jnp.exp2(q[n].astype(F32) * 0.125) * (1.0 / 32000.0)
    return q[0:n].astype(F32) * scale[None]


def kernel(
    route_hbm, index_hbm, value_hbm, site_hbm, env_hbm, out,
    env, site, g, prod, terms, mate_in, x_own, x_out, x_in, final, z_own, z_out, z_in, y_sum, y_out, y_in,
    route, pair_index, pair_value, group, local, pick, place,
    local_sem, g_send, g_recv, c_send, c_recv, x_send, x_recv, z_send, z_recv, y_send, y_recv,
):
    chan, row = lax.axis_index("chan"), lax.axis_index("row")
    z, y = chan // NY, lax.rem(chan, NY)
    x, core = row // 2, lax.rem(row, 2)

    def zi(d):
        return lax.rem(z + d + NZ, NZ)

    def yi(d):
        return lax.rem(y + d + NY, NY)

    def xi(d):
        return lax.rem(x + d + NX, NX)

    def at_zy(dz, dy):
        return (zi(dz) * NY + yi(dy), row)

    def at_x(d):
        return (chan, xi(d) * 2 + core)

    mate = (chan, x * 2 + 1 - core)

    barrier = pltpu.get_barrier_semaphore()
    partners = [mate] + [at_x(d) for d in (1, 2, 3)] + [at_zy(0, d) for d in (1, 2, 3)]
    partners += [at_zy(d, 0) for d in range(1, NZ)]
    for p in partners:
        pl.semaphore_signal(barrier, inc=1, device_id=p, device_id_type=MESH)
    site_copy = pltpu.make_async_copy(site_hbm, site, local_sem.at[1])
    site_copy.start()
    small_copies = [
        pltpu.make_async_copy(src, dst, local_sem.at[2 + n])
        for n, (src, dst) in enumerate(
            ((route_hbm, route), (index_hbm, pair_index), (value_hbm, pair_value))
        )
    ]
    for c in small_copies:
        c.start()
    env_copy = pltpu.make_async_copy(env_hbm, env, local_sem.at[0])
    env_copy.start()

    out[...] = jnp.zeros_like(out)
    for d in range(4):
        final[d, SLOTS] = jnp.zeros((8, 128), F32)
    new = lax.broadcasted_iota(jnp.int32, (64, 64), 0)
    old = lax.broadcasted_iota(jnp.int32, (64, 64), 1)
    moved = (new & 7) * 8 + ((new >> 3) & 1) * 4 + (new >> 4)
    turn = jnp.where(moved == old, 1.0, 0.0).astype(jnp.bfloat16)
    site_copy.wait()
    rows = site[...].astype(F32).reshape(64, site.shape[2]).astype(jnp.bfloat16)
    g[y, z] = jnp.dot(turn, rows, preferred_element_type=F32).astype(jnp.bfloat16)
    pl.semaphore_wait(barrier, len(partners))

    pending = []

    def send(src, dst, s_sem, r_sem, dev):
        c = pltpu.make_async_remote_copy(
            src_ref=src, dst_ref=dst, send_sem=s_sem, recv_sem=r_sem, device_id=dev, device_id_type=MESH
        )
        c.start()
        pending.append(c)

    def arrived(dst, r_sem, s_sem):
        pltpu.make_async_remote_copy(
            src_ref=dst, dst_ref=dst, send_sem=s_sem, recv_sem=r_sem, device_id=mate, device_id_type=MESH
        ).wait_recv()

    g_count = [0]

    def part(dy, h, dz):
        lo, hi = (CUTS_FAR if dy == 2 else CUTS)[h]
        return g.at[yi(dy), zi(dz), lo:hi]

    def g_fwd(dy, h, dz, links):
        for link in links:
            there = (dy - LINKS[link][1] + 1) % NY - 1
            to = 1 if link == 4 else h
            lo, hi = (CUTS_FAR if there == 2 else CUTS)[to]
            ref = g.at[yi(dy), zi(dz), lo:hi]
            send(ref, ref, g_send.at[g_count[0]], g_recv.at[yi(dy), to, zi(dz)], at_zy(*LINKS[link]))
            g_count[0] += 1

    def g_wait(dy, h, dz):
        if (dy, dz) != (0, 0):
            arrived(part(dy, h, dz), g_recv.at[yi(dy), h, zi(dz)], g_send.at[0])

    def read_groups():
        def body(src, _):
            for i in range(SLOTS):
                dest = route[i % K, (src * NY + y) * PER + i // K]
                here = (dest * 10923) >> 16
                group[src, i] = here
                local[src, i] = dest - here * PER
            return 0

        lax.fori_loop(0, NZ, body, 0)

    def read_picks():
        def body(h, _):
            first, last = jnp.int32(SLOTS), jnp.int32(SLOTS)
            for i in range(SLOTS):
                j = SLOTS - 1 - i
                first = jnp.where(group[z, j] == h, j, first)
                last = jnp.where(group[z, i] == h, i, last)
            pick[h, 0] = first
            pick[h, 1] = jnp.where(last == first, SLOTS, last)
            return 0

        lax.fori_loop(0, NZ * NY, body, 0)

    def read_places():
        def body(n, _):
            src, h = n // NY, z * NY + lax.rem(n, NY)
            first, last = jnp.int32(0), jnp.int32(0)
            for i in range(SLOTS):
                j = SLOTS - 1 - i
                first = jnp.where(group[src, j] == h, local[src, j], first)
                last = jnp.where(group[src, i] == h, local[src, i], last)
            place[n, 0] = first
            place[n, 1] = last
            return 0

        lax.fori_loop(0, NZ * NY, body, 0)

    lane_half = lax.broadcasted_iota(jnp.int32, (1, 1, 128), 2) // P_SIZE

    def product(d, half):
        a = yi(OFFS[d])
        at = [zi(dz) for dz in GROUPS[half]]
        lhs = jnp.concatenate([g[a, i] for i in at], axis=0)
        for b in range(PER):
            v = jnp.dot(lhs, env[b], preferred_element_type=F32).reshape(4, 4, 16, 256)
            for s in range(4):
                for t in range(2):
                    prod[d, b, t * 4 + s, 4 * half:4 * half + 4] = v[:, s, :, 128 * t:128 * (t + 1)]

    def make_terms(d, half):
        low = lane_half == 0

        def body(i, _):
            tiles = []
            for n in range(3 * K):
                b, k, total = 3 * i + n // K, n % K, None
                for j in range(2):
                    code = pair_index[k, j, b]
                    s, t = code >> 2, code & 3
                    w = jnp.where(lane_half == (t & 1), pair_value[k, j, b], 0.0)
                    add = w * prod[d, b, (t >> 1) * 4 + s, 4 * half:4 * half + 4]
                    total = add if total is None else total + add
                even, odd = total[:, :8], total[:, 8:]
                tiles.append(jnp.where(low, even, odd) + pltpu.roll(jnp.where(low, odd, even), P_SIZE, 2))
            for k in range(3 * K):
                for n, dz in enumerate(GROUPS[half]):
                    terms[d, dz % NZ, 3 * K * i + k] = tiles[k][n]
            return 0

        lax.fori_loop(0, PER // 3, body, 0)

    def mate_send(d, half):
        for n in (0, 1):
            lo, hi = PAIRS[2 * half + n]
            odd = lax.rem(zi(lo), 2) == core
            theirs = jnp.where(odd, zi(hi), zi(lo)) // 2
            src = terms.at[d, jnp.where(odd, hi % NZ, lo % NZ)]
            send(src, mate_in.at[d, theirs], c_send.at[d, 2 * half + n], c_recv.at[d, 2 * half + n], mate)

    def mate_wait(d):
        for n, (lo, hi) in enumerate(PAIRS):
            mine = jnp.where(lax.rem(zi(lo), 2) == core, zi(lo), zi(hi))
            arrived(mate_in.at[d, mine // 2], c_recv.at[d, n], c_send.at[d, n])

    def x_step(d):
        mate_wait(d)
        for n, dx in enumerate((2, 1, -1, 0)):
            to = xi(dx)
            v = (terms[d, lax.rem(2 * to + core - z + NZ, NZ)] + mate_in[d, to]).reshape(SLOTS // 2, 16, 128)
            if dx == 0:
                x_own[d] = v
                continue
            q, code = encode(v)
            x_out[d, n, 0:SLOTS // 2] = q
            x_out[d, n, SLOTS // 2] = code
            send(x_out.at[d, n], x_in.at[d, n], x_send.at[d, n], x_recv.at[d, n], at_x(dx))

    def z_step(d):
        v = x_own[d]
        for n in (1, 2, 0):
            arrived(x_in.at[d, n], x_recv.at[d, n], x_send.at[d, n])
            v = v + decode(x_in[d, n])
        final[d, 0:SLOTS] = v.reshape(SLOTS, 8, 128)
        for dz in (4, 3, -3, 2, -2, 1, -1, 0):
            to = zi(dz)
            tiles = []
            for q in range(NY):
                for m in range(2):
                    tiles.append(final[d, pick[to * NY + q, m]])
            v = jnp.stack(tiles).reshape(NY, 16, 128)
            if dz == 0:
                z_own[d] = v
                continue
            n = dz % NZ - 1
            q, code = encode(v)
            z_out[d, n, 0:NY] = q
            z_out[d, n, NY] = code
            send(z_out.at[d, n], z_in.at[d, n], z_send.at[d, n], z_recv.at[d, n], at_zy(dz, 0))

    def y_step(d):
        for dz in (1, -1, 2, -2, 3, -3, 4):
            n = dz % NZ - 1
            arrived(z_in.at[d, n], z_recv.at[d, n], z_send.at[d, n])
        sums = [[None] * PER for _ in range(NY)]
        for n in range(NZ):
            src = z if n == 0 else zi(-n)
            v = z_own[d] if n == 0 else decode(z_in[d, n - 1])
            for q in range(NY):
                for m in range(2):
                    at = place[src * NY + q, m]
                    tile = v[q, 8 * m:8 * m + 8]
                    spread = jnp.full((8, 128), at, jnp.int32)
                    for c in range(PER):
                        add = jnp.where(spread == c, tile, 0.0)
                        sums[q][c] = add if sums[q][c] is None else sums[q][c] + add
        for q in range(NY):
            y_sum[d, q] = jnp.stack(sums[q])
        for n, dy in enumerate((2, 1, -1)):
            q, code = encode(y_sum[d, yi(dy)].reshape(PER // 2, 16, 128))
            y_out[d, n, 0:PER // 2] = q
            y_out[d, n, PER // 2] = code
            send(y_out.at[d, n], y_in.at[d, n], y_send.at[d, n], y_recv.at[d, n], at_zy(0, dy))
        out[:, yi(OFFS[d])] += y_sum[d, y]

    def out_step(d):
        for n, dy in ((1, -1), (2, 1), (0, 2)):
            arrived(y_in.at[d, n], y_recv.at[d, n], y_send.at[d, n])
            out[:, yi(dy + OFFS[d])] += decode(y_in[d, n]).reshape(PER, 8, 128)

    waited = False
    for kind, d, h, dz, links in ORDER:
        if kind == "F":
            g_wait(d, h, dz)
            g_fwd(d, h, dz, links)
        elif kind == "G":
            for c in small_copies:
                c.wait()
            read_groups()
        elif kind == "I":
            read_picks()
        elif kind == "L":
            read_places()
        elif kind == "S":
            g_fwd(d, h, dz, links)
        elif kind == "P":
            if not waited:
                env_copy.wait()
                waited = True
            product(d, h)
        elif kind == "T":
            make_terms(d, h)
            mate_send(d, h)
        else:
            early = len(pending)
            {"X": x_step, "Z": z_step, "Y": y_step, "O": out_step}[kind](d)
            if d == 3:
                for c in pending[:early]:
                    c.wait_send()
                del pending[:early]
    for c in pending:
        c.wait_send()


def shards(env_blocks, site_rows, route_dest, pair_index, pair_value):
    depth = env_blocks.shape[1]
    tile = (8, 128)
    tile16 = (16, 128)
    bf16 = jnp.bfloat16
    dma = pltpu.SemaphoreType.DMA
    out = pl.pallas_call(
        kernel,
        out_shape=jax.ShapeDtypeStruct((PER, NY, 8, 128), F32),
        in_specs=[pl.BlockSpec(memory_space=pl.ANY)] * 5,
        out_specs=pl.BlockSpec(memory_space=pltpu.VMEM),
        scratch_shapes=[
            pltpu.VMEM((PER, depth, PD * P_SIZE), bf16),
            pltpu.VMEM(site_rows.shape, bf16),
            pltpu.VMEM((NY, NZ, 64, depth), bf16),
            pltpu.VMEM((4, PER, 8, NZ, 16, 128), F32),
            pltpu.VMEM((4, NZ, SLOTS) + tile, F32),
            pltpu.VMEM((4, NX, SLOTS) + tile, F32),
            pltpu.VMEM((4, SLOTS // 2) + tile16, F32),
            pltpu.VMEM((4, 3, SLOTS // 2 + 1) + tile16, I16),
            pltpu.VMEM((4, 3, SLOTS // 2 + 1) + tile16, I16),
            pltpu.VMEM((4, SLOTS + 1) + tile, F32),
            pltpu.VMEM((4, NY) + tile16, F32),
            pltpu.VMEM((4, NZ - 1, NY + 1) + tile16, I16),
            pltpu.VMEM((4, NZ - 1, NY + 1) + tile16, I16),
            pltpu.VMEM((4, NY, PER) + tile, F32),
            pltpu.VMEM((4, 3, PER // 2 + 1) + tile16, I16),
            pltpu.VMEM((4, 3, PER // 2 + 1) + tile16, I16),
            pltpu.SMEM((K, NZ * NY * PER), jnp.int32),
            pltpu.SMEM((K, 2, PER), jnp.int32),
            pltpu.SMEM((K, 2, PER), F32),
            pltpu.SMEM((NZ, SLOTS), jnp.int32),
            pltpu.SMEM((NZ, SLOTS), jnp.int32),
            pltpu.SMEM((NZ * NY, 2), jnp.int32),
            pltpu.SMEM((NZ * NY, 2), jnp.int32),
            dma((5,)),
            dma((62,)),
            dma((NY, 3, NZ)),
            dma((4, 4)),
            dma((4, 4)),
            dma((4, 3)),
            dma((4, 3)),
            dma((4, NZ - 1)),
            dma((4, NZ - 1)),
            dma((4, 3)),
            dma((4, 3)),
        ],
        compiler_params=pltpu.CompilerParams(
            collective_id=0, has_side_effects=True, vmem_limit_bytes=56 * 1024 * 1024
        ),
        cost_estimate=pl.CostEstimate(
            flops=2 * 2048 * depth * PER * 256, bytes_accessed=4 * 1024 * 1024, transcendentals=0
        ),
    )(route_dest.T, pair_index.transpose(1, 2, 0), pair_value.transpose(1, 2, 0), site_rows, env_blocks)
    return out.reshape(PER, -1)


def solution(mesh):
    in_specs = (
        P("chan", "row", None),
        P("chan", None, "row"),
        P(),
        P("chan", None, None),
        P("chan", None, None),
    )
    out_specs = P("chan", "row")
    return jax.shard_map(shards, mesh=mesh, in_specs=in_specs, out_specs=out_specs, check_vma=False)
```

```python
import jax
import jax.numpy as jnp
from jax import lax
from jax.experimental import pallas as pl
from jax.experimental.pallas import tpu as pltpu
from jax.sharding import PartitionSpec as P

PD = 4
P_SIZE = 64
K = 5
NZ, NY, NX = 8, 4, 4
PER = 6
SLOTS = PER * K
OFFS = (0, 1, -1, 2)
CUTS = ((0, 48), (48, 64))
CUTS_FAR = ((0, 32), (32, 64))
GROUPS = ((0, -1, 1, -2), (2, -3, 3, 4))
PAIRS = ((0, -1), (1, -2), (2, -3), (3, 4))
LINKS = ((1, 0), (-1, 0), (0, 1), (0, -1), (0, 2))
MESH = pl.DeviceIdType.MESH
F32 = jnp.float32
I16 = jnp.int16

PARTS = tuple((dy, h, dz) for dy in OFFS for h in range(len(CUTS_FAR if dy == 2 else CUTS)) for dz in range(-3, 5) if (dy, dz) != (0, 0))
SHARED = {
    0: ((2, 0, 0), (2, 0, -1), (2, 0, 1), (2, 0, -2)),
    1: ((2, 0, 2), (2, 0, -3), (2, 0, 3), (2, 0, 4)),
    2: ((-1, 0, 1), (-1, 0, -2)),
    3: ((-1, 0, 3), (-1, 0, 4)),
    4: ((1, 0, 0), (1, 0, -1)),
    5: ((1, 0, 2), (1, 0, -3)),
}
SEMS = {part: n for n, parts in SHARED.items() for part in parts}
SEMS.update({part: len(SHARED) + n for n, part in enumerate(p for p in PARTS if p not in SEMS)})

ORDER = (
    ("F", 0, 1, 0, (0, 1, 2, 3, 4)),
    ("F", 0, 0, 0, (0, 1, 2, 3)),
    ("G", 0, 0, 0, ()),
    ("I", 0, 0, 0, ()),
    ("L", 0, 0, 0, ()),
    ("F", 0, 1, -1, (0,)),
    ("F", 0, 1, 1, (1,)),
    ("F", -1, 1, 0, ()),
    ("F", 1, 1, 0, ()),
    ("F", 2, 1, 0, ()),
    ("F", 0, 0, -1, (0, 2, 3)),
    ("F", 0, 0, 1, (1, 2, 3)),
    ("F", 1, 0, 0, ()),
    ("S", -1, 1, 0, (0,)),
    ("S", -1, 1, 0, (1,)),
    ("S", 1, 1, 0, (0,)),
    ("S", 1, 1, 0, (1,)),
    ("S", 2, 1, 0, (0,)),
    ("S", 2, 1, 0, (1,)),
    ("F", 0, 1, -2, (0,)),
    ("F", 0, 1, 2, (1,)),
    ("F", -1, 0, 0, ()),
    ("F", 0, 0, -2, (0, 2, 3)),
    ("F", -1, 0, -1, ()),
    ("F", 1, 0, -1, ()),
    ("F", 0, 0, 2, (1, 2, 3)),
    ("P", 0, 0, 0, ()),
    ("F", -1, 1, -1, (0,)),
    ("F", -1, 1, 1, (1,)),
    ("F", 1, 1, -1, (0,)),
    ("T", 0, 0, 0, ()),
    ("F", 1, 1, 1, (1,)),
    ("F", -1, 0, 1, ()),
    ("F", 1, 0, 1, ()),
    ("F", 2, 1, -1, (0,)),
    ("F", 2, 1, 1, (1,)),
    ("F", 0, 1, -3, ()),
    ("F", 0, 1, 3, (1,)),
    ("F", -1, 0, -2, ()),
    ("F", 1, 0, -2, ()),
    ("F", 0, 0, -3, (0, 2, 3)),
    ("F", 0, 0, 3, (2, 3)),
    ("F", -1, 1, -2, (0,)),
    ("F", -1, 0, 2, ()),
    ("F", 1, 0, 2, ()),
    ("P", 2, 0, 0, ()),
    ("F", -1, 1, 2, (1,)),
    ("F", 1, 1, -2, (0,)),
    ("F", 1, 1, 2, (1,)),
    ("T", 2, 0, 0, ()),
    ("P", 1, 0, 0, ()),
    ("F", 2, 1, -2, (0,)),
    ("F", 2, 1, 2, (1,)),
    ("T", 1, 0, 0, ()),
    ("F", 0, 1, 4, ()),
    ("F", -1, 0, -3, ()),
    ("F", 1, 0, -3, ()),
    ("F", -1, 1, 3, (1,)),
    ("F", 0, 0, 4, (2, 3)),
    ("S", -1, 0, 0, (2,)),
    ("S", -1, 0, -1, (2,)),
    ("S", 1, 0, 1, (3,)),
    ("S", 1, 0, -2, (3,)),
    ("S", -1, 0, 2, (2,)),
    ("S", -1, 0, -3, (2,)),
    ("F", 1, 1, 3, (1,)),
    ("P", 0, 1, 0, ()),
    ("F", -1, 1, -3, ()),
    ("F", -1, 0, 3, ()),
    ("F", 1, 0, 3, (3,)),
    ("F", 1, 1, -3, ()),
    ("T", 0, 1, 0, ()),
    ("F", 2, 1, 3, (1,)),
    ("F", -1, 1, 4, ()),
    ("F", 2, 1, -3, ()),
    ("F", 1, 1, 4, ()),
    ("X", 0, 0, 0, ()),
    ("F", -1, 0, 4, ()),
    ("F", 1, 0, 4, (3,)),
    ("P", 1, 1, 0, ()),
    ("T", 1, 1, 0, ()),
    ("F", 2, 1, 4, ()),
    ("F", 2, 0, 0, ()),
    ("F", 2, 0, 1, ()),
    ("P", 2, 1, 0, ()),
    ("T", 2, 1, 0, ()),
    ("F", 2, 0, -1, ()),
    ("F", 2, 0, -2, ()),
    ("P", 3, 0, 0, ()),
    ("X", 1, 0, 0, ()),
    ("F", 2, 0, 2, ()),
    ("F", 2, 0, 3, ()),
    ("T", 3, 0, 0, ()),
    ("X", 2, 0, 0, ()),
    ("Z", 0, 0, 0, ()),
    ("F", 2, 0, -3, ()),
    ("F", 2, 0, 4, ()),
    ("P", 3, 1, 0, ()),
    ("T", 3, 1, 0, ()),
    ("X", 3, 0, 0, ()),
    ("Z", 1, 0, 0, ()),
    ("Y", 0, 0, 0, ()),
    ("Z", 2, 0, 0, ()),
    ("Z", 3, 0, 0, ()),
    ("O", 0, 0, 0, ()),
    ("Y", 1, 0, 0, ()),
    ("O", 1, 0, 0, ()),
    ("Y", 2, 0, 0, ()),
    ("Y", 3, 0, 0, ()),
    ("O", 2, 0, 0, ()),
    ("O", 3, 0, 0, ()),
)


def encode(v):
    most = jnp.maximum(jnp.max(jnp.abs(v), axis=0), 1e-30)
    code = jnp.ceil(jnp.log2(most) * 8.0)
    inverse = 32000.0 / jnp.exp2(code * 0.125)
    q = jnp.round(v * inverse[None]).astype(jnp.int32).astype(I16)
    return q, code.astype(jnp.int32).astype(I16)


def decode(q):
    n = q.shape[0] - 1
    scale = jnp.exp2(q[n].astype(F32) * 0.125) * (1.0 / 32000.0)
    return q[0:n].astype(F32) * scale[None]


def kernel(
    route_hbm, index_hbm, value_hbm, site_hbm, env_hbm, out,
    env, site, g, prod, terms, mate_in, x_own, x_out, x_in, final, z_own, z_out, z_in, y_sum, y_out, y_in,
    route, pair_index, pair_value, group, local, pick, place,
    local_sem, sent, g_recv, c_recv, x_recv, z_recv, y_recv,
):
    chan, row = lax.axis_index("chan"), lax.axis_index("row")
    z, y = chan // NY, lax.rem(chan, NY)
    x, core = row // 2, lax.rem(row, 2)

    def zi(d):
        return lax.rem(z + d + NZ, NZ)

    def yi(d):
        return lax.rem(y + d + NY, NY)

    def xi(d):
        return lax.rem(x + d + NX, NX)

    def at_zy(dz, dy):
        return (zi(dz) * NY + yi(dy), row)

    def at_x(d):
        return (chan, xi(d) * 2 + core)

    mate = (chan, x * 2 + 1 - core)

    barrier = pltpu.get_barrier_semaphore()
    partners = [mate] + [at_x(d) for d in (1, 2, 3)] + [at_zy(0, d) for d in (1, 2, 3)]
    partners += [at_zy(d, 0) for d in range(1, NZ)]
    for p in partners:
        pl.semaphore_signal(barrier, inc=1, device_id=p, device_id_type=MESH)
    site_copy = pltpu.make_async_copy(site_hbm, site, local_sem.at[1])
    site_copy.start()
    small_copies = [
        pltpu.make_async_copy(src, dst, local_sem.at[2 + n])
        for n, (src, dst) in enumerate(
            ((route_hbm, route), (index_hbm, pair_index), (value_hbm, pair_value))
        )
    ]
    for c in small_copies:
        c.start()
    env_copy = pltpu.make_async_copy(env_hbm, env, local_sem.at[0])
    env_copy.start()

    out[...] = jnp.zeros_like(out)
    for d in range(4):
        final[d, SLOTS] = jnp.zeros((8, 128), F32)
    new = lax.broadcasted_iota(jnp.int32, (64, 64), 0)
    old = lax.broadcasted_iota(jnp.int32, (64, 64), 1)
    moved = (new & 7) * 8 + ((new >> 3) & 1) * 4 + (new >> 4)
    turn = jnp.where(moved == old, 1.0, 0.0).astype(jnp.bfloat16)
    site_copy.wait()
    rows = site[...].astype(F32).reshape(64, site.shape[2]).astype(jnp.bfloat16)
    g[y * NZ + z] = jnp.dot(turn, rows, preferred_element_type=F32).astype(jnp.bfloat16)
    pl.semaphore_wait(barrier, len(partners))

    def send(src, dst, s_sem, r_sem, dev):
        pltpu.make_async_remote_copy(
            src_ref=src, dst_ref=dst, send_sem=s_sem, recv_sem=r_sem, device_id=dev, device_id_type=MESH
        ).start()

    def arrived(like, r_sem):
        pltpu.make_async_remote_copy(
            src_ref=like, dst_ref=like, send_sem=sent.at[0], recv_sem=r_sem, device_id=mate, device_id_type=MESH
        ).wait_recv()

    def all_sent(like, n):
        pltpu.make_async_remote_copy(
            src_ref=like, dst_ref=like, send_sem=sent.at[n], recv_sem=g_recv.at[0], device_id=mate, device_id_type=MESH
        ).wait_send()

    def g_fwd(dy, h, dz, links):
        for link in links:
            step_z, step_y = LINKS[link]
            there = ((dy - step_y + 1) % NY - 1, 1 if link == 4 else h, (dz - step_z + 3) % NZ - 3)
            lo, hi = (CUTS_FAR if there[0] == 2 else CUTS)[there[1]]
            ref = g.at[yi(dy) * NZ + zi(dz), lo:hi]
            send(ref, ref, sent.at[0], g_recv.at[SEMS[there]], at_zy(step_z, step_y))

    seen = {n: 0 for n in SEMS.values()}

    def g_wait(dy, h, dz):
        n = SEMS.get((dy, h, dz))
        if n is None:
            return
        seen[n] += 1
        count = len(SHARED.get(n, (0,)))
        if seen[n] == count:
            lo, hi = (CUTS_FAR if dy == 2 else CUTS)[h]
            arrived(g.at[0:count, lo:hi], g_recv.at[n])

    def read_groups():
        def body(src, _):
            for i in range(SLOTS):
                dest = route[i % K, (src * NY + y) * PER + i // K]
                here = (dest * 10923) >> 16
                group[src, i] = here
                local[src, i] = dest - here * PER
            return 0

        lax.fori_loop(0, NZ, body, 0)

    def read_picks():
        def body(h, _):
            first, last = jnp.int32(SLOTS), jnp.int32(SLOTS)
            for i in range(SLOTS):
                j = SLOTS - 1 - i
                first = jnp.where(group[z, j] == h, j, first)
                last = jnp.where(group[z, i] == h, i, last)
            pick[h, 0] = first
            pick[h, 1] = jnp.where(last == first, SLOTS, last)
            return 0

        lax.fori_loop(0, NZ * NY, body, 0)

    def read_places():
        def body(n, _):
            src, h = n // NY, z * NY + lax.rem(n, NY)
            first, last = jnp.int32(0), jnp.int32(0)
            for i in range(SLOTS):
                j = SLOTS - 1 - i
                first = jnp.where(group[src, j] == h, local[src, j], first)
                last = jnp.where(group[src, i] == h, local[src, i], last)
            place[n, 0] = first
            place[n, 1] = last
            return 0

        lax.fori_loop(0, NZ * NY, body, 0)

    lane_half = lax.broadcasted_iota(jnp.int32, (1, 1, 128), 2) // P_SIZE

    def product(d, half):
        a = yi(OFFS[d])
        at = [zi(dz) for dz in GROUPS[half]]
        lhs = jnp.concatenate([g[a * NZ + i] for i in at], axis=0)
        for b in range(PER):
            v = jnp.dot(lhs, env[b], preferred_element_type=F32).reshape(4, 4, 16, 256)
            for s in range(4):
                for t in range(2):
                    prod[d, b, t * 4 + s, 4 * half:4 * half + 4] = v[:, s, :, 128 * t:128 * (t + 1)]

    def make_terms(d, half):
        low = lane_half == 0

        def body(i, _):
            tiles = []
            for n in range(3 * K):
                b, k, total = 3 * i + n // K, n % K, None
                for j in range(2):
                    code = pair_index[k, j, b]
                    s, t = code >> 2, code & 3
                    w = jnp.where(lane_half == (t & 1), pair_value[k, j, b], 0.0)
                    add = w * prod[d, b, (t >> 1) * 4 + s, 4 * half:4 * half + 4]
                    total = add if total is None else total + add
                even, odd = total[:, :8], total[:, 8:]
                tiles.append(jnp.where(low, even, odd) + pltpu.roll(jnp.where(low, odd, even), P_SIZE, 2))
            for k in range(3 * K):
                for n, dz in enumerate(GROUPS[half]):
                    terms[d, dz % NZ, 3 * K * i + k] = tiles[k][n]
            return 0

        lax.fori_loop(0, PER // 3, body, 0)

    def mate_send(d, half):
        for n in (0, 1):
            lo, hi = PAIRS[2 * half + n]
            odd = lax.rem(zi(lo), 2) == core
            theirs = jnp.where(odd, zi(hi), zi(lo)) // 2
            src = terms.at[d, jnp.where(odd, hi % NZ, lo % NZ)]
            send(src, mate_in.at[d, theirs], sent.at[1], c_recv.at[d], mate)

    def x_step(d):
        arrived(mate_in.at[d], c_recv.at[d])
        for n, dx in enumerate((2, 1, -1, 0)):
            to = xi(dx)
            v = (terms[d, lax.rem(2 * to + core - z + NZ, NZ)] + mate_in[d, to]).reshape(SLOTS // 2, 16, 128)
            if dx == 0:
                x_own[d] = v
                continue
            q, code = encode(v)
            x_out[d, n, 0:SLOTS // 2] = q
            x_out[d, n, SLOTS // 2] = code
            send(x_out.at[d, n], x_in.at[d, n], sent.at[2], x_recv.at[d], at_x(dx))

    def z_step(d):
        arrived(x_in.at[d], x_recv.at[d])
        v = x_own[d]
        for n in range(3):
            v = v + decode(x_in[d, n])
        final[d, 0:SLOTS] = v.reshape(SLOTS, 8, 128)
        for dz in (4, 3, -3, 2, -2, 1, -1, 0):
            to = zi(dz)
            tiles = []
            for q in range(NY):
                for m in range(2):
                    tiles.append(final[d, pick[to * NY + q, m]])
            v = jnp.stack(tiles).reshape(NY, 16, 128)
            if dz == 0:
                z_own[d] = v
                continue
            n = dz % NZ - 1
            q, code = encode(v)
            z_out[d, n, 0:NY] = q
            z_out[d, n, NY] = code
            send(z_out.at[d, n], z_in.at[d, n], sent.at[3], z_recv.at[d], at_zy(dz, 0))

    def y_step(d):
        arrived(z_in.at[d], z_recv.at[d])
        sums = [[None] * PER for _ in range(NY)]
        for n in range(NZ):
            src = z if n == 0 else zi(-n)
            v = z_own[d] if n == 0 else decode(z_in[d, n - 1])
            for q in range(NY):
                for m in range(2):
                    at = place[src * NY + q, m]
                    tile = v[q, 8 * m:8 * m + 8]
                    spread = jnp.full((8, 128), at, jnp.int32)
                    for c in range(PER):
                        add = jnp.where(spread == c, tile, 0.0)
                        sums[q][c] = add if sums[q][c] is None else sums[q][c] + add
        for q in range(NY):
            y_sum[d, q] = jnp.stack(sums[q])
        for n, dy in enumerate((2, 1, -1)):
            q, code = encode(y_sum[d, yi(dy)].reshape(PER // 2, 16, 128))
            y_out[d, n, 0:PER // 2] = q
            y_out[d, n, PER // 2] = code
            send(y_out.at[d, n], y_in.at[d, n], sent.at[4], y_recv.at[d], at_zy(0, dy))
        out[:, yi(OFFS[d])] += y_sum[d, y]

    def out_step(d):
        arrived(y_in.at[d], y_recv.at[d])
        for n, dy in ((1, -1), (2, 1), (0, 2)):
            out[:, yi(dy + OFFS[d])] += decode(y_in[d, n]).reshape(PER, 8, 128)

    env_here = False
    for kind, d, h, dz, links in ORDER:
        if kind == "F":
            g_wait(d, h, dz)
            g_fwd(d, h, dz, links)
        elif kind == "G":
            for c in small_copies:
                c.wait()
            read_groups()
        elif kind == "I":
            read_picks()
        elif kind == "L":
            read_places()
        elif kind == "S":
            g_fwd(d, h, dz, links)
        elif kind == "P":
            if not env_here:
                env_copy.wait()
                env_here = True
            product(d, h)
        elif kind == "T":
            make_terms(d, h)
            mate_send(d, h)
        else:
            {"X": x_step, "Z": z_step, "Y": y_step, "O": out_step}[kind](d)
            if (kind, d) == ("X", 3):
                all_sent(g.at[0:NY * NZ - 1], 0)
                all_sent(mate_in, 1)
            if (kind, d) == ("Y", 3):
                all_sent(x_in, 2)
                all_sent(z_in, 3)
    all_sent(y_in, 4)


def shards(env_blocks, site_rows, route_dest, pair_index, pair_value):
    depth = env_blocks.shape[1]
    tile = (8, 128)
    tile16 = (16, 128)
    bf16 = jnp.bfloat16
    dma = pltpu.SemaphoreType.DMA
    out = pl.pallas_call(
        kernel,
        out_shape=jax.ShapeDtypeStruct((PER, NY, 8, 128), F32),
        in_specs=[pl.BlockSpec(memory_space=pl.ANY)] * 5,
        out_specs=pl.BlockSpec(memory_space=pltpu.VMEM),
        scratch_shapes=[
            pltpu.VMEM((PER, depth, PD * P_SIZE), bf16),
            pltpu.VMEM(site_rows.shape, bf16),
            pltpu.VMEM((NY * NZ, 64, depth), bf16),
            pltpu.VMEM((4, PER, 8, NZ, 16, 128), F32),
            pltpu.VMEM((4, NZ, SLOTS) + tile, F32),
            pltpu.VMEM((4, NX, SLOTS) + tile, F32),
            pltpu.VMEM((4, SLOTS // 2) + tile16, F32),
            pltpu.VMEM((4, 3, SLOTS // 2 + 1) + tile16, I16),
            pltpu.VMEM((4, 3, SLOTS // 2 + 1) + tile16, I16),
            pltpu.VMEM((4, SLOTS + 1) + tile, F32),
            pltpu.VMEM((4, NY) + tile16, F32),
            pltpu.VMEM((4, NZ - 1, NY + 1) + tile16, I16),
            pltpu.VMEM((4, NZ - 1, NY + 1) + tile16, I16),
            pltpu.VMEM((4, NY, PER) + tile, F32),
            pltpu.VMEM((4, 3, PER // 2 + 1) + tile16, I16),
            pltpu.VMEM((4, 3, PER // 2 + 1) + tile16, I16),
            pltpu.SMEM((K, NZ * NY * PER), jnp.int32),
            pltpu.SMEM((K, 2, PER), jnp.int32),
            pltpu.SMEM((K, 2, PER), F32),
            pltpu.SMEM((NZ, SLOTS), jnp.int32),
            pltpu.SMEM((NZ, SLOTS), jnp.int32),
            pltpu.SMEM((NZ * NY, 2), jnp.int32),
            pltpu.SMEM((NZ * NY, 2), jnp.int32),
            dma((5,)),
            dma((5,)),
            dma((max(SEMS.values()) + 1,)),
            dma((4,)),
            dma((4,)),
            dma((4,)),
            dma((4,)),
        ],
        compiler_params=pltpu.CompilerParams(
            collective_id=0, has_side_effects=True, vmem_limit_bytes=56 * 1024 * 1024
        ),
        cost_estimate=pl.CostEstimate(
            flops=2 * 2048 * depth * PER * 256, bytes_accessed=4 * 1024 * 1024, transcendentals=0
        ),
    )(route_dest.T, pair_index.transpose(1, 2, 0), pair_value.transpose(1, 2, 0), site_rows, env_blocks)
    return out.reshape(PER, -1)


def solution(mesh):
    in_specs = (
        P("chan", "row", None),
        P("chan", None, "row"),
        P(),
        P("chan", None, None),
        P("chan", None, None),
    )
    out_specs = P("chan", "row")
    return jax.shard_map(shards, mesh=mesh, in_specs=in_specs, out_specs=out_specs, check_vma=False)
```

```python
import jax
import jax.numpy as jnp
from jax import lax
from jax.experimental import pallas as pl
from jax.experimental.pallas import tpu as pltpu
from jax.sharding import PartitionSpec as P

PD = 4
P_SIZE = 64
K = 5
NZ, NY, NX = 8, 4, 4
PER = 6
SLOTS = PER * K
OFFS = (0, 1, -1, 2)
OWN = ((0, 32), (32, 48), (48, 64))
NEAR = ((0, 48), (48, 64))
FAR = ((0, 32), (32, 64))
GROUPS = ((0, -1, 1, -2), (2, -3, 3, 4))
PAIRS = ((0, -1), (1, -2), (2, -3), (3, 4))
LINKS = ((1, 0), (-1, 0), (0, 1), (0, -1), (0, 2))
MESH = pl.DeviceIdType.MESH
F32 = jnp.float32
I16 = jnp.int16

def cut(dy, part):
    return (OWN if dy == 0 else FAR if dy == 2 else NEAR)[part]


PARTS = tuple(
    (dy, part, dz)
    for dy in OFFS
    for part in range(len(OWN) if dy == 0 else 2)
    for dz in range(-3, 5)
    if (dy, dz) != (0, 0)
)
SHARED = {
    0: ((2, 0, 0), (2, 0, -1), (2, 0, 1), (2, 0, -2)),
    1: ((2, 0, 2), (2, 0, -3), (2, 0, 3), (2, 0, 4)),
    2: ((-1, 0, 1), (-1, 0, -2)),
    3: ((-1, 0, 3), (-1, 0, 4)),
    4: ((1, 0, 0), (1, 0, -1)),
    5: ((1, 0, 2), (1, 0, -3)),
}
SEMS = {part: n for n, parts in SHARED.items() for part in parts}
SEMS.update({part: len(SHARED) + n for n, part in enumerate(p for p in PARTS if p not in SEMS)})

ORDER = (
    ("F", 0, 2, 0, (0, 1)),
    ("F", 0, 1, 0, (0, 1)),
    ("F", 0, 0, 0, (0, 1)),
    ("S", 0, 11, 0, (2, 3, 4)),
    ("S", 0, 10, 0, (2, 3)),
    ("G", 0, 0, 0, ()),
    ("I", 0, 0, 0, ()),
    ("L", 0, 0, 0, ()),
    ("F", 0, 2, -1, (0,)),
    ("F", 0, 2, 1, (1,)),
    ("F", -1, 1, 0, ()),
    ("F", 1, 1, 0, ()),
    ("F", 0, 1, -1, (0,)),
    ("F", 0, 1, 1, (1,)),
    ("F", 2, 1, 0, ()),
    ("F", 0, 0, -1, (0,)),
    ("S", 0, 10, -1, (2, 3)),
    ("F", 0, 0, 1, (1,)),
    ("S", 0, 10, 1, (2, 3)),
    ("F", 1, 0, 0, ()),
    ("F", 0, 2, -2, (0,)),
    ("F", 0, 2, 2, (1,)),
    ("F", 0, 1, -2, (0,)),
    ("F", 0, 1, 2, (1,)),
    ("F", -1, 0, 0, ()),
    ("F", 0, 0, -2, (0,)),
    ("S", 0, 10, -2, (2, 3)),
    ("F", 0, 0, 2, (1,)),
    ("S", 0, 10, 2, (2, 3)),
    ("S", -1, 1, 0, (0,)),
    ("S", -1, 1, 0, (1,)),
    ("S", 1, 1, 0, (0,)),
    ("S", 1, 1, 0, (1,)),
    ("S", 2, 1, 0, (0,)),
    ("S", 2, 1, 0, (1,)),
    ("P", 0, 0, 0, ()),
    ("F", 0, 2, -3, ()),
    ("F", -1, 0, -1, ()),
    ("F", 1, 0, -1, ()),
    ("F", 0, 2, 3, (1,)),
    ("F", 0, 1, -3, (0,)),
    ("F", 0, 1, 3, ()),
    ("T", 0, 0, 0, ()),
    ("F", -1, 0, 1, ()),
    ("F", 1, 0, 1, ()),
    ("F", 0, 0, -3, (0,)),
    ("S", 0, 10, -3, (2, 3)),
    ("F", 0, 0, 3, ()),
    ("S", 0, 10, 3, (2, 3)),
    ("F", -1, 1, -1, (0,)),
    ("F", -1, 1, 1, (1,)),
    ("F", 1, 1, -1, (0,)),
    ("F", 1, 1, 1, (1,)),
    ("F", -1, 0, -2, ()),
    ("F", 1, 0, -2, ()),
    ("F", 2, 1, -1, (0,)),
    ("F", 2, 1, 1, (1,)),
    ("F", 0, 1, 4, ()),
    ("F", 0, 2, 4, ()),
    ("F", -1, 0, 2, ()),
    ("F", 1, 0, 2, ()),
    ("F", -1, 1, 2, (1,)),
    ("F", 0, 0, 4, ()),
    ("S", 0, 10, 4, (2, 3)),
    ("S", -1, 0, 0, (2,)),
    ("S", -1, 0, -1, (2,)),
    ("S", 1, 0, 1, (3,)),
    ("S", 1, 0, -2, (3,)),
    ("S", -1, 0, 2, (2,)),
    ("F", 1, 1, 2, (1,)),
    ("P", 0, 1, 0, ()),
    ("F", -1, 1, -2, (0,)),
    ("F", -1, 0, -3, (2,)),
    ("F", 1, 0, -3, ()),
    ("F", 1, 1, -2, (0,)),
    ("F", 2, 1, 2, (1,)),
    ("T", 0, 1, 0, ()),
    ("P", 1, 0, 0, ()),
    ("F", -1, 1, 3, (1,)),
    ("F", 2, 1, -2, (0,)),
    ("F", -1, 0, 3, ()),
    ("F", 1, 1, 3, (1,)),
    ("F", 1, 0, 3, (3,)),
    ("T", 1, 0, 0, ()),
    ("P", 2, 0, 0, ()),
    ("F", -1, 1, -3, ()),
    ("X", 0, 0, 0, ()),
    ("F", 1, 1, -3, ()),
    ("F", 2, 1, 3, (1,)),
    ("F", -1, 0, 4, ()),
    ("F", 1, 0, 4, (3,)),
    ("T", 2, 0, 0, ()),
    ("F", -1, 1, 4, ()),
    ("P", 2, 1, 0, ()),
    ("F", 2, 1, -3, ()),
    ("F", 1, 1, 4, ()),
    ("F", 2, 0, 0, ()),
    ("F", 2, 0, 1, ()),
    ("T", 2, 1, 0, ()),
    ("P", 1, 1, 0, ()),
    ("T", 1, 1, 0, ()),
    ("F", 2, 0, -1, ()),
    ("F", 2, 0, -2, ()),
    ("P", 3, 0, 0, ()),
    ("F", 2, 1, 4, ()),
    ("X", 2, 0, 0, ()),
    ("F", 2, 0, 2, ()),
    ("F", 2, 0, 3, ()),
    ("T", 3, 0, 0, ()),
    ("X", 1, 0, 0, ()),
    ("F", 2, 0, -3, ()),
    ("F", 2, 0, 4, ()),
    ("Z", 0, 0, 0, ()),
    ("P", 3, 1, 0, ()),
    ("T", 3, 1, 0, ()),
    ("X", 3, 0, 0, ()),
    ("Z", 2, 0, 0, ()),
    ("Y", 0, 0, 0, ()),
    ("Z", 1, 0, 0, ()),
    ("Z", 3, 0, 0, ()),
    ("O", 0, 0, 0, ()),
    ("Y", 2, 0, 0, ()),
    ("O", 2, 0, 0, ()),
    ("Y", 1, 0, 0, ()),
    ("Y", 3, 0, 0, ()),
    ("O", 1, 0, 0, ()),
    ("O", 3, 0, 0, ()),
)


def encode(v):
    most = jnp.maximum(jnp.max(jnp.abs(v), axis=0), 1e-30)
    code = jnp.ceil(jnp.log2(most) * 8.0)
    inverse = 32000.0 / jnp.exp2(code * 0.125)
    q = jnp.round(v * inverse[None]).astype(jnp.int32).astype(I16)
    return q, code.astype(jnp.int32).astype(I16)


def decode(q):
    n = q.shape[0] - 1
    scale = jnp.exp2(q[n].astype(F32) * 0.125) * (1.0 / 32000.0)
    return q[0:n].astype(F32) * scale[None]


def kernel(
    route_hbm, index_hbm, value_hbm, site_hbm, env_hbm, out,
    env, site, g, prod, terms, mate_in, x_own, x_out, x_in, final, z_own, z_out, z_in, y_sum, y_out, y_in,
    route, pair_index, pair_value, group, local, pick, place,
    local_sem, sent, g_recv, c_recv, x_recv, z_recv, y_recv,
):
    chan, row = lax.axis_index("chan"), lax.axis_index("row")
    z, y = chan // NY, lax.rem(chan, NY)
    x, core = row // 2, lax.rem(row, 2)

    def zi(d):
        return lax.rem(z + d + NZ, NZ)

    def yi(d):
        return lax.rem(y + d + NY, NY)

    def xi(d):
        return lax.rem(x + d + NX, NX)

    def at_zy(dz, dy):
        return (zi(dz) * NY + yi(dy), row)

    def at_x(d):
        return (chan, xi(d) * 2 + core)

    mate = (chan, x * 2 + 1 - core)

    barrier = pltpu.get_barrier_semaphore()
    partners = [mate] + [at_x(d) for d in (1, 2, 3)] + [at_zy(0, d) for d in (1, 2, 3)]
    partners += [at_zy(d, 0) for d in range(1, NZ)]
    for p in partners:
        pl.semaphore_signal(barrier, inc=1, device_id=p, device_id_type=MESH)
    site_copy = pltpu.make_async_copy(site_hbm, site, local_sem.at[1])
    site_copy.start()
    small_copies = [
        pltpu.make_async_copy(src, dst, local_sem.at[2 + n])
        for n, (src, dst) in enumerate(
            ((route_hbm, route), (index_hbm, pair_index), (value_hbm, pair_value))
        )
    ]
    for c in small_copies:
        c.start()
    env_copy = pltpu.make_async_copy(env_hbm, env, local_sem.at[0])
    env_copy.start()

    out[...] = jnp.zeros_like(out)
    for d in range(4):
        final[d, SLOTS] = jnp.zeros((8, 128), F32)
    new = lax.broadcasted_iota(jnp.int32, (64, 64), 0)
    old = lax.broadcasted_iota(jnp.int32, (64, 64), 1)
    moved = (new & 7) * 8 + ((new >> 3) & 1) * 4 + (new >> 4)
    turn = jnp.where(moved == old, 1.0, 0.0).astype(jnp.bfloat16)
    site_copy.wait()
    rows = site[...].astype(F32).reshape(64, site.shape[2]).astype(jnp.bfloat16)
    g[y * NZ + z] = jnp.dot(turn, rows, preferred_element_type=F32).astype(jnp.bfloat16)
    pl.semaphore_wait(barrier, len(partners))

    def send(src, dst, s_sem, r_sem, dev):
        pltpu.make_async_remote_copy(
            src_ref=src, dst_ref=dst, send_sem=s_sem, recv_sem=r_sem, device_id=dev, device_id_type=MESH
        ).start()

    def arrived(like, r_sem):
        pltpu.make_async_remote_copy(
            src_ref=like, dst_ref=like, send_sem=sent.at[0], recv_sem=r_sem, device_id=mate, device_id_type=MESH
        ).wait_recv()

    def all_sent(like, n):
        pltpu.make_async_remote_copy(
            src_ref=like, dst_ref=like, send_sem=sent.at[n], recv_sem=g_recv.at[0], device_id=mate, device_id_type=MESH
        ).wait_send()

    def g_fwd(dy, h, dz, links):
        for link in links:
            step_z, step_y = LINKS[link]
            there = ((dy - step_y + 1) % NY - 1, 1 if link == 4 else h % 10, (dz - step_z + 3) % NZ - 3)
            lo, hi = cut(there[0], there[1])
            ref = g.at[yi(dy) * NZ + zi(dz), lo:hi]
            send(ref, ref, sent.at[0], g_recv.at[SEMS[there]], at_zy(step_z, step_y))

    seen = {n: 0 for n in SEMS.values()}

    def g_wait(dy, h, dz):
        n = SEMS.get((dy, h, dz))
        if n is None:
            return
        seen[n] += 1
        count = len(SHARED.get(n, (0,)))
        if seen[n] == count:
            lo, hi = cut(dy, h)
            arrived(g.at[0:count, lo:hi], g_recv.at[n])

    def read_groups():
        def body(src, _):
            for i in range(SLOTS):
                dest = route[i % K, (src * NY + y) * PER + i // K]
                here = (dest * 10923) >> 16
                group[src, i] = here
                local[src, i] = dest - here * PER
            return 0

        lax.fori_loop(0, NZ, body, 0)

    def read_picks():
        def body(h, _):
            first, last = jnp.int32(SLOTS), jnp.int32(SLOTS)
            for i in range(SLOTS):
                j = SLOTS - 1 - i
                first = jnp.where(group[z, j] == h, j, first)
                last = jnp.where(group[z, i] == h, i, last)
            pick[h, 0] = first
            pick[h, 1] = jnp.where(last == first, SLOTS, last)
            return 0

        lax.fori_loop(0, NZ * NY, body, 0)

    def read_places():
        def body(n, _):
            src, h = n // NY, z * NY + lax.rem(n, NY)
            first, last = jnp.int32(0), jnp.int32(0)
            for i in range(SLOTS):
                j = SLOTS - 1 - i
                first = jnp.where(group[src, j] == h, local[src, j], first)
                last = jnp.where(group[src, i] == h, local[src, i], last)
            place[n, 0] = first
            place[n, 1] = last
            return 0

        lax.fori_loop(0, NZ * NY, body, 0)

    lane_half = lax.broadcasted_iota(jnp.int32, (1, 1, 128), 2) // P_SIZE

    def product(d, half):
        a = yi(OFFS[d])
        at = [zi(dz) for dz in GROUPS[half]]
        lhs = jnp.concatenate([g[a * NZ + i] for i in at], axis=0)
        for b in range(PER):
            v = jnp.dot(lhs, env[b], preferred_element_type=F32).reshape(4, 4, 16, 256)
            for s in range(4):
                for t in range(2):
                    prod[d, b, t * 4 + s, 4 * half:4 * half + 4] = v[:, s, :, 128 * t:128 * (t + 1)]

    def make_terms(d, half):
        low = lane_half == 0

        def body(i, _):
            tiles = []
            for n in range(3 * K):
                b, k, total = 3 * i + n // K, n % K, None
                for j in range(2):
                    code = pair_index[k, j, b]
                    s, t = code >> 2, code & 3
                    w = jnp.where(lane_half == (t & 1), pair_value[k, j, b], 0.0)
                    add = w * prod[d, b, (t >> 1) * 4 + s, 4 * half:4 * half + 4]
                    total = add if total is None else total + add
                even, odd = total[:, :8], total[:, 8:]
                tiles.append(jnp.where(low, even, odd) + pltpu.roll(jnp.where(low, odd, even), P_SIZE, 2))
            for k in range(3 * K):
                for n, dz in enumerate(GROUPS[half]):
                    terms[d, dz % NZ, 3 * K * i + k] = tiles[k][n]
            return 0

        lax.fori_loop(0, PER // 3, body, 0)

    def mate_send(d, half):
        for n in (0, 1):
            lo, hi = PAIRS[2 * half + n]
            odd = lax.rem(zi(lo), 2) == core
            theirs = jnp.where(odd, zi(hi), zi(lo)) // 2
            src = terms.at[d, jnp.where(odd, hi % NZ, lo % NZ)]
            send(src, mate_in.at[d, theirs], sent.at[1], c_recv.at[d], mate)

    def x_step(d):
        arrived(mate_in.at[d], c_recv.at[d])
        for n, dx in enumerate((2, 1, -1, 0)):
            to = xi(dx)
            v = (terms[d, lax.rem(2 * to + core - z + NZ, NZ)] + mate_in[d, to]).reshape(SLOTS // 2, 16, 128)
            if dx == 0:
                x_own[d] = v
                continue
            q, code = encode(v)
            x_out[d, n, 0:SLOTS // 2] = q
            x_out[d, n, SLOTS // 2] = code
            send(x_out.at[d, n], x_in.at[d, n], sent.at[2], x_recv.at[d], at_x(dx))

    def z_step(d):
        arrived(x_in.at[d], x_recv.at[d])
        v = x_own[d]
        for n in range(3):
            v = v + decode(x_in[d, n])
        final[d, 0:SLOTS] = v.reshape(SLOTS, 8, 128)
        for dz in (4, 3, -3, 2, -2, 1, -1, 0):
            to = zi(dz)
            tiles = []
            for q in range(NY):
                for m in range(2):
                    tiles.append(final[d, pick[to * NY + q, m]])
            v = jnp.stack(tiles).reshape(NY, 16, 128)
            if dz == 0:
                z_own[d] = v
                continue
            n = dz % NZ - 1
            q, code = encode(v)
            z_out[d, n, 0:NY] = q
            z_out[d, n, NY] = code
            send(z_out.at[d, n], z_in.at[d, n], sent.at[3], z_recv.at[d], at_zy(dz, 0))

    def y_step(d):
        arrived(z_in.at[d], z_recv.at[d])
        sums = [[None] * PER for _ in range(NY)]
        for n in range(NZ):
            src = z if n == 0 else zi(-n)
            v = z_own[d] if n == 0 else decode(z_in[d, n - 1])
            for q in range(NY):
                for m in range(2):
                    at = place[src * NY + q, m]
                    tile = v[q, 8 * m:8 * m + 8]
                    spread = jnp.full((8, 128), at, jnp.int32)
                    for c in range(PER):
                        add = jnp.where(spread == c, tile, 0.0)
                        sums[q][c] = add if sums[q][c] is None else sums[q][c] + add
        for q in range(NY):
            y_sum[d, q] = jnp.stack(sums[q])
        for n, dy in enumerate((2, 1, -1)):
            q, code = encode(y_sum[d, yi(dy)].reshape(PER // 2, 16, 128))
            y_out[d, n, 0:PER // 2] = q
            y_out[d, n, PER // 2] = code
            send(y_out.at[d, n], y_in.at[d, n], sent.at[4], y_recv.at[d], at_zy(0, dy))
        out[:, yi(OFFS[d])] += y_sum[d, y]

    def out_step(d):
        arrived(y_in.at[d], y_recv.at[d])
        for n, dy in ((1, -1), (2, 1), (0, 2)):
            out[:, yi(dy + OFFS[d])] += decode(y_in[d, n]).reshape(PER, 8, 128)

    env_here = False
    for kind, d, h, dz, links in ORDER:
        if kind == "F":
            g_wait(d, h, dz)
            g_fwd(d, h, dz, links)
        elif kind == "G":
            for c in small_copies:
                c.wait()
            read_groups()
        elif kind == "I":
            read_picks()
        elif kind == "L":
            read_places()
        elif kind == "S":
            g_fwd(d, h, dz, links)
        elif kind == "P":
            if not env_here:
                env_copy.wait()
                env_here = True
            product(d, h)
        elif kind == "T":
            make_terms(d, h)
            mate_send(d, h)
        else:
            {"X": x_step, "Z": z_step, "Y": y_step, "O": out_step}[kind](d)
            if (kind, d) == ("X", 3):
                all_sent(g.at[0:NY * NZ - 1], 0)
                all_sent(mate_in, 1)
            if (kind, d) == ("Y", 3):
                all_sent(x_in, 2)
                all_sent(z_in, 3)
    all_sent(y_in, 4)


def shards(env_blocks, site_rows, route_dest, pair_index, pair_value):
    depth = env_blocks.shape[1]
    tile = (8, 128)
    tile16 = (16, 128)
    bf16 = jnp.bfloat16
    dma = pltpu.SemaphoreType.DMA
    out = pl.pallas_call(
        kernel,
        out_shape=jax.ShapeDtypeStruct((PER, NY, 8, 128), F32),
        in_specs=[pl.BlockSpec(memory_space=pl.ANY)] * 5,
        out_specs=pl.BlockSpec(memory_space=pltpu.VMEM),
        scratch_shapes=[
            pltpu.VMEM((PER, depth, PD * P_SIZE), bf16),
            pltpu.VMEM(site_rows.shape, bf16),
            pltpu.VMEM((NY * NZ, 64, depth), bf16),
            pltpu.VMEM((4, PER, 8, NZ, 16, 128), F32),
            pltpu.VMEM((4, NZ, SLOTS) + tile, F32),
            pltpu.VMEM((4, NX, SLOTS) + tile, F32),
            pltpu.VMEM((4, SLOTS // 2) + tile16, F32),
            pltpu.VMEM((4, 3, SLOTS // 2 + 1) + tile16, I16),
            pltpu.VMEM((4, 3, SLOTS // 2 + 1) + tile16, I16),
            pltpu.VMEM((4, SLOTS + 1) + tile, F32),
            pltpu.VMEM((4, NY) + tile16, F32),
            pltpu.VMEM((4, NZ - 1, NY + 1) + tile16, I16),
            pltpu.VMEM((4, NZ - 1, NY + 1) + tile16, I16),
            pltpu.VMEM((4, NY, PER) + tile, F32),
            pltpu.VMEM((4, 3, PER // 2 + 1) + tile16, I16),
            pltpu.VMEM((4, 3, PER // 2 + 1) + tile16, I16),
            pltpu.SMEM((K, NZ * NY * PER), jnp.int32),
            pltpu.SMEM((K, 2, PER), jnp.int32),
            pltpu.SMEM((K, 2, PER), F32),
            pltpu.SMEM((NZ, SLOTS), jnp.int32),
            pltpu.SMEM((NZ, SLOTS), jnp.int32),
            pltpu.SMEM((NZ * NY, 2), jnp.int32),
            pltpu.SMEM((NZ * NY, 2), jnp.int32),
            dma((5,)),
            dma((5,)),
            dma((max(SEMS.values()) + 1,)),
            dma((4,)),
            dma((4,)),
            dma((4,)),
            dma((4,)),
        ],
        compiler_params=pltpu.CompilerParams(
            collective_id=0, has_side_effects=True, vmem_limit_bytes=56 * 1024 * 1024
        ),
        cost_estimate=pl.CostEstimate(
            flops=2 * 2048 * depth * PER * 256, bytes_accessed=4 * 1024 * 1024, transcendentals=0
        ),
    )(route_dest.T, pair_index.transpose(1, 2, 0), pair_value.transpose(1, 2, 0), site_rows, env_blocks)
    return out.reshape(PER, -1)


def solution(mesh):
    in_specs = (
        P("chan", "row", None),
        P("chan", None, "row"),
        P(),
        P("chan", None, None),
        P("chan", None, None),
    )
    out_specs = P("chan", "row")
    return jax.shard_map(shards, mesh=mesh, in_specs=in_specs, out_specs=out_specs, check_vma=False)
```

```python
import jax
import jax.numpy as jnp
from jax import lax
from jax.experimental import pallas as pl
from jax.experimental.pallas import tpu as pltpu
from jax.sharding import PartitionSpec as P

PD = 4
P_SIZE = 64
K = 5
NZ, NY, NX = 8, 4, 4
PER = 6
SLOTS = PER * K
OFFS = (0, 1, -1, 2)
OWN = ((0, 32), (32, 48), (48, 64))
NEAR = ((0, 48), (48, 64))
FAR = ((0, 32), (32, 64))
GROUPS = ((0, -1, 1, -2), (2, -3, 3, 4))
PAIRS = ((0, -1), (1, -2), (2, -3), (3, 4))
LINKS = ((1, 0), (-1, 0), (0, 1), (0, -1), (0, 2))
MESH = pl.DeviceIdType.MESH
F32 = jnp.float32
I16 = jnp.int16

def cut(dy, part):
    return (OWN if dy == 0 else FAR if dy == 2 else NEAR)[part]


PARTS = tuple(
    (dy, part, dz)
    for dy in OFFS
    for part in range(len(OWN) if dy == 0 else 2)
    for dz in range(-3, 5)
    if (dy, dz) != (0, 0)
)
SHARED = {
    0: ((2, 0, 0), (2, 0, -1), (2, 0, 1), (2, 0, -2)),
    1: ((2, 0, 2), (2, 0, -3), (2, 0, 3), (2, 0, 4)),
    2: ((-1, 0, 1), (-1, 0, -2)),
    3: ((-1, 0, 3), (-1, 0, 4)),
    4: ((1, 0, 0), (1, 0, -1)),
    5: ((1, 0, 2), (1, 0, -3)),
}
SEMS = {part: n for n, parts in SHARED.items() for part in parts}
SEMS.update({part: len(SHARED) + n for n, part in enumerate(p for p in PARTS if p not in SEMS)})

ORDER = (
    ("F", 0, 2, 0, (0, 1)),
    ("F", 0, 1, 0, (0, 1)),
    ("F", 0, 0, 0, (0, 1)),
    ("S", 0, 11, 0, (2, 3, 4)),
    ("S", 0, 10, 0, (2, 3)),
    ("G", 0, 0, 0, ()),
    ("I", 0, 0, 0, ()),
    ("L", 0, 0, 0, ()),
    ("F", 0, 2, -1, (0,)),
    ("F", 0, 2, 1, (1,)),
    ("F", -1, 1, 0, ()),
    ("F", 1, 1, 0, ()),
    ("F", 0, 1, -1, (0,)),
    ("F", 0, 1, 1, (1,)),
    ("F", 2, 1, 0, ()),
    ("F", 0, 0, -1, (0,)),
    ("S", 0, 10, -1, (2, 3)),
    ("F", 0, 0, 1, (1,)),
    ("S", 0, 10, 1, (2, 3)),
    ("F", 1, 0, 0, ()),
    ("F", 0, 2, -2, (0,)),
    ("F", 0, 2, 2, (1,)),
    ("F", 0, 1, -2, (0,)),
    ("F", 0, 1, 2, (1,)),
    ("F", -1, 0, 0, ()),
    ("F", 0, 0, -2, (0,)),
    ("S", 0, 10, -2, (2, 3)),
    ("F", 0, 0, 2, (1,)),
    ("S", 0, 10, 2, (2, 3)),
    ("S", -1, 1, 0, (0,)),
    ("S", -1, 1, 0, (1,)),
    ("S", 1, 1, 0, (0,)),
    ("S", 1, 1, 0, (1,)),
    ("S", 2, 1, 0, (0,)),
    ("S", 2, 1, 0, (1,)),
    ("P", 0, 0, 0, ()),
    ("F", 0, 2, -3, ()),
    ("F", -1, 0, -1, ()),
    ("F", 1, 0, -1, ()),
    ("F", 0, 2, 3, (1,)),
    ("F", 0, 1, -3, (0,)),
    ("F", 0, 1, 3, ()),
    ("T", 0, 0, 0, ()),
    ("F", -1, 0, 1, ()),
    ("F", 1, 0, 1, ()),
    ("F", 0, 0, -3, (0,)),
    ("S", 0, 10, -3, (2, 3)),
    ("F", 0, 0, 3, ()),
    ("S", 0, 10, 3, (2, 3)),
    ("F", -1, 1, -1, (0,)),
    ("F", -1, 1, 1, (1,)),
    ("F", 1, 1, -1, (0,)),
    ("F", 1, 1, 1, (1,)),
    ("F", -1, 0, -2, ()),
    ("F", 1, 0, -2, ()),
    ("F", 2, 1, -1, (0,)),
    ("F", 2, 1, 1, (1,)),
    ("F", 0, 1, 4, ()),
    ("F", 0, 2, 4, ()),
    ("F", -1, 0, 2, ()),
    ("F", 1, 0, 2, ()),
    ("F", -1, 1, 2, (1,)),
    ("F", 0, 0, 4, ()),
    ("S", 0, 10, 4, (2, 3)),
    ("S", -1, 0, 0, (2,)),
    ("S", -1, 0, -1, (2,)),
    ("S", 1, 0, 1, (3,)),
    ("S", 1, 0, -2, (3,)),
    ("S", -1, 0, 2, (2,)),
    ("F", 1, 1, 2, (1,)),
    ("P", 0, 1, 0, ()),
    ("F", -1, 1, -2, (0,)),
    ("F", -1, 0, -3, (2,)),
    ("F", 1, 0, -3, ()),
    ("F", 1, 1, -2, (0,)),
    ("F", 2, 1, 2, (1,)),
    ("T", 0, 1, 0, ()),
    ("P", 1, 0, 0, ()),
    ("F", -1, 1, 3, (1,)),
    ("F", 2, 1, -2, (0,)),
    ("F", -1, 0, 3, ()),
    ("F", 1, 1, 3, (1,)),
    ("F", 1, 0, 3, (3,)),
    ("T", 1, 0, 0, ()),
    ("P", 2, 0, 0, ()),
    ("F", -1, 1, -3, ()),
    ("X", 0, 0, 0, ()),
    ("F", 1, 1, -3, ()),
    ("F", 2, 1, 3, (1,)),
    ("F", -1, 0, 4, ()),
    ("F", 1, 0, 4, (3,)),
    ("T", 2, 0, 0, ()),
    ("F", -1, 1, 4, ()),
    ("P", 2, 1, 0, ()),
    ("F", 2, 1, -3, ()),
    ("F", 1, 1, 4, ()),
    ("F", 2, 0, 0, ()),
    ("F", 2, 0, 1, ()),
    ("T", 2, 1, 0, ()),
    ("P", 1, 1, 0, ()),
    ("T", 1, 1, 0, ()),
    ("F", 2, 0, -1, ()),
    ("F", 2, 0, -2, ()),
    ("P", 3, 0, 0, ()),
    ("F", 2, 1, 4, ()),
    ("X", 2, 0, 0, ()),
    ("F", 2, 0, 2, ()),
    ("F", 2, 0, 3, ()),
    ("T", 3, 0, 0, ()),
    ("X", 1, 0, 0, ()),
    ("F", 2, 0, -3, ()),
    ("F", 2, 0, 4, ()),
    ("Z", 0, 0, 0, ()),
    ("P", 3, 1, 0, ()),
    ("T", 3, 1, 0, ()),
    ("X", 3, 0, 0, ()),
    ("Z", 2, 0, 0, ()),
    ("Y", 0, 0, 0, ()),
    ("Z", 1, 0, 0, ()),
    ("O", 0, 0, 0, ()),
    ("Z", 3, 0, 0, ()),
    ("Y", 2, 0, 0, ()),
    ("Y", 1, 0, 0, ()),
    ("O", 2, 0, 0, ()),
    ("Y", 3, 0, 0, ()),
    ("O", 1, 0, 0, ()),
    ("O", 3, 0, 0, ()),
)


def encode(v):
    most = jnp.maximum(jnp.max(jnp.abs(v), axis=0), 1e-30)
    code = jnp.ceil(jnp.log2(most) * 8.0)
    inverse = 32000.0 / jnp.exp2(code * 0.125)
    q = jnp.round(v * inverse[None]).astype(jnp.int32).astype(I16)
    return q, code.astype(jnp.int32).astype(I16)


def decode(q):
    n = q.shape[0] - 1
    scale = jnp.exp2(q[n].astype(F32) * 0.125) * (1.0 / 32000.0)
    return q[0:n].astype(F32) * scale[None]


def encode_rows(v):
    most = jnp.max(jnp.max(jnp.abs(v), axis=0), axis=0, keepdims=True)
    most = jnp.maximum(most, 1e-30)
    return jnp.round(v * (32000.0 / most)[None]).astype(jnp.int32).astype(I16), most


def decode_rows(q, most):
    return q.astype(F32) * (most * (1.0 / 32000.0))[None]


def kernel(
    route_hbm, index_hbm, value_hbm, site_hbm, env_hbm, out,
    env, site, g, prod, terms, mate_in, x_own, x_out, x_in, final, z_own, z_out, z_in, zc_out, zc_in, y_sum, y_out, y_in, yc_out, yc_in,
    route, pair_index, pair_value, group, local, pick, place,
    local_sem, sent, g_recv, c_recv, x_recv, z_recv, y_recv, zc_recv, yc_recv,
):
    chan, row = lax.axis_index("chan"), lax.axis_index("row")
    z, y = chan // NY, lax.rem(chan, NY)
    x, core = row // 2, lax.rem(row, 2)

    def zi(d):
        return lax.rem(z + d + NZ, NZ)

    def yi(d):
        return lax.rem(y + d + NY, NY)

    def xi(d):
        return lax.rem(x + d + NX, NX)

    def at_zy(dz, dy):
        return (zi(dz) * NY + yi(dy), row)

    def at_x(d):
        return (chan, xi(d) * 2 + core)

    mate = (chan, x * 2 + 1 - core)

    barrier = pltpu.get_barrier_semaphore()
    partners = [mate] + [at_x(d) for d in (1, 2, 3)] + [at_zy(0, d) for d in (1, 2, 3)]
    partners += [at_zy(d, 0) for d in range(1, NZ)]
    for p in partners:
        pl.semaphore_signal(barrier, inc=1, device_id=p, device_id_type=MESH)
    site_copy = pltpu.make_async_copy(site_hbm, site, local_sem.at[1])
    site_copy.start()
    small_copies = [
        pltpu.make_async_copy(src, dst, local_sem.at[2 + n])
        for n, (src, dst) in enumerate(
            ((route_hbm, route), (index_hbm, pair_index), (value_hbm, pair_value))
        )
    ]
    for c in small_copies:
        c.start()
    env_copy = pltpu.make_async_copy(env_hbm, env, local_sem.at[0])
    env_copy.start()

    out[...] = jnp.zeros_like(out)
    for d in range(4):
        final[d, SLOTS] = jnp.zeros((8, 128), F32)
    new = lax.broadcasted_iota(jnp.int32, (64, 64), 0)
    old = lax.broadcasted_iota(jnp.int32, (64, 64), 1)
    moved = (new & 7) * 8 + ((new >> 3) & 1) * 4 + (new >> 4)
    turn = jnp.where(moved == old, 1.0, 0.0).astype(jnp.bfloat16)
    site_copy.wait()
    rows = site[...].astype(F32).reshape(64, site.shape[2]).astype(jnp.bfloat16)
    g[y * NZ + z] = jnp.dot(turn, rows, preferred_element_type=F32).astype(jnp.bfloat16)
    pl.semaphore_wait(barrier, len(partners))

    def send(src, dst, s_sem, r_sem, dev):
        pltpu.make_async_remote_copy(
            src_ref=src, dst_ref=dst, send_sem=s_sem, recv_sem=r_sem, device_id=dev, device_id_type=MESH
        ).start()

    def arrived(like, r_sem):
        pltpu.make_async_remote_copy(
            src_ref=like, dst_ref=like, send_sem=sent.at[0], recv_sem=r_sem, device_id=mate, device_id_type=MESH
        ).wait_recv()

    def all_sent(like, n):
        pltpu.make_async_remote_copy(
            src_ref=like, dst_ref=like, send_sem=sent.at[n], recv_sem=g_recv.at[0], device_id=mate, device_id_type=MESH
        ).wait_send()

    def g_fwd(dy, h, dz, links):
        for link in links:
            step_z, step_y = LINKS[link]
            there = ((dy - step_y + 1) % NY - 1, 1 if link == 4 else h % 10, (dz - step_z + 3) % NZ - 3)
            lo, hi = cut(there[0], there[1])
            ref = g.at[yi(dy) * NZ + zi(dz), lo:hi]
            send(ref, ref, sent.at[0], g_recv.at[SEMS[there]], at_zy(step_z, step_y))

    seen = {n: 0 for n in SEMS.values()}

    def g_wait(dy, h, dz):
        n = SEMS.get((dy, h, dz))
        if n is None:
            return
        seen[n] += 1
        count = len(SHARED.get(n, (0,)))
        if seen[n] == count:
            lo, hi = cut(dy, h)
            arrived(g.at[0:count, lo:hi], g_recv.at[n])

    def read_groups():
        def body(src, _):
            for i in range(SLOTS):
                dest = route[i % K, (src * NY + y) * PER + i // K]
                here = (dest * 10923) >> 16
                group[src, i] = here
                local[src, i] = dest - here * PER
            return 0

        lax.fori_loop(0, NZ, body, 0)

    def read_picks():
        def body(h, _):
            first, last = jnp.int32(SLOTS), jnp.int32(SLOTS)
            for i in range(SLOTS):
                j = SLOTS - 1 - i
                first = jnp.where(group[z, j] == h, j, first)
                last = jnp.where(group[z, i] == h, i, last)
            pick[h, 0] = first
            pick[h, 1] = jnp.where(last == first, SLOTS, last)
            return 0

        lax.fori_loop(0, NZ * NY, body, 0)

    def read_places():
        def body(n, _):
            src, h = n // NY, z * NY + lax.rem(n, NY)
            first, last = jnp.int32(0), jnp.int32(0)
            for i in range(SLOTS):
                j = SLOTS - 1 - i
                first = jnp.where(group[src, j] == h, local[src, j], first)
                last = jnp.where(group[src, i] == h, local[src, i], last)
            place[n, 0] = first
            place[n, 1] = last
            return 0

        lax.fori_loop(0, NZ * NY, body, 0)

    lane_half = lax.broadcasted_iota(jnp.int32, (1, 1, 128), 2) // P_SIZE

    def product(d, half):
        a = yi(OFFS[d])
        at = [zi(dz) for dz in GROUPS[half]]
        lhs = jnp.concatenate([g[a * NZ + i] for i in at], axis=0)
        for b in range(PER):
            v = jnp.dot(lhs, env[b], preferred_element_type=F32).reshape(4, 4, 16, 256)
            for s in range(4):
                for t in range(2):
                    prod[d, b, t * 4 + s, 4 * half:4 * half + 4] = v[:, s, :, 128 * t:128 * (t + 1)]

    def make_terms(d, half):
        low = lane_half == 0

        def body(i, _):
            tiles = []
            for n in range(3 * K):
                b, k, total = 3 * i + n // K, n % K, None
                for j in range(2):
                    code = pair_index[k, j, b]
                    s, t = code >> 2, code & 3
                    w = jnp.where(lane_half == (t & 1), pair_value[k, j, b], 0.0)
                    add = w * prod[d, b, (t >> 1) * 4 + s, 4 * half:4 * half + 4]
                    total = add if total is None else total + add
                even, odd = total[:, :8], total[:, 8:]
                tiles.append(jnp.where(low, even, odd) + pltpu.roll(jnp.where(low, odd, even), P_SIZE, 2))
            for k in range(3 * K):
                for n, dz in enumerate(GROUPS[half]):
                    terms[d, dz % NZ, 3 * K * i + k] = tiles[k][n]
            return 0

        lax.fori_loop(0, PER // 3, body, 0)

    def mate_send(d, half):
        for n in (0, 1):
            lo, hi = PAIRS[2 * half + n]
            odd = lax.rem(zi(lo), 2) == core
            theirs = jnp.where(odd, zi(hi), zi(lo)) // 2
            src = terms.at[d, jnp.where(odd, hi % NZ, lo % NZ)]
            send(src, mate_in.at[d, theirs], sent.at[1], c_recv.at[d], mate)

    def x_step(d):
        arrived(mate_in.at[d], c_recv.at[d])
        for n, dx in enumerate((2, 1, -1, 0)):
            to = xi(dx)
            v = (terms[d, lax.rem(2 * to + core - z + NZ, NZ)] + mate_in[d, to]).reshape(SLOTS // 2, 16, 128)
            if dx == 0:
                x_own[d] = v
                continue
            q, code = encode(v)
            x_out[d, n, 0:SLOTS // 2] = q
            x_out[d, n, SLOTS // 2] = code
            send(x_out.at[d, n], x_in.at[d, n], sent.at[2], x_recv.at[d], at_x(dx))

    def z_step(d):
        arrived(x_in.at[d], x_recv.at[d])
        v = x_own[d]
        for n in range(3):
            v = v + decode(x_in[d, n])
        final[d, 0:SLOTS] = v.reshape(SLOTS, 8, 128)
        for dz in (4, 3, -3, 2, -2, 1, -1, 0):
            to = zi(dz)
            tiles = []
            for q in range(NY):
                for m in range(2):
                    tiles.append(final[d, pick[to * NY + q, m]])
            v = jnp.stack(tiles).reshape(NY, 16, 128)
            if dz == 0:
                z_own[d] = v
                continue
            n = dz % NZ - 1
            z_out[d, n], zc_out[d, n] = encode_rows(v)
            send(z_out.at[d, n], z_in.at[d, n], sent.at[3], z_recv.at[d], at_zy(dz, 0))
            send(zc_out.at[d, n], zc_in.at[d, n], sent.at[5], zc_recv.at[d], at_zy(dz, 0))

    def y_step(d):
        arrived(z_in.at[d], z_recv.at[d])
        arrived(zc_in.at[d], zc_recv.at[d])
        sums = [[None] * PER for _ in range(NY)]
        for n in range(NZ):
            src = z if n == 0 else zi(-n)
            v = z_own[d] if n == 0 else decode_rows(z_in[d, n - 1], zc_in[d, n - 1])
            for q in range(NY):
                for m in range(2):
                    at = place[src * NY + q, m]
                    tile = v[q, 8 * m:8 * m + 8]
                    spread = jnp.full((8, 128), at, jnp.int32)
                    for c in range(PER):
                        add = jnp.where(spread == c, tile, 0.0)
                        sums[q][c] = add if sums[q][c] is None else sums[q][c] + add
        for q in range(NY):
            y_sum[d, q] = jnp.stack(sums[q])
        for n, dy in enumerate((2, 1, -1)):
            y_out[d, n], yc_out[d, n] = encode_rows(y_sum[d, yi(dy)].reshape(PER // 2, 16, 128))
            send(y_out.at[d, n], y_in.at[d, n], sent.at[4], y_recv.at[d], at_zy(0, dy))
            send(yc_out.at[d, n], yc_in.at[d, n], sent.at[6], yc_recv.at[d], at_zy(0, dy))
        out[:, yi(OFFS[d])] += y_sum[d, y]

    def out_step(d):
        arrived(y_in.at[d], y_recv.at[d])
        arrived(yc_in.at[d], yc_recv.at[d])
        for n, dy in ((1, -1), (2, 1), (0, 2)):
            out[:, yi(dy + OFFS[d])] += decode_rows(y_in[d, n], yc_in[d, n]).reshape(PER, 8, 128)

    env_here = False
    for kind, d, h, dz, links in ORDER:
        if kind == "F":
            g_wait(d, h, dz)
            g_fwd(d, h, dz, links)
        elif kind == "G":
            for c in small_copies:
                c.wait()
            read_groups()
        elif kind == "I":
            read_picks()
        elif kind == "L":
            read_places()
        elif kind == "S":
            g_fwd(d, h, dz, links)
        elif kind == "P":
            if not env_here:
                env_copy.wait()
                env_here = True
            product(d, h)
        elif kind == "T":
            make_terms(d, h)
            mate_send(d, h)
        else:
            {"X": x_step, "Z": z_step, "Y": y_step, "O": out_step}[kind](d)
            if (kind, d) == ("X", 3):
                all_sent(g.at[0:NY * NZ - 1], 0)
                all_sent(mate_in, 1)
            if (kind, d) == ("Y", 3):
                all_sent(x_in, 2)
                all_sent(z_in, 3)
                all_sent(zc_in, 5)
    all_sent(y_in, 4)
    all_sent(yc_in, 6)


def shards(env_blocks, site_rows, route_dest, pair_index, pair_value):
    depth = env_blocks.shape[1]
    tile = (8, 128)
    tile16 = (16, 128)
    bf16 = jnp.bfloat16
    dma = pltpu.SemaphoreType.DMA
    out = pl.pallas_call(
        kernel,
        out_shape=jax.ShapeDtypeStruct((PER, NY, 8, 128), F32),
        in_specs=[pl.BlockSpec(memory_space=pl.ANY)] * 5,
        out_specs=pl.BlockSpec(memory_space=pltpu.VMEM),
        scratch_shapes=[
            pltpu.VMEM((PER, depth, PD * P_SIZE), bf16),
            pltpu.VMEM(site_rows.shape, bf16),
            pltpu.VMEM((NY * NZ, 64, depth), bf16),
            pltpu.VMEM((4, PER, 8, NZ, 16, 128), F32),
            pltpu.VMEM((4, NZ, SLOTS) + tile, F32),
            pltpu.VMEM((4, NX, SLOTS) + tile, F32),
            pltpu.VMEM((4, SLOTS // 2) + tile16, F32),
            pltpu.VMEM((4, 3, SLOTS // 2 + 1) + tile16, I16),
            pltpu.VMEM((4, 3, SLOTS // 2 + 1) + tile16, I16),
            pltpu.VMEM((4, SLOTS + 1) + tile, F32),
            pltpu.VMEM((4, NY) + tile16, F32),
            pltpu.VMEM((4, NZ - 1, NY) + tile16, I16),
            pltpu.VMEM((4, NZ - 1, NY) + tile16, I16),
            pltpu.VMEM((4, NZ - 1, 1, 128), F32),
            pltpu.VMEM((4, NZ - 1, 1, 128), F32),
            pltpu.VMEM((4, NY, PER) + tile, F32),
            pltpu.VMEM((4, 3, PER // 2) + tile16, I16),
            pltpu.VMEM((4, 3, PER // 2) + tile16, I16),
            pltpu.VMEM((4, 3, 1, 128), F32),
            pltpu.VMEM((4, 3, 1, 128), F32),
            pltpu.SMEM((K, NZ * NY * PER), jnp.int32),
            pltpu.SMEM((K, 2, PER), jnp.int32),
            pltpu.SMEM((K, 2, PER), F32),
            pltpu.SMEM((NZ, SLOTS), jnp.int32),
            pltpu.SMEM((NZ, SLOTS), jnp.int32),
            pltpu.SMEM((NZ * NY, 2), jnp.int32),
            pltpu.SMEM((NZ * NY, 2), jnp.int32),
            dma((5,)),
            dma((7,)),
            dma((max(SEMS.values()) + 1,)),
            dma((4,)),
            dma((4,)),
            dma((4,)),
            dma((4,)),
            dma((4,)),
            dma((4,)),
        ],
        compiler_params=pltpu.CompilerParams(
            collective_id=0, has_side_effects=True, vmem_limit_bytes=56 * 1024 * 1024
        ),
        cost_estimate=pl.CostEstimate(
            flops=2 * 2048 * depth * PER * 256, bytes_accessed=4 * 1024 * 1024, transcendentals=0
        ),
    )(route_dest.T, pair_index.transpose(1, 2, 0), pair_value.transpose(1, 2, 0), site_rows, env_blocks)
    return out.reshape(PER, -1)


def solution(mesh):
    in_specs = (
        P("chan", "row", None),
        P("chan", None, "row"),
        P(),
        P("chan", None, None),
        P("chan", None, None),
    )
    out_specs = P("chan", "row")
    return jax.shard_map(shards, mesh=mesh, in_specs=in_specs, out_specs=out_specs, check_vma=False)
```

```python
import jax
import jax.numpy as jnp
from jax import lax
from jax.experimental import pallas as pl
from jax.experimental.pallas import tpu as pltpu
from jax.sharding import PartitionSpec as P

PD = 4
P_SIZE = 64
K = 5
NZ, NY, NX = 8, 4, 4
PER = 6
SLOTS = PER * K
OFFS = (0, 1, -1, 2)
OWN = ((0, 32), (32, 48), (48, 64))
NEAR = ((0, 48), (48, 64))
FAR = ((0, 32), (32, 64))
GROUPS = ((0, -1, 1, -2), (2, -3, 3, 4))
PAIRS = ((0, -1), (1, -2), (2, -3), (3, 4))
LINKS = ((1, 0), (-1, 0), (0, 1), (0, -1), (0, 2))
MESH = pl.DeviceIdType.MESH
F32 = jnp.float32
I16 = jnp.int16

def cut(dy, part):
    return (OWN if dy == 0 else FAR if dy == 2 else NEAR)[part]


PARTS = tuple(
    (dy, part, dz)
    for dy in OFFS
    for part in range(len(OWN) if dy == 0 else 2)
    for dz in range(-3, 5)
    if (dy, dz) != (0, 0)
)
SHARED = {
    0: ((2, 0, 0), (2, 0, -1), (2, 0, 1), (2, 0, -2)),
    1: ((2, 0, 2), (2, 0, -3), (2, 0, 3), (2, 0, 4)),
    2: ((-1, 0, 1), (-1, 0, -2)),
    3: ((-1, 0, 3), (-1, 0, 4)),
    4: ((1, 0, 0), (1, 0, -1)),
    5: ((1, 0, 2), (1, 0, -3)),
}
SEMS = {part: n for n, parts in SHARED.items() for part in parts}
SEMS.update({part: len(SHARED) + n for n, part in enumerate(p for p in PARTS if p not in SEMS)})

ORDER = (
    ("F", 0, 2, 0, (0, 1)),
    ("F", 0, 1, 0, (0, 1)),
    ("F", 0, 0, 0, (0, 1)),
    ("S", 0, 11, 0, (2, 3, 4)),
    ("S", 0, 10, 0, (2, 3)),
    ("G", 0, 0, 0, ()),
    ("I", 0, 0, 0, ()),
    ("L", 0, 0, 0, ()),
    ("F", 0, 2, -1, (0,)),
    ("F", 0, 2, 1, (1,)),
    ("F", -1, 1, 0, ()),
    ("F", 1, 1, 0, ()),
    ("F", 0, 1, -1, (0,)),
    ("F", 0, 1, 1, (1,)),
    ("F", 2, 1, 0, ()),
    ("F", 0, 0, -1, (0,)),
    ("S", 0, 10, -1, (2, 3)),
    ("F", 0, 0, 1, (1,)),
    ("S", 0, 10, 1, (2, 3)),
    ("F", 1, 0, 0, ()),
    ("F", 0, 2, -2, (0,)),
    ("F", 0, 2, 2, (1,)),
    ("F", 0, 1, -2, (0,)),
    ("F", 0, 1, 2, (1,)),
    ("F", -1, 0, 0, ()),
    ("F", 0, 0, -2, (0,)),
    ("S", 0, 10, -2, (2, 3)),
    ("F", 0, 0, 2, (1,)),
    ("S", 0, 10, 2, (2, 3)),
    ("S", -1, 1, 0, (0,)),
    ("S", -1, 1, 0, (1,)),
    ("S", 1, 1, 0, (0,)),
    ("S", 1, 1, 0, (1,)),
    ("S", 2, 1, 0, (0,)),
    ("S", 2, 1, 0, (1,)),
    ("P", 0, 0, 0, ()),
    ("F", 0, 2, -3, ()),
    ("F", -1, 0, -1, ()),
    ("F", 1, 0, -1, ()),
    ("F", 0, 2, 3, (1,)),
    ("F", 0, 1, -3, (0,)),
    ("F", 0, 1, 3, ()),
    ("T", 0, 0, 0, ()),
    ("F", -1, 0, 1, ()),
    ("F", 1, 0, 1, ()),
    ("F", 0, 0, -3, (0,)),
    ("S", 0, 10, -3, (2, 3)),
    ("F", 0, 0, 3, ()),
    ("S", 0, 10, 3, (2, 3)),
    ("F", -1, 1, -1, (0,)),
    ("F", -1, 1, 1, (1,)),
    ("F", 1, 1, -1, (0,)),
    ("F", 1, 1, 1, (1,)),
    ("F", -1, 0, -2, ()),
    ("F", 1, 0, -2, ()),
    ("F", 2, 1, -1, (0,)),
    ("F", 2, 1, 1, (1,)),
    ("F", 0, 1, 4, ()),
    ("F", 0, 2, 4, ()),
    ("F", -1, 0, 2, ()),
    ("F", 1, 0, 2, ()),
    ("F", -1, 1, 2, (1,)),
    ("F", 0, 0, 4, ()),
    ("S", 0, 10, 4, (2, 3)),
    ("S", -1, 0, 0, (2,)),
    ("S", -1, 0, -1, (2,)),
    ("S", 1, 0, 1, (3,)),
    ("S", 1, 0, -2, (3,)),
    ("S", -1, 0, 2, (2,)),
    ("F", 1, 1, 2, (1,)),
    ("P", 0, 1, 0, ()),
    ("F", -1, 1, -2, (0,)),
    ("F", -1, 0, -3, (2,)),
    ("F", 1, 0, -3, ()),
    ("F", 1, 1, -2, (0,)),
    ("F", 2, 1, 2, (1,)),
    ("T", 0, 1, 0, ()),
    ("P", 1, 0, 0, ()),
    ("F", -1, 1, 3, (1,)),
    ("F", 2, 1, -2, (0,)),
    ("F", -1, 0, 3, ()),
    ("F", 1, 1, 3, (1,)),
    ("F", 1, 0, 3, (3,)),
    ("T", 1, 0, 0, ()),
    ("P", 2, 0, 0, ()),
    ("F", -1, 1, -3, ()),
    ("X", 0, 0, 0, ()),
    ("F", 1, 1, -3, ()),
    ("F", 2, 1, 3, (1,)),
    ("F", -1, 0, 4, ()),
    ("F", 1, 0, 4, (3,)),
    ("T", 2, 0, 0, ()),
    ("F", -1, 1, 4, ()),
    ("P", 2, 1, 0, ()),
    ("F", 2, 1, -3, ()),
    ("F", 1, 1, 4, ()),
    ("F", 2, 0, 0, ()),
    ("F", 2, 0, 1, ()),
    ("T", 2, 1, 0, ()),
    ("P", 1, 1, 0, ()),
    ("T", 1, 1, 0, ()),
    ("F", 2, 0, -1, ()),
    ("F", 2, 0, -2, ()),
    ("P", 3, 0, 0, ()),
    ("F", 2, 1, 4, ()),
    ("X", 2, 0, 0, ()),
    ("F", 2, 0, 2, ()),
    ("F", 2, 0, 3, ()),
    ("T", 3, 0, 0, ()),
    ("X", 1, 0, 0, ()),
    ("F", 2, 0, -3, ()),
    ("F", 2, 0, 4, ()),
    ("Z", 0, 0, 0, ()),
    ("P", 3, 1, 0, ()),
    ("T", 3, 1, 0, ()),
    ("X", 3, 0, 0, ()),
    ("Z", 2, 0, 0, ()),
    ("Y", 0, 0, 0, ()),
    ("Z", 1, 0, 0, ()),
    ("O", 0, 0, 0, ()),
    ("Z", 3, 0, 0, ()),
    ("Y", 2, 0, 0, ()),
    ("Y", 1, 0, 0, ()),
    ("O", 2, 0, 0, ()),
    ("Y", 3, 0, 0, ()),
    ("O", 1, 0, 0, ()),
    ("O", 3, 0, 0, ()),
)


def encode(v):
    most = jnp.maximum(jnp.max(jnp.abs(v), axis=0), 1e-30)
    code = jnp.ceil(jnp.log2(most) * 8.0)
    inverse = 32000.0 / jnp.exp2(code * 0.125)
    q = jnp.round(v * inverse[None]).astype(jnp.int32).astype(I16)
    return q, code.astype(jnp.int32).astype(I16)


def decode(q):
    n = q.shape[0] - 1
    scale = jnp.exp2(q[n].astype(F32) * 0.125) * (1.0 / 32000.0)
    return q[0:n].astype(F32) * scale[None]


def encode_rows(v):
    most = jnp.max(jnp.max(jnp.abs(v), axis=0), axis=0, keepdims=True)
    most = jnp.maximum(most, 1e-30)
    return jnp.round(v * (32000.0 / most)[None]).astype(jnp.int32).astype(I16), most


def decode_rows(q, most):
    return q.astype(F32) * (most * (1.0 / 32000.0))[None]


def kernel(
    route_hbm, index_hbm, value_hbm, site_hbm, env_hbm, out,
    env, site, g, prod, terms, mate_in, x_own, x_out, x_in, final, z_own, z_out, z_in, zc_out, zc_in, y_sum, y_out, y_in, yc_out, yc_in,
    route, pair_index, pair_value, group, local, pick, place,
    local_sem, sent, g_recv, c_recv, x_recv, z_recv, y_recv, zc_recv, yc_recv,
):
    chan, row = lax.axis_index("chan"), lax.axis_index("row")
    z, y = chan // NY, lax.rem(chan, NY)
    x, core = row // 2, lax.rem(row, 2)

    def zi(d):
        return lax.rem(z + d + NZ, NZ)

    def yi(d):
        return lax.rem(y + d + NY, NY)

    def xi(d):
        return lax.rem(x + d + NX, NX)

    def at_zy(dz, dy):
        return (zi(dz) * NY + yi(dy), row)

    def at_x(d):
        return (chan, xi(d) * 2 + core)

    mate = (chan, x * 2 + 1 - core)

    barrier = pltpu.get_barrier_semaphore()
    partners = [mate] + [at_x(d) for d in (1, 2, 3)] + [at_zy(0, d) for d in (1, 2, 3)]
    partners += [at_zy(d, 0) for d in range(1, NZ)]
    for p in partners:
        pl.semaphore_signal(barrier, inc=1, device_id=p, device_id_type=MESH)
    site_copy = pltpu.make_async_copy(site_hbm, site, local_sem.at[1])
    site_copy.start()
    small_copies = [
        pltpu.make_async_copy(src, dst, local_sem.at[2 + n])
        for n, (src, dst) in enumerate(
            ((route_hbm, route), (index_hbm, pair_index), (value_hbm, pair_value))
        )
    ]
    for c in small_copies:
        c.start()
    env_copy = pltpu.make_async_copy(env_hbm, env, local_sem.at[0])
    env_copy.start()

    out[...] = jnp.zeros_like(out)
    for d in range(4):
        final[d, SLOTS] = jnp.zeros((8, 128), F32)
    new = lax.broadcasted_iota(jnp.int32, (64, 64), 0)
    old = lax.broadcasted_iota(jnp.int32, (64, 64), 1)
    moved = (new & 7) * 8 + ((new >> 3) & 1) * 4 + (new >> 4)
    turn = jnp.where(moved == old, 1.0, 0.0).astype(jnp.bfloat16)
    site_copy.wait()
    rows = site[...].astype(F32).reshape(64, site.shape[2]).astype(jnp.bfloat16)
    g[y * NZ + z] = jnp.dot(turn, rows, preferred_element_type=F32).astype(jnp.bfloat16)
    pl.semaphore_wait(barrier, len(partners))

    def send(src, dst, s_sem, r_sem, dev):
        pltpu.make_async_remote_copy(
            src_ref=src, dst_ref=dst, send_sem=s_sem, recv_sem=r_sem, device_id=dev, device_id_type=MESH
        ).start()

    def arrived(like, r_sem):
        pltpu.make_async_remote_copy(
            src_ref=like, dst_ref=like, send_sem=sent.at[0], recv_sem=r_sem, device_id=mate, device_id_type=MESH
        ).wait_recv()

    def all_sent(like, n):
        pltpu.make_async_remote_copy(
            src_ref=like, dst_ref=like, send_sem=sent.at[n], recv_sem=g_recv.at[0], device_id=mate, device_id_type=MESH
        ).wait_send()

    def g_fwd(dy, h, dz, links):
        for link in links:
            step_z, step_y = LINKS[link]
            there = ((dy - step_y + 1) % NY - 1, 1 if link == 4 else h % 10, (dz - step_z + 3) % NZ - 3)
            lo, hi = cut(there[0], there[1])
            ref = g.at[yi(dy) * NZ + zi(dz), lo:hi]
            send(ref, ref, sent.at[0], g_recv.at[SEMS[there]], at_zy(step_z, step_y))

    seen = {n: 0 for n in SEMS.values()}

    def g_wait(dy, h, dz):
        n = SEMS.get((dy, h, dz))
        if n is None:
            return
        seen[n] += 1
        count = len(SHARED.get(n, (0,)))
        if seen[n] == count:
            lo, hi = cut(dy, h)
            arrived(g.at[0:count, lo:hi], g_recv.at[n])

    def read_groups():
        def body(src, _):
            for i in range(SLOTS):
                dest = route[i % K, (src * NY + y) * PER + i // K]
                here = (dest * 10923) >> 16
                group[src, i] = here
                local[src, i] = dest - here * PER
            return 0

        lax.fori_loop(0, NZ, body, 0)

    def read_picks():
        def body(h, _):
            first, last = jnp.int32(SLOTS), jnp.int32(SLOTS)
            for i in range(SLOTS):
                j = SLOTS - 1 - i
                first = jnp.where(group[z, j] == h, j, first)
                last = jnp.where(group[z, i] == h, i, last)
            pick[h, 0] = first
            pick[h, 1] = jnp.where(last == first, SLOTS, last)
            return 0

        lax.fori_loop(0, NZ * NY, body, 0)

    def read_places():
        def body(n, _):
            src, h = n // NY, z * NY + lax.rem(n, NY)
            first, last = jnp.int32(0), jnp.int32(0)
            for i in range(SLOTS):
                j = SLOTS - 1 - i
                first = jnp.where(group[src, j] == h, local[src, j], first)
                last = jnp.where(group[src, i] == h, local[src, i], last)
            place[n, 0] = first
            place[n, 1] = last
            return 0

        lax.fori_loop(0, NZ * NY, body, 0)

    lane_half = lax.broadcasted_iota(jnp.int32, (1, 1, 128), 2) // P_SIZE

    def product(d, half):
        a = yi(OFFS[d])
        at = [zi(dz) for dz in GROUPS[half]]
        lhs = jnp.concatenate([g[a * NZ + i] for i in at], axis=0)
        for b in range(PER):
            v = jnp.dot(lhs, env[b], preferred_element_type=F32).reshape(4, 4, 16, 256)
            for s in range(4):
                for t in range(2):
                    prod[d, b, t * 4 + s, 4 * half:4 * half + 4] = v[:, s, :, 128 * t:128 * (t + 1)]

    def make_terms(d, half):
        low = lane_half == 0

        def body(i, _):
            tiles = []
            for n in range(3 * K):
                b, k, total = 3 * i + n // K, n % K, None
                for j in range(2):
                    code = pair_index[k, j, b]
                    s, t = code >> 2, code & 3
                    w = jnp.where(lane_half == (t & 1), pair_value[k, j, b], 0.0)
                    add = w * prod[d, b, (t >> 1) * 4 + s, 4 * half:4 * half + 4]
                    total = add if total is None else total + add
                even, odd = total[:, :8], total[:, 8:]
                tiles.append(jnp.where(low, even, odd) + pltpu.roll(jnp.where(low, odd, even), P_SIZE, 2))
            for k in range(3 * K):
                for n, dz in enumerate(GROUPS[half]):
                    terms[d, dz % NZ, 3 * K * i + k] = tiles[k][n]
            return 0

        lax.fori_loop(0, PER // 3, body, 0)

    def mate_send(d, half):
        for n in (0, 1):
            lo, hi = PAIRS[2 * half + n]
            odd = lax.rem(zi(lo), 2) == core
            theirs = jnp.where(odd, zi(hi), zi(lo)) // 2
            src = terms.at[d, jnp.where(odd, hi % NZ, lo % NZ)]
            send(src, mate_in.at[d, theirs], sent.at[1], c_recv.at[d], mate)

    def x_step(d):
        arrived(mate_in.at[d], c_recv.at[d])
        for n, dx in enumerate((2, 1, -1, 0)):
            to = xi(dx)
            v = (terms[d, lax.rem(2 * to + core - z + NZ, NZ)] + mate_in[d, to]).reshape(SLOTS // 2, 16, 128)
            if dx == 0:
                x_own[d] = v
                continue
            q, code = encode(v)
            x_out[d, n, 0:SLOTS // 2] = q
            x_out[d, n, SLOTS // 2] = code
            send(x_out.at[d, n], x_in.at[d, n], sent.at[2], x_recv.at[d], at_x(dx))

    def z_step(d):
        arrived(x_in.at[d], x_recv.at[d])
        v = x_own[d]
        for n in range(3):
            v = v + decode(x_in[d, n])
        final[d, 0:SLOTS] = v.reshape(SLOTS, 8, 128)
        for dz in (4, 3, -3, 2, -2, 1, -1, 0):
            to = zi(dz)
            tiles = []
            for q in range(NY):
                for m in range(2):
                    tiles.append(final[d, pick[to * NY + q, m]])
            v = jnp.stack(tiles).reshape(NY, 16, 128)
            if dz == 0:
                z_own[d] = v
                continue
            n = dz % NZ - 1
            z_out[d, n], zc_out[d, n] = encode_rows(v)
            send(z_out.at[d, n], z_in.at[d, n], sent.at[3], z_recv.at[d], at_zy(dz, 0))
            send(zc_out.at[d, n], zc_in.at[d, n], sent.at[5], zc_recv.at[d], at_zy(dz, 0))

    def y_step(d):
        arrived(z_in.at[d], z_recv.at[d])
        arrived(zc_in.at[d], zc_recv.at[d])
        sums = [[None] * PER for _ in range(NY)]
        for n in range(NZ):
            src = z if n == 0 else zi(-n)
            v = z_own[d] if n == 0 else decode_rows(z_in[d, n - 1], zc_in[d, n - 1])
            for q in range(NY):
                for m in range(2):
                    at = place[src * NY + q, m]
                    tile = v[q, 8 * m:8 * m + 8]
                    spread = jnp.full((8, 128), at, jnp.int32)
                    for c in range(PER):
                        add = jnp.where(spread == c, tile, 0.0)
                        sums[q][c] = add if sums[q][c] is None else sums[q][c] + add
        for q in range(NY):
            y_sum[d, q] = jnp.stack(sums[q])
        for n, dy in enumerate((2, 1, -1)):
            y_out[d, n], yc_out[d, n] = encode_rows(y_sum[d, yi(dy)].reshape(PER // 2, 16, 128))
            send(y_out.at[d, n], y_in.at[d, n], sent.at[4], y_recv.at[d], at_zy(0, dy))
            send(yc_out.at[d, n], yc_in.at[d, n], sent.at[6], yc_recv.at[d], at_zy(0, dy))
        out[:, yi(OFFS[d])] += y_sum[d, y]

    def out_step(d):
        arrived(y_in.at[d], y_recv.at[d])
        arrived(yc_in.at[d], yc_recv.at[d])
        for n, dy in ((1, -1), (2, 1), (0, 2)):
            out[:, yi(dy + OFFS[d])] += decode_rows(y_in[d, n], yc_in[d, n]).reshape(PER, 8, 128)

    env_here = False
    for kind, d, h, dz, links in ORDER:
        if kind == "F":
            g_wait(d, h, dz)
            g_fwd(d, h, dz, links)
        elif kind == "G":
            for c in small_copies:
                c.wait()
            read_groups()
        elif kind == "I":
            read_picks()
        elif kind == "L":
            read_places()
        elif kind == "S":
            g_fwd(d, h, dz, links)
        elif kind == "P":
            if not env_here:
                env_copy.wait()
                env_here = True
            product(d, h)
        elif kind == "T":
            make_terms(d, h)
            mate_send(d, h)
        else:
            {"X": x_step, "Z": z_step, "Y": y_step, "O": out_step}[kind](d)
            if (kind, d) == ("X", 3):
                all_sent(g.at[0:NY * NZ - 1], 0)
                all_sent(mate_in, 1)
            if (kind, d) == ("Y", 3):
                all_sent(x_in, 2)
                all_sent(z_in, 3)
                all_sent(zc_in, 5)
    all_sent(y_in, 4)
    all_sent(yc_in, 6)


def lay_out(blocks, new_env):
    for n in range(NY * 8):
        new_env[:, 128 * n:128 * (n + 1)] = blocks[:, n // 8, n % 8, :]


def shards(env_blocks, site_rows, route_dest, pair_index, pair_value):
    depth = env_blocks.shape[1]
    tile = (8, 128)
    tile16 = (16, 128)
    bf16 = jnp.bfloat16
    dma = pltpu.SemaphoreType.DMA
    out = pl.pallas_call(
        kernel,
        out_shape=jax.ShapeDtypeStruct((PER, NY, 8, 128), F32),
        in_specs=[pl.BlockSpec(memory_space=pl.ANY)] * 5,
        out_specs=pl.BlockSpec(memory_space=pltpu.VMEM),
        scratch_shapes=[
            pltpu.VMEM((PER, depth, PD * P_SIZE), bf16),
            pltpu.VMEM(site_rows.shape, bf16),
            pltpu.VMEM((NY * NZ, 64, depth), bf16),
            pltpu.VMEM((4, PER, 8, NZ, 16, 128), F32),
            pltpu.VMEM((4, NZ, SLOTS) + tile, F32),
            pltpu.VMEM((4, NX, SLOTS) + tile, F32),
            pltpu.VMEM((4, SLOTS // 2) + tile16, F32),
            pltpu.VMEM((4, 3, SLOTS // 2 + 1) + tile16, I16),
            pltpu.VMEM((4, 3, SLOTS // 2 + 1) + tile16, I16),
            pltpu.VMEM((4, SLOTS + 1) + tile, F32),
            pltpu.VMEM((4, NY) + tile16, F32),
            pltpu.VMEM((4, NZ - 1, NY) + tile16, I16),
            pltpu.VMEM((4, NZ - 1, NY) + tile16, I16),
            pltpu.VMEM((4, NZ - 1, 1, 128), F32),
            pltpu.VMEM((4, NZ - 1, 1, 128), F32),
            pltpu.VMEM((4, NY, PER) + tile, F32),
            pltpu.VMEM((4, 3, PER // 2) + tile16, I16),
            pltpu.VMEM((4, 3, PER // 2) + tile16, I16),
            pltpu.VMEM((4, 3, 1, 128), F32),
            pltpu.VMEM((4, 3, 1, 128), F32),
            pltpu.SMEM((K, NZ * NY * PER), jnp.int32),
            pltpu.SMEM((K, 2, PER), jnp.int32),
            pltpu.SMEM((K, 2, PER), F32),
            pltpu.SMEM((NZ, SLOTS), jnp.int32),
            pltpu.SMEM((NZ, SLOTS), jnp.int32),
            pltpu.SMEM((NZ * NY, 2), jnp.int32),
            pltpu.SMEM((NZ * NY, 2), jnp.int32),
            dma((5,)),
            dma((7,)),
            dma((max(SEMS.values()) + 1,)),
            dma((4,)),
            dma((4,)),
            dma((4,)),
            dma((4,)),
            dma((4,)),
            dma((4,)),
        ],
        compiler_params=pltpu.CompilerParams(
            collective_id=0, has_side_effects=True, vmem_limit_bytes=56 * 1024 * 1024
        ),
        cost_estimate=pl.CostEstimate(
            flops=2 * 2048 * depth * PER * 256, bytes_accessed=4 * 1024 * 1024, transcendentals=0
        ),
    )(route_dest.T, pair_index.transpose(1, 2, 0), pair_value.transpose(1, 2, 0), site_rows, env_blocks)
    return pl.pallas_call(
        lay_out,
        out_shape=jax.ShapeDtypeStruct((PER, NY * 8 * 128), F32),
        in_specs=[pl.BlockSpec(memory_space=pltpu.VMEM)],
        out_specs=pl.BlockSpec(memory_space=pltpu.VMEM),
    )(out)


def solution(mesh):
    in_specs = (
        P("chan", "row", None),
        P("chan", None, "row"),
        P(),
        P("chan", None, None),
        P("chan", None, None),
    )
    out_specs = P("chan", "row")
    return jax.shard_map(shards, mesh=mesh, in_specs=in_specs, out_specs=out_specs, check_vma=False)
```

```python
import jax
import jax.numpy as jnp
from jax import lax
from jax.experimental import pallas as pl
from jax.experimental.pallas import tpu as pltpu
from jax.sharding import PartitionSpec as P

PD = 4
P_SIZE = 64
K = 5
NZ, NY, NX = 8, 4, 4
PER = 6
SLOTS = PER * K
OFFS = (0, 1, -1, 2)
OWN = ((0, 32), (32, 48), (48, 64))
NEAR = ((0, 48), (48, 64))
FAR = ((0, 32), (32, 64))
GROUPS = (((0, -1), (1, -2)), ((2, -3), (3, 4)))
GROUPS_FAR = (((0, -1), (1, -2), (2, 3)), ((-3, 4),))
LINKS = ((1, 0), (-1, 0), (0, 1), (0, -1), (0, 2))
MESH = pl.DeviceIdType.MESH
F32 = jnp.float32
I16 = jnp.int16

def cut(dy, part):
    return (OWN if dy == 0 else FAR if dy == 2 else NEAR)[part]


PARTS = tuple(
    (dy, part, dz)
    for dy in OFFS
    for part in range(len(OWN) if dy == 0 else 2)
    for dz in range(-3, 5)
    if (dy, dz) != (0, 0)
)
SHARED = {
    0: ((2, 0, 0), (2, 0, -1), (2, 0, 1), (2, 0, -2)),
    1: ((2, 0, 2), (2, 0, 3)),
    6: ((2, 0, -3), (2, 0, 4)),
    2: ((-1, 0, 1), (-1, 0, -2)),
    3: ((-1, 0, 3), (-1, 0, 4)),
    4: ((1, 0, 0), (1, 0, -1)),
    5: ((1, 0, 2), (1, 0, -3)),
}
SEMS = {part: n for n, parts in SHARED.items() for part in parts}
SEMS.update({part: len(SHARED) + n for n, part in enumerate(p for p in PARTS if p not in SEMS)})

ORDER = (
    ("F", 0, 2, 0, (0, 1)),
    ("F", 0, 1, 0, (0, 1)),
    ("F", 0, 0, 0, (0, 1)),
    ("S", 0, 11, 0, (2, 3, 4)),
    ("S", 0, 10, 0, (2, 3)),
    ("G", 0, 0, 0, ()),
    ("I", 0, 0, 0, ()),
    ("L", 0, 0, 0, ()),
    ("F", 0, 2, -1, (0,)),
    ("F", 0, 2, 1, (1,)),
    ("F", -1, 1, 0, ()),
    ("F", 1, 1, 0, ()),
    ("F", 0, 1, -1, (0,)),
    ("F", 0, 1, 1, (1,)),
    ("F", 2, 1, 0, ()),
    ("F", 0, 0, -1, (0,)),
    ("S", 0, 10, -1, (2, 3)),
    ("F", 0, 0, 1, (1,)),
    ("S", 0, 10, 1, (2, 3)),
    ("F", 1, 0, 0, ()),
    ("F", 0, 2, -2, (0,)),
    ("F", 0, 2, 2, (1,)),
    ("F", 0, 1, -2, (0,)),
    ("F", 0, 1, 2, (1,)),
    ("F", -1, 0, 0, ()),
    ("F", 0, 0, -2, (0,)),
    ("S", 0, 10, -2, (2, 3)),
    ("F", 0, 0, 2, (1,)),
    ("S", 0, 10, 2, (2, 3)),
    ("S", -1, 1, 0, (0,)),
    ("S", -1, 1, 0, (1,)),
    ("S", 1, 1, 0, (0,)),
    ("S", 1, 1, 0, (1,)),
    ("S", 2, 1, 0, (0,)),
    ("S", 2, 1, 0, (1,)),
    ("P", 0, 0, 0, ()),
    ("F", 0, 2, -3, ()),
    ("F", -1, 0, -1, ()),
    ("F", 1, 0, -1, ()),
    ("F", 0, 2, 3, (1,)),
    ("F", 0, 1, -3, (0,)),
    ("F", 0, 1, 3, ()),
    ("T", 0, 0, 0, ()),
    ("F", -1, 0, 1, ()),
    ("F", 1, 0, 1, ()),
    ("F", 0, 0, -3, (0,)),
    ("S", 0, 10, -3, (2, 3)),
    ("F", 0, 0, 3, ()),
    ("S", 0, 10, 3, (2, 3)),
    ("F", -1, 1, -1, (0,)),
    ("F", -1, 1, 1, (1,)),
    ("F", 1, 1, -1, (0,)),
    ("F", 1, 1, 1, (1,)),
    ("F", -1, 0, -2, ()),
    ("F", 1, 0, -2, ()),
    ("F", 2, 1, -1, (0,)),
    ("F", 2, 1, 1, (1,)),
    ("F", 0, 1, 4, ()),
    ("F", 0, 2, 4, ()),
    ("F", -1, 0, 2, ()),
    ("F", 1, 0, 2, ()),
    ("F", -1, 1, 2, (1,)),
    ("F", 0, 0, 4, ()),
    ("S", 0, 10, 4, (2, 3)),
    ("S", -1, 0, 0, (2,)),
    ("S", -1, 0, -1, (2,)),
    ("S", 1, 0, 1, (3,)),
    ("S", 1, 0, -2, (3,)),
    ("S", -1, 0, 2, (2,)),
    ("F", 1, 1, 2, (1,)),
    ("P", 0, 1, 0, ()),
    ("F", -1, 1, -2, (0,)),
    ("F", -1, 0, -3, (2,)),
    ("F", 1, 0, -3, ()),
    ("F", 1, 1, -2, (0,)),
    ("F", 2, 1, 2, (1,)),
    ("T", 0, 1, 0, ()),
    ("P", 1, 0, 0, ()),
    ("F", -1, 1, 3, (1,)),
    ("F", 2, 1, -2, (0,)),
    ("F", -1, 0, 3, ()),
    ("F", 1, 1, 3, (1,)),
    ("F", 1, 0, 3, (3,)),
    ("T", 1, 0, 0, ()),
    ("P", 2, 0, 0, ()),
    ("F", -1, 1, -3, ()),
    ("X", 0, 0, 0, ()),
    ("F", 1, 1, -3, ()),
    ("F", 2, 1, 3, (1,)),
    ("F", -1, 0, 4, ()),
    ("F", 1, 0, 4, (3,)),
    ("T", 2, 0, 0, ()),
    ("F", -1, 1, 4, ()),
    ("P", 2, 1, 0, ()),
    ("F", 2, 1, -3, ()),
    ("F", 1, 1, 4, ()),
    ("F", 2, 0, 0, ()),
    ("F", 2, 0, 1, ()),
    ("T", 2, 1, 0, ()),
    ("P", 1, 1, 0, ()),
    ("T", 1, 1, 0, ()),
    ("F", 2, 0, -1, ()),
    ("F", 2, 0, -2, ()),
    ("F", 2, 1, 4, ()),
    ("X", 2, 0, 0, ()),
    ("F", 2, 0, 2, ()),
    ("F", 2, 0, 3, ()),
    ("P", 3, 0, 0, ()),
    ("X", 1, 0, 0, ()),
    ("F", 2, 0, -3, ()),
    ("F", 2, 0, 4, ()),
    ("Z", 0, 0, 0, ()),
    ("T", 3, 0, 0, ()),
    ("P", 3, 1, 0, ()),
    ("T", 3, 1, 0, ()),
    ("Z", 2, 0, 0, ()),
    ("X", 3, 0, 0, ()),
    ("Z", 1, 0, 0, ()),
    ("Y", 0, 0, 0, ()),
    ("Y", 2, 0, 0, ()),
    ("Z", 3, 0, 0, ()),
    ("O", 0, 0, 0, ()),
    ("Y", 1, 0, 0, ()),
    ("O", 2, 0, 0, ()),
    ("O", 1, 0, 0, ()),
    ("Y", 3, 0, 0, ()),
    ("O", 3, 0, 0, ()),
)


def encode(v):
    most = jnp.maximum(jnp.max(jnp.abs(v), axis=0), 1e-30)
    code = jnp.ceil(jnp.log2(most) * 8.0)
    inverse = 32000.0 / jnp.exp2(code * 0.125)
    q = jnp.round(v * inverse[None]).astype(jnp.int32).astype(I16)
    return q, code.astype(jnp.int32).astype(I16)


def decode(q):
    n = q.shape[0] - 1
    scale = jnp.exp2(q[n].astype(F32) * 0.125) * (1.0 / 32000.0)
    return q[0:n].astype(F32) * scale[None]


def encode_rows(v):
    most = jnp.max(jnp.max(jnp.abs(v), axis=0), axis=0, keepdims=True)
    most = jnp.maximum(most, 1e-30)
    return jnp.round(v * (32000.0 / most)[None]).astype(jnp.int32).astype(I16), most


def decode_rows(q, most):
    return q.astype(F32) * (most * (1.0 / 32000.0))[None]


def kernel(
    route_hbm, index_hbm, value_hbm, site_hbm, env_hbm, out,
    env, site, g, prod, terms, mate_in, x_own, x_out, x_in, final, z_own, z_out, z_in, zc_out, zc_in, y_sum, y_out, y_in, yc_out, yc_in,
    route, pair_index, pair_value, group, local, pick, place,
    local_sem, sent, g_recv, c_recv, x_recv, z_recv, y_recv, zc_recv, yc_recv,
):
    chan, row = lax.axis_index("chan"), lax.axis_index("row")
    z, y = chan // NY, lax.rem(chan, NY)
    x, core = row // 2, lax.rem(row, 2)

    def zi(d):
        return lax.rem(z + d + NZ, NZ)

    def yi(d):
        return lax.rem(y + d + NY, NY)

    def xi(d):
        return lax.rem(x + d + NX, NX)

    def at_zy(dz, dy):
        return (zi(dz) * NY + yi(dy), row)

    def at_x(d):
        return (chan, xi(d) * 2 + core)

    mate = (chan, x * 2 + 1 - core)

    barrier = pltpu.get_barrier_semaphore()
    partners = [mate] + [at_x(d) for d in (1, 2, 3)] + [at_zy(0, d) for d in (1, 2, 3)]
    partners += [at_zy(d, 0) for d in range(1, NZ)]
    for p in partners:
        pl.semaphore_signal(barrier, inc=1, device_id=p, device_id_type=MESH)
    site_copy = pltpu.make_async_copy(site_hbm, site, local_sem.at[1])
    site_copy.start()
    small_copies = [
        pltpu.make_async_copy(src, dst, local_sem.at[2 + n])
        for n, (src, dst) in enumerate(
            ((route_hbm, route), (index_hbm, pair_index), (value_hbm, pair_value))
        )
    ]
    for c in small_copies:
        c.start()
    env_copy = pltpu.make_async_copy(env_hbm, env, local_sem.at[0])
    env_copy.start()

    out[...] = jnp.zeros_like(out)
    for d in range(4):
        final[d, SLOTS] = jnp.zeros((8, 128), F32)
    new = lax.broadcasted_iota(jnp.int32, (64, 64), 0)
    old = lax.broadcasted_iota(jnp.int32, (64, 64), 1)
    moved = (new & 7) * 8 + ((new >> 3) & 1) * 4 + (new >> 4)
    turn = jnp.where(moved == old, 1.0, 0.0).astype(jnp.bfloat16)
    site_copy.wait()
    rows = site[...].astype(F32).reshape(64, site.shape[2]).astype(jnp.bfloat16)
    g[y * NZ + z] = jnp.dot(turn, rows, preferred_element_type=F32).astype(jnp.bfloat16)
    pl.semaphore_wait(barrier, len(partners))

    def send(src, dst, s_sem, r_sem, dev):
        pltpu.make_async_remote_copy(
            src_ref=src, dst_ref=dst, send_sem=s_sem, recv_sem=r_sem, device_id=dev, device_id_type=MESH
        ).start()

    def arrived(like, r_sem):
        pltpu.make_async_remote_copy(
            src_ref=like, dst_ref=like, send_sem=sent.at[0], recv_sem=r_sem, device_id=mate, device_id_type=MESH
        ).wait_recv()

    def all_sent(like, n):
        pltpu.make_async_remote_copy(
            src_ref=like, dst_ref=like, send_sem=sent.at[n], recv_sem=g_recv.at[0], device_id=mate, device_id_type=MESH
        ).wait_send()

    def g_fwd(dy, h, dz, links):
        for link in links:
            step_z, step_y = LINKS[link]
            there = ((dy - step_y + 1) % NY - 1, 1 if link == 4 else h % 10, (dz - step_z + 3) % NZ - 3)
            lo, hi = cut(there[0], there[1])
            ref = g.at[yi(dy) * NZ + zi(dz), lo:hi]
            send(ref, ref, sent.at[0], g_recv.at[SEMS[there]], at_zy(step_z, step_y))

    seen = {n: 0 for n in SEMS.values()}

    def g_wait(dy, h, dz):
        n = SEMS.get((dy, h, dz))
        if n is None:
            return
        seen[n] += 1
        count = len(SHARED.get(n, (0,)))
        if seen[n] == count:
            lo, hi = cut(dy, h)
            arrived(g.at[0:count, lo:hi], g_recv.at[n])

    def read_groups():
        def body(src, _):
            for i in range(SLOTS):
                dest = route[i % K, (src * NY + y) * PER + i // K]
                here = (dest * 10923) >> 16
                group[src, i] = here
                local[src, i] = dest - here * PER
            return 0

        lax.fori_loop(0, NZ, body, 0)

    def read_picks():
        def body(h, _):
            first, last = jnp.int32(SLOTS), jnp.int32(SLOTS)
            for i in range(SLOTS):
                j = SLOTS - 1 - i
                first = jnp.where(group[z, j] == h, j, first)
                last = jnp.where(group[z, i] == h, i, last)
            pick[h, 0] = first
            pick[h, 1] = jnp.where(last == first, SLOTS, last)
            return 0

        lax.fori_loop(0, NZ * NY, body, 0)

    def read_places():
        def body(n, _):
            src, h = n // NY, z * NY + lax.rem(n, NY)
            first, last = jnp.int32(0), jnp.int32(0)
            for i in range(SLOTS):
                j = SLOTS - 1 - i
                first = jnp.where(group[src, j] == h, local[src, j], first)
                last = jnp.where(group[src, i] == h, local[src, i], last)
            place[n, 0] = first
            place[n, 1] = last
            return 0

        lax.fori_loop(0, NZ * NY, body, 0)

    lane_half = lax.broadcasted_iota(jnp.int32, (1, 1, 128), 2) // P_SIZE

    def group_of(d, half):
        groups = GROUPS_FAR if d == 3 else GROUPS
        offsets = [dz for pair in groups[half] for dz in pair]
        first = 2 * len(groups[0]) if half else 0
        return groups[half], offsets, slice(first, first + len(offsets))

    def product(d, half):
        a = yi(OFFS[d])
        _, offsets, span = group_of(d, half)
        at = [zi(dz) for dz in offsets]
        lhs = jnp.concatenate([g[a * NZ + i] for i in at], axis=0)
        for b in range(PER):
            v = jnp.dot(lhs, env[b], preferred_element_type=F32).reshape(len(at), 4, 16, 256)
            for s in range(4):
                for t in range(2):
                    prod[d, b, t * 4 + s, span] = v[:, s, :, 128 * t:128 * (t + 1)]

    def make_terms(d, half):
        low = lane_half == 0
        _, offsets, span = group_of(d, half)

        def body(i, _):
            tiles = []
            for n in range(3 * K):
                b, k, total = 3 * i + n // K, n % K, None
                for j in range(2):
                    code = pair_index[k, j, b]
                    s, t = code >> 2, code & 3
                    w = jnp.where(lane_half == (t & 1), pair_value[k, j, b], 0.0)
                    add = w * prod[d, b, (t >> 1) * 4 + s, span]
                    total = add if total is None else total + add
                even, odd = total[:, :8], total[:, 8:]
                tiles.append(jnp.where(low, even, odd) + pltpu.roll(jnp.where(low, odd, even), P_SIZE, 2))
            for k in range(3 * K):
                for n, dz in enumerate(offsets):
                    terms[d, dz % NZ, 3 * K * i + k] = tiles[k][n]
            return 0

        if d == 3:
            for i in range(PER // 3):
                body(i, 0)
                mate_send(d, half, 3 * K * i, 3 * K)
        else:
            lax.fori_loop(0, PER // 3, body, 0)
            mate_send(d, half, 0, SLOTS)

    def mate_send(d, half, lo_term, n_terms):
        span = pl.ds(lo_term, n_terms)
        for lo, hi in group_of(d, half)[0]:
            odd = lax.rem(zi(lo), 2) == core
            theirs = jnp.where(odd, zi(hi), zi(lo)) // 2
            src = terms.at[d, jnp.where(odd, hi % NZ, lo % NZ), span]
            send(src, mate_in.at[d, theirs, span], sent.at[1], c_recv.at[d], mate)

    def x_step(d):
        arrived(mate_in.at[d], c_recv.at[d])
        for n, dx in enumerate((2, 1, -1, 0)):
            to = xi(dx)
            v = (terms[d, lax.rem(2 * to + core - z + NZ, NZ)] + mate_in[d, to]).reshape(SLOTS // 2, 16, 128)
            if dx == 0:
                x_own[d] = v
                continue
            q, code = encode(v)
            x_out[d, n, 0:SLOTS // 2] = q
            x_out[d, n, SLOTS // 2] = code
            send(x_out.at[d, n], x_in.at[d, n], sent.at[2], x_recv.at[d], at_x(dx))

    def z_step(d):
        arrived(x_in.at[d], x_recv.at[d])
        v = x_own[d]
        for n in range(3):
            v = v + decode(x_in[d, n])
        final[d, 0:SLOTS] = v.reshape(SLOTS, 8, 128)
        for dz in (4, 3, -3, 2, -2, 1, -1, 0):
            to = zi(dz)
            tiles = []
            for q in range(NY):
                for m in range(2):
                    tiles.append(final[d, pick[to * NY + q, m]])
            v = jnp.stack(tiles).reshape(NY, 16, 128)
            if dz == 0:
                z_own[d] = v
                continue
            n = dz % NZ - 1
            z_out[d, n], zc_out[d, n] = encode_rows(v)
            send(z_out.at[d, n], z_in.at[d, n], sent.at[3], z_recv.at[d], at_zy(dz, 0))
            send(zc_out.at[d, n], zc_in.at[d, n], sent.at[5], zc_recv.at[d], at_zy(dz, 0))

    def y_step(d):
        arrived(z_in.at[d], z_recv.at[d])
        arrived(zc_in.at[d], zc_recv.at[d])
        sums = [[None] * PER for _ in range(NY)]
        for n in range(NZ):
            src = z if n == 0 else zi(-n)
            v = z_own[d] if n == 0 else decode_rows(z_in[d, n - 1], zc_in[d, n - 1])
            for q in range(NY):
                for m in range(2):
                    at = place[src * NY + q, m]
                    tile = v[q, 8 * m:8 * m + 8]
                    spread = jnp.full((8, 128), at, jnp.int32)
                    for c in range(PER):
                        add = jnp.where(spread == c, tile, 0.0)
                        sums[q][c] = add if sums[q][c] is None else sums[q][c] + add
        for q in range(NY):
            y_sum[d, q] = jnp.stack(sums[q])
        for n, dy in enumerate((2, 1, -1)):
            y_out[d, n], yc_out[d, n] = encode_rows(y_sum[d, yi(dy)].reshape(PER // 2, 16, 128))
            send(y_out.at[d, n], y_in.at[d, n], sent.at[4], y_recv.at[d], at_zy(0, dy))
            send(yc_out.at[d, n], yc_in.at[d, n], sent.at[6], yc_recv.at[d], at_zy(0, dy))
        out[:, yi(OFFS[d])] += y_sum[d, y]

    def out_step(d):
        arrived(y_in.at[d], y_recv.at[d])
        arrived(yc_in.at[d], yc_recv.at[d])
        for n, dy in ((1, -1), (2, 1), (0, 2)):
            out[:, yi(dy + OFFS[d])] += decode_rows(y_in[d, n], yc_in[d, n]).reshape(PER, 8, 128)

    env_here = False
    for kind, d, h, dz, links in ORDER:
        if kind == "F":
            g_wait(d, h, dz)
            g_fwd(d, h, dz, links)
        elif kind == "G":
            for c in small_copies:
                c.wait()
            read_groups()
        elif kind == "I":
            read_picks()
        elif kind == "L":
            read_places()
        elif kind == "S":
            g_fwd(d, h, dz, links)
        elif kind == "P":
            if not env_here:
                env_copy.wait()
                env_here = True
            product(d, h)
        elif kind == "T":
            make_terms(d, h)
        else:
            {"X": x_step, "Z": z_step, "Y": y_step, "O": out_step}[kind](d)
            if (kind, d) == ("X", 3):
                all_sent(g.at[0:NY * NZ - 1], 0)
                all_sent(mate_in, 1)
            if (kind, d) == ("Y", 3):
                all_sent(x_in, 2)
                all_sent(z_in, 3)
                all_sent(zc_in, 5)
    all_sent(y_in, 4)
    all_sent(yc_in, 6)


def shards(env_blocks, site_rows, route_dest, pair_index, pair_value):
    depth = env_blocks.shape[1]
    tile = (8, 128)
    tile16 = (16, 128)
    bf16 = jnp.bfloat16
    dma = pltpu.SemaphoreType.DMA
    out = pl.pallas_call(
        kernel,
        out_shape=jax.ShapeDtypeStruct((PER, NY, 8, 128), F32),
        in_specs=[pl.BlockSpec(memory_space=pl.ANY)] * 5,
        out_specs=pl.BlockSpec(memory_space=pltpu.VMEM),
        scratch_shapes=[
            pltpu.VMEM((PER, depth, PD * P_SIZE), bf16),
            pltpu.VMEM(site_rows.shape, bf16),
            pltpu.VMEM((NY * NZ, 64, depth), bf16),
            pltpu.VMEM((4, PER, 8, NZ, 16, 128), F32),
            pltpu.VMEM((4, NZ, SLOTS) + tile, F32),
            pltpu.VMEM((4, NX, SLOTS) + tile, F32),
            pltpu.VMEM((4, SLOTS // 2) + tile16, F32),
            pltpu.VMEM((4, 3, SLOTS // 2 + 1) + tile16, I16),
            pltpu.VMEM((4, 3, SLOTS // 2 + 1) + tile16, I16),
            pltpu.VMEM((4, SLOTS + 1) + tile, F32),
            pltpu.VMEM((4, NY) + tile16, F32),
            pltpu.VMEM((4, NZ - 1, NY) + tile16, I16),
            pltpu.VMEM((4, NZ - 1, NY) + tile16, I16),
            pltpu.VMEM((4, NZ - 1, 1, 128), F32),
            pltpu.VMEM((4, NZ - 1, 1, 128), F32),
            pltpu.VMEM((4, NY, PER) + tile, F32),
            pltpu.VMEM((4, 3, PER // 2) + tile16, I16),
            pltpu.VMEM((4, 3, PER // 2) + tile16, I16),
            pltpu.VMEM((4, 3, 1, 128), F32),
            pltpu.VMEM((4, 3, 1, 128), F32),
            pltpu.SMEM((K, NZ * NY * PER), jnp.int32),
            pltpu.SMEM((K, 2, PER), jnp.int32),
            pltpu.SMEM((K, 2, PER), F32),
            pltpu.SMEM((NZ, SLOTS), jnp.int32),
            pltpu.SMEM((NZ, SLOTS), jnp.int32),
            pltpu.SMEM((NZ * NY, 2), jnp.int32),
            pltpu.SMEM((NZ * NY, 2), jnp.int32),
            dma((5,)),
            dma((7,)),
            dma((max(SEMS.values()) + 1,)),
            dma((4,)),
            dma((4,)),
            dma((4,)),
            dma((4,)),
            dma((4,)),
            dma((4,)),
        ],
        compiler_params=pltpu.CompilerParams(
            collective_id=0, has_side_effects=True, vmem_limit_bytes=56 * 1024 * 1024
        ),
        cost_estimate=pl.CostEstimate(
            flops=2 * 2048 * depth * PER * 256, bytes_accessed=4 * 1024 * 1024, transcendentals=0
        ),
    )(route_dest.T, pair_index.transpose(1, 2, 0), pair_value.transpose(1, 2, 0), site_rows, env_blocks)
    return out.reshape(PER, -1)


def solution(mesh):
    in_specs = (
        P("chan", "row", None),
        P("chan", None, "row"),
        P(),
        P("chan", None, None),
        P("chan", None, None),
    )
    out_specs = P("chan", "row")
    return jax.shard_map(shards, mesh=mesh, in_specs=in_specs, out_specs=out_specs, check_vma=False)
```

```python
import jax
import jax.numpy as jnp
from jax import lax
from jax.experimental import pallas as pl
from jax.experimental.pallas import tpu as pltpu
from jax.sharding import PartitionSpec as P

PD = 4
P_SIZE = 64
K = 5
NZ, NY, NX = 8, 4, 4
PER = 6
SLOTS = PER * K
OFFS = (0, 1, -1, 2)
OWN = ((0, 32), (32, 48), (48, 64))
NEAR = ((0, 48), (48, 64))
FAR = ((0, 32), (32, 64))
GROUPS = ((0, -1, 1, -2), (2, -3, 3, 4))
PAIRS = ((0, -1), (1, -2), (2, -3), (3, 4))
LINKS = ((1, 0), (-1, 0), (0, 1), (0, -1), (0, 2))
MESH = pl.DeviceIdType.MESH
F32 = jnp.float32
I16 = jnp.int16

def cut(dy, part):
    return (OWN if dy == 0 else FAR if dy == 2 else NEAR)[part]


PARTS = tuple(
    (dy, part, dz)
    for dy in OFFS
    for part in range(len(OWN) if dy == 0 else 2)
    for dz in range(-3, 5)
    if (dy, dz) != (0, 0)
)
SHARED = {
    0: ((2, 0, 0), (2, 0, -1), (2, 0, 1), (2, 0, -2)),
    1: ((2, 0, 2), (2, 0, -3), (2, 0, 3), (2, 0, 4)),
    2: ((-1, 0, 1), (-1, 0, -2)),
    3: ((-1, 0, 3), (-1, 0, 4)),
    4: ((1, 0, 0), (1, 0, -1)),
    5: ((1, 0, 2), (1, 0, -3)),
}
SEMS = {part: n for n, parts in SHARED.items() for part in parts}
SEMS.update({part: len(SHARED) + n for n, part in enumerate(p for p in PARTS if p not in SEMS)})

ORDER = (
    ("F", 0, 2, 0, (0, 1)),
    ("F", 0, 1, 0, (0, 1)),
    ("F", 0, 0, 0, (0, 1)),
    ("S", 0, 11, 0, (2, 3, 4)),
    ("S", 0, 10, 0, (2, 3)),
    ("G", 0, 0, 0, ()),
    ("I", 0, 0, 0, ()),
    ("L", 0, 0, 0, ()),
    ("F", 0, 2, -1, (0,)),
    ("F", 0, 2, 1, (1,)),
    ("F", -1, 1, 0, ()),
    ("F", 1, 1, 0, ()),
    ("F", 0, 1, -1, (0,)),
    ("F", 0, 1, 1, (1,)),
    ("F", 2, 1, 0, ()),
    ("F", 0, 0, -1, (0,)),
    ("S", 0, 10, -1, (2, 3)),
    ("F", 0, 0, 1, (1,)),
    ("S", 0, 10, 1, (2, 3)),
    ("F", 1, 0, 0, ()),
    ("F", 0, 2, -2, (0,)),
    ("F", 0, 2, 2, (1,)),
    ("F", 0, 1, -2, (0,)),
    ("F", 0, 1, 2, (1,)),
    ("F", -1, 0, 0, ()),
    ("F", 0, 0, -2, (0,)),
    ("S", 0, 10, -2, (2, 3)),
    ("F", 0, 0, 2, (1,)),
    ("S", 0, 10, 2, (2, 3)),
    ("S", -1, 1, 0, (0,)),
    ("S", -1, 1, 0, (1,)),
    ("S", 1, 1, 0, (0,)),
    ("S", 1, 1, 0, (1,)),
    ("S", 2, 1, 0, (0,)),
    ("S", 2, 1, 0, (1,)),
    ("P", 0, 0, 0, ()),
    ("F", 0, 2, -3, ()),
    ("F", -1, 0, -1, ()),
    ("F", 1, 0, -1, ()),
    ("F", 0, 2, 3, (1,)),
    ("F", 0, 1, -3, (0,)),
    ("F", 0, 1, 3, ()),
    ("T", 0, 0, 0, ()),
    ("F", -1, 0, 1, ()),
    ("F", 1, 0, 1, ()),
    ("F", 0, 0, -3, (0,)),
    ("S", 0, 10, -3, (2, 3)),
    ("F", 0, 0, 3, ()),
    ("S", 0, 10, 3, (2, 3)),
    ("F", -1, 1, -1, (0,)),
    ("F", -1, 1, 1, (1,)),
    ("F", 1, 1, -1, (0,)),
    ("F", 1, 1, 1, (1,)),
    ("F", -1, 0, -2, ()),
    ("F", 1, 0, -2, ()),
    ("F", 2, 1, -1, (0,)),
    ("F", 2, 1, 1, (1,)),
    ("F", 0, 1, 4, ()),
    ("F", 0, 2, 4, ()),
    ("F", -1, 0, 2, ()),
    ("F", 1, 0, 2, ()),
    ("F", -1, 1, 2, (1,)),
    ("F", 0, 0, 4, ()),
    ("S", 0, 10, 4, (2, 3)),
    ("S", -1, 0, 0, (2,)),
    ("S", -1, 0, -1, (2,)),
    ("S", 1, 0, 1, (3,)),
    ("S", 1, 0, -2, (3,)),
    ("S", -1, 0, 2, (2,)),
    ("F", 1, 1, 2, (1,)),
    ("P", 0, 1, 0, ()),
    ("F", -1, 1, -2, (0,)),
    ("F", -1, 0, -3, (2,)),
    ("F", 1, 0, -3, ()),
    ("F", 1, 1, -2, (0,)),
    ("F", 2, 1, 2, (1,)),
    ("T", 0, 1, 0, ()),
    ("P", 1, 0, 0, ()),
    ("F", -1, 1, 3, (1,)),
    ("F", 2, 1, -2, (0,)),
    ("F", -1, 0, 3, ()),
    ("F", 1, 1, 3, (1,)),
    ("F", 1, 0, 3, (3,)),
    ("T", 1, 0, 0, ()),
    ("P", 2, 0, 0, ()),
    ("F", -1, 1, -3, ()),
    ("X", 0, 0, 0, ()),
    ("F", 1, 1, -3, ()),
    ("F", 2, 1, 3, (1,)),
    ("F", -1, 0, 4, ()),
    ("F", 1, 0, 4, (3,)),
    ("T", 2, 0, 0, ()),
    ("F", -1, 1, 4, ()),
    ("P", 2, 1, 0, ()),
    ("F", 2, 1, -3, ()),
    ("F", 1, 1, 4, ()),
    ("F", 2, 0, 0, ()),
    ("F", 2, 0, 1, ()),
    ("T", 2, 1, 0, ()),
    ("P", 1, 1, 0, ()),
    ("T", 1, 1, 0, ()),
    ("F", 2, 0, -1, ()),
    ("F", 2, 0, -2, ()),
    ("P", 3, 0, 0, ()),
    ("F", 2, 1, 4, ()),
    ("X", 2, 0, 0, ()),
    ("F", 2, 0, 2, ()),
    ("F", 2, 0, 3, ()),
    ("T", 3, 0, 0, ()),
    ("X", 1, 0, 0, ()),
    ("F", 2, 0, -3, ()),
    ("F", 2, 0, 4, ()),
    ("Z", 0, 0, 0, ()),
    ("P", 3, 1, 0, ()),
    ("T", 3, 1, 0, ()),
    ("X", 3, 0, 0, ()),
    ("Z", 2, 0, 0, ()),
    ("Y", 0, 0, 0, ()),
    ("Z", 1, 0, 0, ()),
    ("O", 0, 0, 0, ()),
    ("Z", 3, 0, 0, ()),
    ("Y", 2, 0, 0, ()),
    ("Y", 1, 0, 0, ()),
    ("O", 2, 0, 0, ()),
    ("Y", 3, 0, 0, ()),
    ("O", 1, 0, 0, ()),
    ("O", 3, 0, 0, ()),
)


def encode(v):
    most = jnp.maximum(jnp.max(jnp.abs(v), axis=0), 1e-30)
    code = jnp.ceil(jnp.log2(most) * 8.0)
    inverse = 32000.0 / jnp.exp2(code * 0.125)
    q = jnp.round(v * inverse[None]).astype(jnp.int32).astype(I16)
    return q, code.astype(jnp.int32).astype(I16)


def decode(q):
    n = q.shape[0] - 1
    scale = jnp.exp2(q[n].astype(F32) * 0.125) * (1.0 / 32000.0)
    return q[0:n].astype(F32) * scale[None]


def encode_rows(v):
    most = jnp.max(jnp.max(jnp.abs(v), axis=0), axis=0, keepdims=True)
    most = jnp.maximum(most, 1e-30)
    return jnp.round(v * (32000.0 / most)[None]).astype(jnp.int32).astype(I16), most


def decode_rows(q, most):
    return q.astype(F32) * (most * (1.0 / 32000.0))[None]


def kernel(
    route_hbm, index_hbm, value_hbm, site_hbm, env_hbm, out,
    env, site, g, prod, terms, mate_in, x_own, x_out, x_in, final, z_own, z_out, z_in, zc_out, zc_in, y_sum, y_out, y_in, yc_out, yc_in,
    route, pair_index, pair_value, group, local, pick, place,
    local_sem, sent, g_recv, c_recv, x_recv, z_recv, y_recv, zc_recv, yc_recv,
):
    chan, row = lax.axis_index("chan"), lax.axis_index("row")
    z, y = chan // NY, lax.rem(chan, NY)
    x, core = row // 2, lax.rem(row, 2)

    def zi(d):
        return lax.rem(z + d + NZ, NZ)

    def yi(d):
        return lax.rem(y + d + NY, NY)

    def xi(d):
        return lax.rem(x + d + NX, NX)

    def at_zy(dz, dy):
        return (zi(dz) * NY + yi(dy), row)

    def at_x(d):
        return (chan, xi(d) * 2 + core)

    mate = (chan, x * 2 + 1 - core)

    barrier = pltpu.get_barrier_semaphore()
    partners = [mate] + [at_x(d) for d in (1, 2, 3)] + [at_zy(0, d) for d in (1, 2, 3)]
    partners += [at_zy(d, 0) for d in range(1, NZ)]
    for p in partners:
        pl.semaphore_signal(barrier, inc=1, device_id=p, device_id_type=MESH)
    site_copy = pltpu.make_async_copy(site_hbm, site, local_sem.at[1])
    site_copy.start()
    small_copies = [
        pltpu.make_async_copy(src, dst, local_sem.at[2 + n])
        for n, (src, dst) in enumerate(
            ((route_hbm, route), (index_hbm, pair_index), (value_hbm, pair_value))
        )
    ]
    for c in small_copies:
        c.start()
    env_copy = pltpu.make_async_copy(env_hbm, env, local_sem.at[0])
    env_copy.start()

    out[...] = jnp.zeros_like(out)
    for d in range(4):
        final[d, SLOTS] = jnp.zeros((8, 128), F32)
    new = lax.broadcasted_iota(jnp.int32, (64, 64), 0)
    old = lax.broadcasted_iota(jnp.int32, (64, 64), 1)
    moved = (new & 7) * 8 + ((new >> 3) & 1) * 4 + (new >> 4)
    turn = jnp.where(moved == old, 1.0, 0.0).astype(jnp.bfloat16)
    site_copy.wait()
    rows = site[...].astype(F32).reshape(64, site.shape[2]).astype(jnp.bfloat16)
    g[y * NZ + z] = jnp.dot(turn, rows, preferred_element_type=F32).astype(jnp.bfloat16)
    pl.semaphore_wait(barrier, len(partners))

    def send(src, dst, s_sem, r_sem, dev):
        pltpu.make_async_remote_copy(
            src_ref=src, dst_ref=dst, send_sem=s_sem, recv_sem=r_sem, device_id=dev, device_id_type=MESH
        ).start()

    def arrived(like, r_sem):
        pltpu.make_async_remote_copy(
            src_ref=like, dst_ref=like, send_sem=sent.at[0], recv_sem=r_sem, device_id=mate, device_id_type=MESH
        ).wait_recv()

    def all_sent(like, n):
        pltpu.make_async_remote_copy(
            src_ref=like, dst_ref=like, send_sem=sent.at[n], recv_sem=g_recv.at[0], device_id=mate, device_id_type=MESH
        ).wait_send()

    def g_fwd(dy, h, dz, links):
        for link in links:
            step_z, step_y = LINKS[link]
            there = ((dy - step_y + 1) % NY - 1, 1 if link == 4 else h % 10, (dz - step_z + 3) % NZ - 3)
            lo, hi = cut(there[0], there[1])
            ref = g.at[yi(dy) * NZ + zi(dz), lo:hi]
            send(ref, ref, sent.at[0], g_recv.at[SEMS[there]], at_zy(step_z, step_y))

    seen = {n: 0 for n in SEMS.values()}

    def g_wait(dy, h, dz):
        n = SEMS.get((dy, h, dz))
        if n is None:
            return
        seen[n] += 1
        count = len(SHARED.get(n, (0,)))
        if seen[n] == count:
            lo, hi = cut(dy, h)
            arrived(g.at[0:count, lo:hi], g_recv.at[n])

    def read_groups():
        def body(src, _):
            for i in range(SLOTS):
                dest = route[i % K, (src * NY + y) * PER + i // K]
                here = (dest * 10923) >> 16
                group[src, i] = here
                local[src, i] = dest - here * PER
            return 0

        lax.fori_loop(0, NZ, body, 0)

    def read_picks():
        def body(h, _):
            first, last = jnp.int32(SLOTS), jnp.int32(SLOTS)
            for i in range(SLOTS):
                j = SLOTS - 1 - i
                first = jnp.where(group[z, j] == h, j, first)
                last = jnp.where(group[z, i] == h, i, last)
            pick[h, 0] = first
            pick[h, 1] = jnp.where(last == first, SLOTS, last)
            return 0

        lax.fori_loop(0, NZ * NY, body, 0)

    def read_places():
        def body(n, _):
            src, h = n // NY, z * NY + lax.rem(n, NY)
            first, last = jnp.int32(0), jnp.int32(0)
            for i in range(SLOTS):
                j = SLOTS - 1 - i
                first = jnp.where(group[src, j] == h, local[src, j], first)
                last = jnp.where(group[src, i] == h, local[src, i], last)
            place[n, 0] = first
            place[n, 1] = last
            return 0

        lax.fori_loop(0, NZ * NY, body, 0)

    lane_half = lax.broadcasted_iota(jnp.int32, (1, 1, 128), 2) // P_SIZE

    def product(d, half):
        a = yi(OFFS[d])
        at = [zi(dz) for dz in GROUPS[half]]
        lhs = jnp.concatenate([g[a * NZ + i] for i in at], axis=0)
        for b in range(PER):
            v = jnp.dot(lhs, env[b], preferred_element_type=F32).reshape(4, 4, 16, 256)
            for s in range(4):
                for t in range(2):
                    prod[d, b, t * 4 + s, 4 * half:4 * half + 4] = v[:, s, :, 128 * t:128 * (t + 1)]

    def make_terms(d, half):
        low = lane_half == 0

        def body(i, _):
            tiles = []
            for n in range(3 * K):
                b, k, total = 3 * i + n // K, n % K, None
                for j in range(2):
                    code = pair_index[k, j, b]
                    s, t = code >> 2, code & 3
                    w = jnp.where(lane_half == (t & 1), pair_value[k, j, b], 0.0)
                    add = w * prod[d, b, (t >> 1) * 4 + s, 4 * half:4 * half + 4]
                    total = add if total is None else total + add
                even, odd = total[:, :8], total[:, 8:]
                tiles.append(jnp.where(low, even, odd) + pltpu.roll(jnp.where(low, odd, even), P_SIZE, 2))
            for k in range(3 * K):
                for n, dz in enumerate(GROUPS[half]):
                    terms[d, dz % NZ, 3 * K * i + k] = tiles[k][n]
            return 0

        if d == 3:
            for i in range(PER // 3):
                body(i, 0)
                mate_send(d, half, 3 * K * i, 3 * K)
        else:
            lax.fori_loop(0, PER // 3, body, 0)
            mate_send(d, half, 0, SLOTS)

    def mate_send(d, half, lo_term, n_terms):
        span = pl.ds(lo_term, n_terms)
        for n in (0, 1):
            lo, hi = PAIRS[2 * half + n]
            odd = lax.rem(zi(lo), 2) == core
            theirs = jnp.where(odd, zi(hi), zi(lo)) // 2
            src = terms.at[d, jnp.where(odd, hi % NZ, lo % NZ), span]
            send(src, mate_in.at[d, theirs, span], sent.at[1], c_recv.at[d], mate)

    def x_step(d):
        arrived(mate_in.at[d], c_recv.at[d])
        for n, dx in enumerate((2, 1, -1, 0)):
            to = xi(dx)
            v = (terms[d, lax.rem(2 * to + core - z + NZ, NZ)] + mate_in[d, to]).reshape(SLOTS // 2, 16, 128)
            if dx == 0:
                x_own[d] = v
                continue
            q, code = encode(v)
            x_out[d, n, 0:SLOTS // 2] = q
            x_out[d, n, SLOTS // 2] = code
            send(x_out.at[d, n], x_in.at[d, n], sent.at[2], x_recv.at[d], at_x(dx))

    def z_step(d):
        arrived(x_in.at[d], x_recv.at[d])
        v = x_own[d]
        for n in range(3):
            v = v + decode(x_in[d, n])
        final[d, 0:SLOTS] = v.reshape(SLOTS, 8, 128)
        for dz in (4, 3, -3, 2, -2, 1, -1, 0):
            to = zi(dz)
            tiles = []
            for q in range(NY):
                for m in range(2):
                    tiles.append(final[d, pick[to * NY + q, m]])
            v = jnp.stack(tiles).reshape(NY, 16, 128)
            if dz == 0:
                z_own[d] = v
                continue
            n = dz % NZ - 1
            z_out[d, n], zc_out[d, n] = encode_rows(v)
            send(z_out.at[d, n], z_in.at[d, n], sent.at[3], z_recv.at[d], at_zy(dz, 0))
            send(zc_out.at[d, n], zc_in.at[d, n], sent.at[5], zc_recv.at[d], at_zy(dz, 0))

    def y_step(d):
        arrived(z_in.at[d], z_recv.at[d])
        arrived(zc_in.at[d], zc_recv.at[d])
        sums = [[None] * PER for _ in range(NY)]
        for n in range(NZ):
            src = z if n == 0 else zi(-n)
            v = z_own[d] if n == 0 else decode_rows(z_in[d, n - 1], zc_in[d, n - 1])
            for q in range(NY):
                for m in range(2):
                    at = place[src * NY + q, m]
                    tile = v[q, 8 * m:8 * m + 8]
                    spread = jnp.full((8, 128), at, jnp.int32)
                    for c in range(PER):
                        add = jnp.where(spread == c, tile, 0.0)
                        sums[q][c] = add if sums[q][c] is None else sums[q][c] + add
        for q in range(NY):
            y_sum[d, q] = jnp.stack(sums[q])
        for n, dy in enumerate((2, 1, -1)):
            y_out[d, n], yc_out[d, n] = encode_rows(y_sum[d, yi(dy)].reshape(PER // 2, 16, 128))
            send(y_out.at[d, n], y_in.at[d, n], sent.at[4], y_recv.at[d], at_zy(0, dy))
            send(yc_out.at[d, n], yc_in.at[d, n], sent.at[6], yc_recv.at[d], at_zy(0, dy))
        out[:, yi(OFFS[d])] += y_sum[d, y]

    def out_step(d):
        arrived(y_in.at[d], y_recv.at[d])
        arrived(yc_in.at[d], yc_recv.at[d])
        for n, dy in ((1, -1), (2, 1), (0, 2)):
            out[:, yi(dy + OFFS[d])] += decode_rows(y_in[d, n], yc_in[d, n]).reshape(PER, 8, 128)

    env_here = False
    for kind, d, h, dz, links in ORDER:
        if kind == "F":
            g_wait(d, h, dz)
            g_fwd(d, h, dz, links)
        elif kind == "G":
            for c in small_copies:
                c.wait()
            read_groups()
        elif kind == "I":
            read_picks()
        elif kind == "L":
            read_places()
        elif kind == "S":
            g_fwd(d, h, dz, links)
        elif kind == "P":
            if not env_here:
                env_copy.wait()
                env_here = True
            product(d, h)
        elif kind == "T":
            make_terms(d, h)
        else:
            {"X": x_step, "Z": z_step, "Y": y_step, "O": out_step}[kind](d)
            if (kind, d) == ("X", 3):
                all_sent(g.at[0:NY * NZ - 1], 0)
                all_sent(mate_in, 1)
            if (kind, d) == ("Y", 3):
                all_sent(x_in, 2)
                all_sent(z_in, 3)
                all_sent(zc_in, 5)
    all_sent(y_in, 4)
    all_sent(yc_in, 6)


def shards(env_blocks, site_rows, route_dest, pair_index, pair_value):
    depth = env_blocks.shape[1]
    tile = (8, 128)
    tile16 = (16, 128)
    bf16 = jnp.bfloat16
    dma = pltpu.SemaphoreType.DMA
    out = pl.pallas_call(
        kernel,
        out_shape=jax.ShapeDtypeStruct((PER, NY, 8, 128), F32),
        in_specs=[pl.BlockSpec(memory_space=pl.ANY)] * 5,
        out_specs=pl.BlockSpec(memory_space=pltpu.VMEM),
        scratch_shapes=[
            pltpu.VMEM((PER, depth, PD * P_SIZE), bf16),
            pltpu.VMEM(site_rows.shape, bf16),
            pltpu.VMEM((NY * NZ, 64, depth), bf16),
            pltpu.VMEM((4, PER, 8, NZ, 16, 128), F32),
            pltpu.VMEM((4, NZ, SLOTS) + tile, F32),
            pltpu.VMEM((4, NX, SLOTS) + tile, F32),
            pltpu.VMEM((4, SLOTS // 2) + tile16, F32),
            pltpu.VMEM((4, 3, SLOTS // 2 + 1) + tile16, I16),
            pltpu.VMEM((4, 3, SLOTS // 2 + 1) + tile16, I16),
            pltpu.VMEM((4, SLOTS + 1) + tile, F32),
            pltpu.VMEM((4, NY) + tile16, F32),
            pltpu.VMEM((4, NZ - 1, NY) + tile16, I16),
            pltpu.VMEM((4, NZ - 1, NY) + tile16, I16),
            pltpu.VMEM((4, NZ - 1, 1, 128), F32),
            pltpu.VMEM((4, NZ - 1, 1, 128), F32),
            pltpu.VMEM((4, NY, PER) + tile, F32),
            pltpu.VMEM((4, 3, PER // 2) + tile16, I16),
            pltpu.VMEM((4, 3, PER // 2) + tile16, I16),
            pltpu.VMEM((4, 3, 1, 128), F32),
            pltpu.VMEM((4, 3, 1, 128), F32),
            pltpu.SMEM((K, NZ * NY * PER), jnp.int32),
            pltpu.SMEM((K, 2, PER), jnp.int32),
            pltpu.SMEM((K, 2, PER), F32),
            pltpu.SMEM((NZ, SLOTS), jnp.int32),
            pltpu.SMEM((NZ, SLOTS), jnp.int32),
            pltpu.SMEM((NZ * NY, 2), jnp.int32),
            pltpu.SMEM((NZ * NY, 2), jnp.int32),
            dma((5,)),
            dma((7,)),
            dma((max(SEMS.values()) + 1,)),
            dma((4,)),
            dma((4,)),
            dma((4,)),
            dma((4,)),
            dma((4,)),
            dma((4,)),
        ],
        compiler_params=pltpu.CompilerParams(
            collective_id=0, has_side_effects=True, vmem_limit_bytes=56 * 1024 * 1024
        ),
        cost_estimate=pl.CostEstimate(
            flops=2 * 2048 * depth * PER * 256, bytes_accessed=4 * 1024 * 1024, transcendentals=0
        ),
    )(route_dest.T, pair_index.transpose(1, 2, 0), pair_value.transpose(1, 2, 0), site_rows, env_blocks)
    return out.reshape(PER, -1)


def solution(mesh):
    in_specs = (
        P("chan", "row", None),
        P("chan", None, "row"),
        P(),
        P("chan", None, None),
        P("chan", None, None),
    )
    out_specs = P("chan", "row")
    return jax.shard_map(shards, mesh=mesh, in_specs=in_specs, out_specs=out_specs, check_vma=False)
```
